512 devices in a mesh: gx: 4 (over z_hi), gy: 8 (over y, core), gz: 16 (over x, z_lo).
Axes of the slice: x: 4, y: 4, z: 16 (z_hi: 4, z_lo: 4; z = z_hi * 4 + z_lo), core: 2. Of those that a mesh axis runs over, the one named last changes fastest.
Arguments:
- right_side: float32 [64, 256, 2048], P('gx', 'gy', 'gz'), may hold values from -64 to 64
- coefficient: float32 [64, 256, 2048], P('gx', 'gy', 'gz'), may hold values from 0.1 to 10
Outputs:
- solution_field: float32 [64, 256, 2048], P('gx', 'gy', 'gz')
- residual: float32 [64, 256, 2048], P('gx', 'gy', 'gz')
The draws below stay inside these ranges and needn't reach their ends.
All inputs are finite; a program needn't handle non-finite values.
Results may differ from the reference program's by a relative error of at most 0.02.
Values sent between devices are 32-bit elements; how exact they have to be, the bound alone decides.
A program may use at most 64 MiB of HBM per device.

```python
import functools
import math
from functools import partial
import jax
import jax.numpy as jnp
import numpy as np
from jax import lax

ORDER = 7
ITERS = 2
EX = 8
EY = 32
EZ = 256
NX = 64
NY = 256
NZ = 2048


def draw_right_side(key, part):
    key = jax.random.fold_in(key, 17)
    ramp_level = (jnp.arange(NX, dtype=jnp.float32) / NX)[:, None, None] + (jnp.arange(NY, dtype=jnp.float32) / NY)[None, :, None] + (jnp.arange(NZ, dtype=jnp.float32) / NZ)[None, None, :]
    rough_part = jnp.clip(jax.random.normal(key, (NX, NY, NZ), jnp.float32), -6.0, 6.0)
    return rough_part * jnp.exp(0.5 * jnp.log(3.0) * ramp_level)


def block_scale(key, shape, split, smallest, high):
    level = 1.0
    for axis_at, shards_of in split:
        steps = jax.random.uniform(jax.random.fold_in(jax.random.fold_in(key, 6), axis_at), (shards_of,), jnp.float32, smallest / len(split), high / len(split))
        level = level * jnp.repeat(jnp.exp(steps), shape[axis_at] // shards_of).reshape((-1,) + (1,) * (len(shape) - 1 - axis_at))
    return level


def setup_inputs(seed: int = 0) -> dict:
    splits = jax.random.split(jax.random.key(seed), 3)
    return {
        "right_side": draw_right_side(jax.random.fold_in(splits[2], 71), 0),
        "coefficient": jnp.clip(jnp.exp(math.log(10.0) - 4.6051702 * jax.random.uniform(splits[1], (NX, NY, NZ), jnp.float32) ** block_scale(splits[1], (NX, NY, NZ), ((0, 4), (1, 8), (2, 16)), -0.2, 0.2)), 0.1, 10.0),
    }


HIGHEST_MODE = lax.Precision.HIGHEST

def legendre_rows(points, degree):
    table_rows = [np.ones(points.shape), points * 1.0]
    for k in range(2, degree + 1):
        table_rows.append(((2 * k - 1) * points * table_rows[k - 1] - (k - 1) * table_rows[k - 2]) / k)
    return table_rows

def lobatto_tables(degree):
    per_side = degree + 1
    points = np.cos(np.pi * np.arange(per_side) / degree)
    for newton_step in range(60):
        table_rows = legendre_rows(points, degree)
        points = points - (points * table_rows[degree] - table_rows[degree - 1]) / (per_side * table_rows[degree])
    top_row = legendre_rows(points, degree)[degree][::-1]
    points = points[::-1]
    weights = 2.0 / (degree * per_side * top_row ** 2)
    deriv_np = np.zeros((per_side, per_side))
    for a in range(per_side):
        for b in range(per_side):
            if a != b:
                deriv_np[a, b] = top_row[a] / (top_row[b] * (points[a] - points[b]))
    deriv_np[0, 0] = -degree * per_side / 4.0
    deriv_np[-1, -1] = degree * per_side / 4.0
    return (weights, deriv_np)

def sine_tables(degree):
    box_side = degree + 3
    grid_index = np.arange(1, box_side + 1)
    sine_np = np.sqrt(2.0 / (box_side + 1)) * np.sin(np.pi * np.outer(grid_index, grid_index) / (box_side + 1))
    eigen_values = 2.0 - 2.0 * np.cos(np.pi * grid_index / (box_side + 1))
    summed = eigen_values[:, None, None] + eigen_values[None, :, None] + eigen_values[None, None, :]
    return (sine_np, 1.0 / summed)

def along(function, field, axis):
    if axis == 0:
        return function(field)
    return jax.vmap(functools.partial(along, function, axis=axis - 1))(field)

def pad_first(field, lower, upper):
    return jnp.pad(field, [(lower, upper)] + [(0, 0)] * (field.ndim - 1))

def assemble_first(field, offset, per_side):
    length = field.shape[0]
    local_index = (np.arange(length) - offset) % per_side
    bcast_shape = (length,) + (1,) * (field.ndim - 1)
    at_start = jnp.asarray((local_index == 0).reshape(bcast_shape), jnp.float32)
    at_end = jnp.asarray((local_index == per_side - 1).reshape(bcast_shape), jnp.float32)
    before = pad_first(field[:-1], 1, 0)
    after = pad_first(field[1:], 0, 1)
    return field + at_start * before + at_end * after

def gather_boxes_first(field, per_side):
    elements = (field.shape[0] - 4) // per_side
    trailing = field.shape[1:]
    own_part = field[2:2 + per_side * elements].reshape((elements, per_side) + trailing)
    left_part = field[0:per_side * elements:per_side][:, None]
    right_part = field[per_side + 3:per_side * elements + 4:per_side][:, None]
    joined = jnp.concatenate([left_part, own_part, right_part], axis=1)
    return joined.reshape((elements * (per_side + 2),) + trailing)

def scatter_boxes_first(boxes, per_side):
    elements = boxes.shape[0] // (per_side + 2)
    trailing = boxes.shape[1:]
    shaped = boxes.reshape((elements, per_side + 2) + trailing)
    extent = elements * per_side
    own_part = shaped[:, 1:per_side + 1].reshape((extent,) + trailing)
    zero_slot = jnp.zeros_like(shaped[:, :1])
    left_part = jnp.concatenate([shaped[:, :1]] + [zero_slot] * (per_side - 1), axis=1).reshape((extent,) + trailing)
    right_part = jnp.concatenate([zero_slot] * 3 + [shaped[:, -1:]] + [zero_slot] * (per_side - 4), axis=1).reshape((extent,) + trailing)
    return pad_first(own_part, 2, 2) + pad_first(left_part, 0, 4) + pad_first(right_part, per_side, 0)[:extent + 4]

def contract_first(matrix, field, per_side):
    shaped = field.reshape((field.shape[0] // per_side, per_side) + field.shape[1:])
    product = jnp.einsum('ij,aj...->ai...', matrix, shaped, precision=HIGHEST_MODE)
    return product.reshape((-1,) + field.shape[1:])

def edge_vector(total, per_side):
    local_index = np.arange(total) % per_side
    vector = np.where((local_index == 0) | (local_index == per_side - 1), 0.5, 1.0)
    vector[0] = 1.0
    vector[-1] = 1.0
    return vector

def reference(right_side, coefficient):
    per_side = ORDER + 1
    box_side = ORDER + 3
    weights, deriv_np = lobatto_tables(ORDER)
    sine_np, inverse = sine_tables(ORDER)
    deriv_mat = jnp.asarray(deriv_np, jnp.float32)
    deriv_tr = jnp.asarray(deriv_np.T, jnp.float32)
    sine_basis = jnp.asarray(sine_np, jnp.float32)
    quad_x = jnp.asarray(np.tile(weights, EX), jnp.float32)
    quad_y = jnp.asarray(np.tile(weights, EY), jnp.float32)
    quad_z = jnp.asarray(np.tile(weights, EZ), jnp.float32)
    weighted = coefficient * (quad_x[:, None, None] * quad_y[None, :, None] * quad_z[None, None, :])
    mask_np = np.ones(NX)
    mask_np[-1] = 0.0
    mask_in = jnp.asarray(mask_np, jnp.float32)[:, None, None]
    multiplicity = jnp.asarray(edge_vector(NX, per_side), jnp.float32)[:, None, None] * jnp.asarray(edge_vector(NY, per_side), jnp.float32)[None, :, None] * jnp.asarray(edge_vector(NZ, per_side), jnp.float32)[None, None, :]
    cell_mean = coefficient.reshape(EX, per_side, EY, per_side, EZ, per_side).mean(axis=(1, 3, 5))
    repeated = jnp.repeat(jnp.repeat(jnp.repeat(1.0 / cell_mean, box_side, 0), box_side, 1), box_side, 2)
    box_scale = repeated * jnp.asarray(np.tile(inverse, (EX, EY, EZ)), jnp.float32)

    def assemble_all(field):
        padded = jnp.pad(field, 1)
        for dim_id in range(3):
            padded = along(partial(assemble_first, offset=1, per_side=per_side), padded, dim_id)
        return padded[1:-1, 1:-1, 1:-1]

    def operate(field):
        summed = jnp.zeros_like(field)
        for dim_id in range(3):
            gradient = along(partial(contract_first, deriv_mat, per_side=per_side), field, dim_id)
            summed = summed + along(partial(contract_first, deriv_tr, per_side=per_side), weighted * gradient, dim_id)
        return mask_in * assemble_all(summed)

    def precondition(field):
        boxes = jnp.pad(field, 2)
        for dim_id in range(3):
            boxes = along(partial(gather_boxes_first, per_side=per_side), boxes, dim_id)
            boxes = along(partial(contract_first, sine_basis, per_side=box_side), boxes, dim_id)
        boxes = boxes * box_scale
        for dim_id in range(3):
            boxes = along(partial(contract_first, sine_basis, per_side=box_side), boxes, dim_id)
            boxes = along(partial(scatter_boxes_first, per_side=per_side), boxes, dim_id)
        return mask_in * assemble_all(boxes[2:-2, 2:-2, 2:-2])

    def inner_sum(first, second):
        return jnp.sum(multiplicity * first * second)
    solution = jnp.zeros_like(right_side)
    residual = mask_in * assemble_all(right_side)
    precond = precondition(residual)
    direction = precond
    rz_now = inner_sum(residual, precond)
    for iteration in range(ITERS):
        op_image = operate(direction)
        step_size = rz_now / inner_sum(direction, op_image)
        solution = solution + step_size * direction
        residual = residual - step_size * op_image
        if iteration + 1 < ITERS:
            precond = precondition(residual)
            rz_next = inner_sum(residual, precond)
            direction = precond + rz_next / rz_now * direction
            rz_now = rz_next
    return (solution, residual)
```

```python
import itertools

import jax
import jax.numpy as jnp
import numpy as np
from jax import lax
from jax.experimental import pallas as pl
from jax.experimental.pallas import tpu as pltpu
from jax.sharding import PartitionSpec as P

ORDER = 7
SIDE = ORDER + 1
BOX = ORDER + 3
AXES = ("gx", "gy", "gz")
MESH = pl.DeviceIdType.MESH
F32 = jnp.float32
NEAR = [o for o in itertools.product((-1, 0, 1), repeat=3) if o != (0, 0, 0)]


def legendre_rows(points, degree):
    table_rows = [np.ones(points.shape), points * 1.0]
    for k in range(2, degree + 1):
        table_rows.append(
            ((2 * k - 1) * points * table_rows[k - 1] - (k - 1) * table_rows[k - 2]) / k
        )
    return table_rows


def lobatto_tables(degree):
    per_side = degree + 1
    points = np.cos(np.pi * np.arange(per_side) / degree)
    for newton_step in range(60):
        table_rows = legendre_rows(points, degree)
        points = points - (points * table_rows[degree] - table_rows[degree - 1]) / (
            per_side * table_rows[degree]
        )
    top_row = legendre_rows(points, degree)[degree][::-1]
    points = points[::-1]
    weights = 2.0 / (degree * per_side * top_row**2)
    deriv_np = np.zeros((per_side, per_side))
    for a in range(per_side):
        for b in range(per_side):
            if a != b:
                deriv_np[a, b] = top_row[a] / (top_row[b] * (points[a] - points[b]))
    deriv_np[0, 0] = -degree * per_side / 4.0
    deriv_np[-1, -1] = degree * per_side / 4.0
    return (weights, deriv_np)


def sine_tables(degree):
    box_side = degree + 3
    grid_index = np.arange(1, box_side + 1)
    sine_np = np.sqrt(2.0 / (box_side + 1)) * np.sin(
        np.pi * np.outer(grid_index, grid_index) / (box_side + 1)
    )
    eigen_values = 2.0 - 2.0 * np.cos(np.pi * grid_index / (box_side + 1))
    summed = eigen_values[:, None, None] + eigen_values[None, :, None] + eigen_values[None, None, :]
    return (sine_np, 1.0 / summed)


WEIGHTS, DERIV = lobatto_tables(ORDER)
SINE, INVERSE = sine_tables(ORDER)


def z_tables(elements):
    span = elements * SIDE
    assemble = np.zeros((span + 2, 2 * span))
    for i in range(span):
        assemble[1 + i, i] = 1.0
        if i % SIDE == 0 and i > 0:
            assemble[1 + i, i - 1] = 1.0
        if i % SIDE == SIDE - 1 and i < span - 1:
            assemble[1 + i, i + 1] = 1.0
    assemble[0, span] = 1.0
    assemble[1, span + 1] = 1.0
    assemble[span, 2 * span - 2] = 1.0
    assemble[span + 1, 2 * span - 1] = 1.0
    gather = np.zeros((elements * BOX, span + 2))
    for e in range(elements):
        gather[e * BOX, 0 if e == 0 else 1 + SIDE * e - 2] = 1.0
        for k in range(SIDE):
            gather[e * BOX + 1 + k, 1 + SIDE * e + k] = 1.0
        gather[e * BOX + BOX - 1, span + 1 if e == elements - 1 else 1 + SIDE * (e + 1) + 1] = 1.0
    to_modes = np.kron(np.eye(elements), SINE) @ gather @ assemble
    forward = np.zeros((2 * span, 2 * span))
    forward[:, : elements * BOX] = to_modes.T
    return forward, assemble[1:-1].T


def rotate(x, shift, axis):
    return pltpu.roll(x, shift % x.shape[axis], axis)


class Halo:
    def __init__(self, n, hf, hs, lf, ls):
        self.n, self.hf, self.hs, self.lf, self.ls = n, hf, hs, lf, ls
        self.packed = 4 * n + 4
        self.own_z = -(-n * n // 64)
        self.z_hi = self.packed
        self.z_lo = self.packed + self.own_z + 1
        self.total = self.packed + 2 * (self.own_z + 1)
        self.slot, at = {}, 0
        for o in NEAR:
            self.slot[o] = (at, self.part(o)[1])
            at += self.part(o)[1]
        self.received = at

    def part(self, o):
        n = self.n
        if o[2]:
            base = self.z_hi if o[2] > 0 else self.z_lo
            return (base, self.own_z) if o[:2] == (0, 0) else (base + self.own_z, 1)
        if o[0] == 0:
            return (0 if o[1] > 0 else n, n)
        if o[1] == 0:
            return (2 * n if o[0] > 0 else 3 * n, n)
        return (4 * n + {(1, 1): 0, (1, -1): 1, (-1, 1): 2, (-1, -1): 3}[o[:2]], 1)


IN = Halo(SIDE, 7, 6, 0, 1)
OUT = Halo(BOX, 8, 9, 1, 0)
RED = (8, 4, 16)


def make_kernel(sizes, z_run):
    nx, ny, nz = sizes
    runs = nz // z_run
    ring = nx * z_run

    def kernel(b_ref, c_ref, wyz_ref, fwd_ref, bwd_ref, asm_ref, der_ref, inv_ref, mean_ref,
               sol_ref, res_ref,
               rows, raw, wc, icb, gs, gr, ug, e, x, sp, c1p, ss, sr, us, zs, acc,
               red_y, red_x, red_z, gsend, grecv, ssend, srecv, rsend, rrecv):
        gx, gy, gz = (lax.axis_index(a) for a in AXES)

        def near(o):
            return ((gx + o[0] + nx) % nx, (gy + o[1] + ny) % ny, (gz + o[2] + nz) % nz)

        def ring_y(t):
            return (gx, (gy + t) % ny, gz)

        def ring_x(t):
            return (gx, gy, ((gz // z_run + t) % runs) * z_run + gz % z_run)

        def ring_z(t):
            to = (gx * z_run + gz % z_run + t) % ring
            return (to // z_run, gy, (gz // z_run) * z_run + to % z_run)

        partners = [near(o) for o in NEAR]
        partners += [ring_y(t) for t in range(1, ny)]
        partners += [ring_x(t) for t in range(1, runs)]
        partners += [ring_z(t) for t in range(1, ring)]
        barrier = pltpu.get_barrier_semaphore()
        for device in partners:
            pl.semaphore_signal(barrier, inc=1, device_id=device, device_id_type=MESH)

        sub = lax.broadcasted_iota(jnp.int32, (8, 128), 0)
        lane = lax.broadcasted_iota(jnp.int32, (8, 128), 1)
        pair = lane // 2
        ey = sub % 4
        lower = sub < 4

        def flag(condition):
            return jnp.where(condition, 1.0, 0.0).astype(F32)

        fx_lo, fx_hi = flag(gx > 0), flag(gx < nx - 1)
        fy_lo, fy_hi = flag(gy > 0), flag(gy < ny - 1)
        fz_lo, fz_hi = flag(gz > 0), flag(gz < nz - 1)
        y_mask = jnp.where(ey >= 2, fy_lo, fy_hi)
        z_mask = jnp.where(lane < 2, fz_lo, jnp.where(lane >= 126, fz_hi, 0.0))
        x_mask = jnp.where(lower, 1.0, fx_hi)

        def pack(u, halo):
            y_hi = jnp.where(ey == 3, u[:, halo.hf], rotate(u[:, halo.hs], 7, 1))
            y_lo = jnp.where(ey == 0, u[:, halo.lf], rotate(u[:, halo.ls], 1, 1))
            x_hi = jnp.where(lower, rotate(u[halo.hs], 4, 1), u[halo.hf])
            x_lo = jnp.where(lower, u[halo.lf], rotate(u[halo.ls], 4, 1))
            corner = [
                jnp.where(lower, rotate(y_hi[halo.hs], 4, 0), y_hi[halo.hf]),
                jnp.where(lower, rotate(y_lo[halo.hs], 4, 0), y_lo[halo.hf]),
                jnp.where(lower, y_hi[halo.lf], rotate(y_hi[halo.ls], 4, 0)),
                jnp.where(lower, y_lo[halo.lf], rotate(y_lo[halo.ls], 4, 0)),
            ]
            return y_hi, y_lo, x_hi, x_lo, corner

        def store_packed(ref, parts, n):
            for k in range(4):
                ref[k * n : (k + 1) * n] = parts[k]
            for k in range(4):
                ref[4 * n + k] = parts[4][k]

        def lane_pack(values, up):
            total = None
            for k, value in enumerate(values):
                moved = rotate(value, 2 * k + 2 if up else 2 * k, 1)
                total = moved if total is None else jnp.where(pair == k, moved, total)
            return total

        def send(src, dst, halo, send_sem, recv_sem):
            for o in NEAR:
                at, count = halo.part(o)
                to, _ = halo.slot[(-o[0], -o[1], -o[2])]
                pltpu.make_async_remote_copy(
                    src_ref=src.at[pl.ds(at, count)],
                    dst_ref=dst.at[pl.ds(to, count)],
                    send_sem=send_sem,
                    recv_sem=recv_sem,
                    device_id=near(o),
                    device_id_type=MESH,
                ).start()

        def wait_all(ref, sem):
            pltpu.make_async_copy(ref, ref, sem).wait()

        def merged_lanes(dst, halo, dz):
            n = halo.n

            def got(dx, dy):
                return dst[halo.slot[(dx, dy, dz)][0]]

            out = jnp.where(ey >= 2, got(0, -1), rotate(got(0, 1), -2 * n, 1))
            out = jnp.where(pair >= 2 * n, got(-1, 0), out)
            out = jnp.where(pair >= 3 * n, got(1, 0), out)
            low = jnp.where(ey >= 2, got(-1, -1), rotate(got(-1, 1), -2, 1))
            high = jnp.where(ey >= 2, got(1, -1), rotate(got(1, 1), -2, 1))
            out = jnp.where(pair >= 4 * n, low, out)
            return jnp.where(pair >= 4 * n + 2, high, out)

        def unlane(low, high, k):
            return z_mask * jnp.where(
                lane < 2, rotate(low, -2 * k, 1), rotate(high, 126 - 2 * k, 1)
            )

        def receive(dst, halo, put):
            n = halo.n

            def at(o, k=0):
                return dst[halo.slot[o][0] + k]

            own_lo = [dst[halo.slot[(0, 0, -1)][0] + k] for k in range(halo.own_z)]
            own_hi = [dst[halo.slot[(0, 0, 1)][0] + k] for k in range(halo.own_z)]
            for i in range(n):
                for j in range(n):
                    k = i * n + j
                    put(1, i, j, unlane(own_lo[k // 64], own_hi[k // 64], k % 64))
            low, high = merged_lanes(dst, halo, -1), merged_lanes(dst, halo, 1)
            for k in range(n):
                put(0, k, n, y_mask * jnp.where(ey >= 2, at((0, -1, 0), k), at((0, 1, 0), k)))
                put(1, k, n, y_mask * unlane(low, high, k))
                put(0, n, k, fx_lo * at((-1, 0, 0), k))
                put(1, n, k, fx_lo * unlane(low, high, 2 * n + k))
                put(0, n + 1, k, fx_hi * at((1, 0, 0), k))
                put(1, n + 1, k, fx_hi * unlane(low, high, 3 * n + k))
            put(0, n, n, fx_lo * y_mask * jnp.where(ey >= 2, at((-1, -1, 0)), at((-1, 1, 0))))
            put(1, n, n, fx_lo * y_mask * unlane(low, high, 4 * n))
            put(0, n + 1, n, fx_hi * y_mask * jnp.where(ey >= 2, at((1, -1, 0)), at((1, 1, 0))))
            put(1, n + 1, n, fx_hi * y_mask * unlane(low, high, 4 * n + 2))

        def from_x(u, plo, phi, hf, hs, lf, ls):
            face_lo = rotate(jnp.where(lower, u[hf], plo), 4, 1)
            next_lo = jnp.where(lower, plo, rotate(u[hs], 4, 1))
            face_hi = rotate(jnp.where(lower, phi, u[lf]), 4, 1)
            next_hi = jnp.where(lower, rotate(u[ls], 4, 1), phi)
            return face_lo, next_lo, face_hi, next_hi

        def from_y(u, h, hf, hs, lf, ls):
            turned = rotate(h, 4, 1)
            face_lo = rotate(jnp.where(ey == 3, turned, u(hf)), 1, 1)
            next_lo = jnp.where(ey == 0, rotate(h, 6, 1), rotate(u(hs), 1, 1))
            face_hi = rotate(jnp.where(ey == 0, turned, u(lf)), 7, 1)
            next_hi = jnp.where(ey == 3, rotate(h, 2, 1), rotate(u(ls), 7, 1))
            return face_lo, next_lo, face_hi, next_hi

        def gather_send(it):
            u = raw[it].reshape(8, 8, 8, 128)
            store_packed(gs.at[it], pack(u, IN), SIDE)
            own = [raw[it, k] for k in range(64)]
            edge = [gs[it, k] for k in range(IN.packed)]
            gs[it, IN.z_hi] = lane_pack(own, True)
            gs[it, IN.z_hi + 1] = lane_pack(edge, True)
            gs[it, IN.z_lo] = lane_pack(own, False)
            gs[it, IN.z_lo + 1] = lane_pack(edge, False)

        def gather_receive(it):
            def put(tile, i, j, value):
                ug[tile, i, j] = value

            receive(gr.at[it], IN, put)
            ug[0, 0:8, 0:8] = raw[it].reshape(8, 8, 8, 128)
            for tile in range(2):
                u = [ug[tile, i] for i in range(10)]
                face_lo, next_lo, face_hi, next_hi = from_x(u, u[8], u[9], 7, 6, 0, 1)
                wide = [next_lo, u[0] + face_lo] + u[1:7]
                wide += [(u[7] + face_hi) * x_mask, next_hi]
                for i in range(10):
                    w = wide[i]
                    face_lo, next_lo, face_hi, next_hi = from_y(
                        lambda j: w[j : j + 1], w[8:9], 7, 6, 0, 1
                    )
                    e[tile, i, 0:1] = next_lo
                    e[tile, i, 1:2] = w[0:1] + face_lo
                    e[tile, i, 2:8] = w[1:7]
                    e[tile, i, 8:9] = w[7:8] + face_hi
                    e[tile, i, 9:10] = next_hi
                x[it, tile] = e[tile, 1:9, 1:9].reshape(64, 8, 128)

        def halves(v, even, odd):
            plus = [v[a] + v[9 - a] for a in range(5)]
            minus = [v[a] - v[9 - a] for a in range(5)]
            out = []
            for k in range(10):
                part = plus if k % 2 == 0 else minus
                total = part[0] * float(SINE[0, k])
                for a in range(1, 5):
                    total = total + part[a] * float(SINE[a, k])
                out.append(total)
            return out

        def unhalves(f):
            first, last = [], []
            for a in range(5):
                even = f[0] * float(SINE[a, 0])
                odd = f[1] * float(SINE[a, 1])
                for k in range(1, 5):
                    even = even + f[2 * k] * float(SINE[a, 2 * k])
                    odd = odd + f[2 * k + 1] * float(SINE[a, 2 * k + 1])
                first.append(even + odd)
                last.append(even - odd)
            return first + last[::-1]

        def boxes(it):
            wide = jnp.concatenate(
                [e[0].reshape(800, 128), e[1].reshape(800, 128)], axis=1
            )
            modes = jnp.dot(wide, fwd_ref[...], precision=lax.Precision.HIGHEST,
                            preferred_element_type=F32)
            sp[0] = modes[:, :128].reshape(10, 10, 8, 128)
            sp[1] = modes[:, 128:].reshape(10, 10, 8, 128)

            def along_x(j, carry):
                for tile in range(2):
                    out = halves([sp[tile, i, j] for i in range(10)], None, None)
                    for i in range(10):
                        sp[tile, i, j] = out[i]
                return carry

            def middle(i, total):
                for tile in range(2):
                    f = halves([sp[tile, i, j] for j in range(10)], None, None)
                    scale = icb[tile]
                    g = [f[j] * (inv_ref[tile, i, j : j + 1] * scale) for j in range(10)]
                    for j in range(10):
                        total = total + f[j] * g[j]
                    out = unhalves(g)
                    for j in range(10):
                        sp[tile, i, j] = out[j]
                return total

            def back_x(j, carry):
                for tile in range(2):
                    out = unhalves([sp[tile, i, j] for i in range(10)])
                    for i in range(10):
                        sp[tile, i, j] = out[i]
                return carry

            lax.fori_loop(0, 10, along_x, 0)
            acc[2 * it] = lax.fori_loop(0, 10, middle, jnp.zeros((8, 128), F32))
            lax.fori_loop(0, 10, back_x, 0)
            wide = jnp.concatenate(
                [sp[0].reshape(800, 128), sp[1].reshape(800, 128)], axis=1
            )
            back = jnp.dot(wide, bwd_ref[...], precision=lax.Precision.HIGHEST,
                           preferred_element_type=F32)
            sp[0] = back[:, :128].reshape(10, 10, 8, 128)
            sp[1] = back[:, 128:].reshape(10, 10, 8, 128)

        def scatter_send(it):
            store_packed(ss.at[it], pack(sp[0], OUT), BOX)
            store_packed(c1p, pack(sp[1], OUT), BOX)
            own = [sp[1, k // 10, k % 10] for k in range(100)]
            edge = [c1p[k] for k in range(OUT.packed)]
            for base, up in ((OUT.z_hi, True), (OUT.z_lo, False)):
                ss[it, base] = lane_pack(own[:64], up)
                ss[it, base + 1] = lane_pack(own[64:], up)
                ss[it, base + 2] = lane_pack(edge, up)

        def scatter_receive(it):
            def put(tile, i, j, value):
                if tile == 0:
                    us[i, j] = value
                else:
                    us[i, j] = us[i, j] + value

            us[0:10, 0:10] = sp[0]
            later = []
            receive(sr.at[it], OUT, lambda t, i, j, v: put(t, i, j, v) if t == 0
                    else later.append((i, j, v)))
            for i, j, v in later:
                put(1, i, j, v)
            u = [us[i] for i in range(12)]
            face_lo, next_lo, face_hi, next_hi = from_x(u, u[10], u[11], 8, 9, 1, 0)
            fold = [u[1] + face_lo, u[2] + next_lo, u[3], u[4], u[5], u[6],
                    u[7] + next_hi, (u[8] + face_hi) * x_mask]
            for i in range(8):
                w = fold[i]
                last = x_mask if i == 7 else 1.0
                face_lo, next_lo, face_hi, next_hi = from_y(
                    lambda j: w[j : j + 1], w[10:11], 8, 9, 1, 0
                )
                zs[it, 8 * i : 8 * i + 1] = (w[1:2] + face_lo) * last
                zs[it, 8 * i + 1 : 8 * i + 2] = (w[2:3] + next_lo) * last
                zs[it, 8 * i + 2 : 8 * i + 6] = w[3:7] * last
                zs[it, 8 * i + 6 : 8 * i + 7] = (w[7:8] + next_hi) * last
                zs[it, 8 * i + 7 : 8 * i + 8] = (w[8:9] + face_hi) * last

        def derive(v, matrix):
            plus = [v[k] + v[7 - k] for k in range(4)]
            minus = [v[k] - v[7 - k] for k in range(4)]
            first, last = [], []
            for a in range(4):
                even = odd = None
                for k in range(4):
                    p = plus[k] * float(0.5 * (matrix[a, k] + matrix[a, 7 - k]))
                    m = minus[k] * float(0.5 * (matrix[a, k] - matrix[a, 7 - k]))
                    even = p if even is None else even + p
                    odd = m if odd is None else odd + m
                first.append(even + odd)
                last.append(odd - even)
            return first + last[::-1]

        def stiffness(it):
            def over_x(j, carry):
                grad = derive([zs[it, 8 * i + j] for i in range(8)], DERIV)
                flux = [grad[i] * wc[8 * i + j] for i in range(8)]
                out = derive(flux, DERIV.T)
                for i in range(8):
                    raw[it + 1, 8 * i + j] = out[i]
                return carry

            def over_y(i, carry):
                grad = derive([zs[it, 8 * i + j] for j in range(8)], DERIV)
                flux = [grad[j] * wc[8 * i + j] for j in range(8)]
                out = derive(flux, DERIV.T)
                for j in range(8):
                    raw[it + 1, 8 * i + j] = raw[it + 1, 8 * i + j] + out[j]
                return carry

            lax.fori_loop(0, 8, over_x, 0)
            lax.fori_loop(0, 8, over_y, 0)
            field = zs[it].reshape(512, 128)
            grad = jnp.dot(field, der_ref[0], precision=lax.Precision.HIGHEST,
                           preferred_element_type=F32)
            flux = grad * wc[...].reshape(512, 128)
            out = jnp.dot(flux, der_ref[1], precision=lax.Precision.HIGHEST,
                          preferred_element_type=F32)
            total = raw[it + 1].reshape(512, 128) + out
            raw[it + 1] = total.reshape(64, 8, 128)
            acc[2 * it + 1] = jnp.sum((total * field).reshape(64, 8, 128), axis=0)

        rings = ((red_y, ny, gy, ring_y), (red_x, runs, gz // z_run, ring_x),
                 (red_z, ring, gx * z_run + gz % z_run, ring_z))

        def reduce_start(phase, value):
            ref, count, me, to = rings[phase]
            ref[me] = value
            for t in range(1, count):
                pltpu.make_async_remote_copy(
                    src_ref=ref.at[me],
                    dst_ref=ref.at[me],
                    send_sem=rsend.at[phase],
                    recv_sem=rrecv.at[phase],
                    device_id=to(t),
                    device_id_type=MESH,
                ).start()

        def reduce_wait(phase):
            ref, count, _, _ = rings[phase]
            if count > 1:
                part = ref.at[pl.ds(0, count - 1)]
                wait_all(part, rrecv.at[phase])
            return jnp.sum(ref[0:count], axis=0)

        def reduce_end(phase):
            ref, count, _, _ = rings[phase]
            if count > 1:
                wait_all(ref.at[pl.ds(0, count - 1)], rsend.at[phase])

        def relaid(ref, store):
            for i in range(8):
                for ex in range(2):
                    rows[i * 64 + ex * 32 : i * 64 + ex * 32 + 32] = ref[ex * 8 + i]
            for i in range(8):
                for j in range(8):
                    store(8 * i + j, rows[pl.ds(i * 64 + j, 8, stride=8), :])

        def put_b(k, value):
            raw[0, k] = value

        def put_c(k, value):
            zs[0, k] = value

        relaid(b_ref, put_b)
        relaid(c_ref, put_c)
        mean = jnp.dot(jnp.sum(zs[0], axis=0), mean_ref[...], precision=lax.Precision.HIGHEST,
                       preferred_element_type=F32)
        icb[0] = 1.0 / mean[:, :128]
        icb[1] = 1.0 / mean[:, 128:]
        for i in range(8):
            wc[8 * i : 8 * i + 8] = zs[0, 8 * i : 8 * i + 8] * (wyz_ref[...] * float(WEIGHTS[i]))

        def step(it, carry):
            gather_send(it)

            @pl.when(it == 0)
            def _():
                pl.semaphore_wait(barrier, len(partners))

            send(gs.at[it], gr.at[it], IN, gsend.at[it], grecv.at[it])
            wait_all(gr.at[it], grecv.at[it])
            gather_receive(it)
            boxes(it)
            scatter_send(it)
            send(ss.at[it], sr.at[it], OUT, ssend.at[it], srecv.at[it])
            wait_all(sr.at[it], srecv.at[it])
            scatter_receive(it)
            stiffness(it)
            return carry

        lax.fori_loop(0, 2, step, 0)
        local = jnp.zeros((8, 128), F32)
        for k in range(4):
            local = jnp.where(sub == k, jnp.sum(acc[k], axis=(0, 1), keepdims=True), local)
        reduce_start(0, local)
        gather_send(2)
        send(gs.at[2], gr.at[2], IN, gsend.at[2], grecv.at[2])
        reduce_start(1, reduce_wait(0))
        reduce_start(2, reduce_wait(1))
        wait_all(gr.at[2], grecv.at[2])
        gather_receive(2)
        sums = reduce_wait(2)
        rho, delta, gamma, eps = (sums[k : k + 1] for k in range(4))
        a0 = rho / delta
        rz = a0 * a0 * gamma - rho
        up = 1.0 + rz / rho
        curve = up * up * delta - 2.0 * a0 * up * gamma + a0 * a0 * eps
        a1 = rz / curve
        first = a0 + a1 * up
        second = a1 * a0

        def write(values, ref):
            for k in range(64):
                rows[pl.ds((k // 8) * 64 + k % 8, 8, stride=8), :] = values[k]
            for i in range(8):
                for ex in range(2):
                    ref[ex * 8 + i] = rows[i * 64 + ex * 32 : i * 64 + ex * 32 + 32]

        write(zs[0] * first - zs[1] * second, sol_ref)
        mixed = x[0] - x[1] * first + x[2] * second
        wide = jnp.concatenate(
            [mixed[0].reshape(512, 128), mixed[1].reshape(512, 128)], axis=1
        )
        out = jnp.dot(wide, asm_ref[...], precision=lax.Precision.HIGHEST,
                      preferred_element_type=F32)
        write(out.reshape(64, 8, 128), res_ref)
        for it in range(3):
            wait_all(gr.at[it], gsend.at[it])
        for it in range(2):
            wait_all(sr.at[it], ssend.at[it])
        for phase in range(3):
            reduce_end(phase)

    return kernel


def solution(mesh):
    sizes = tuple(mesh.shape[a] for a in AXES)
    z_run = 4 if sizes[2] % 4 == 0 else sizes[2]
    ring = sizes[0] * z_run
    forward, assemble = z_tables(16)
    der = np.kron(np.eye(16), DERIV)
    inverse = np.zeros((2, 10, 10, 128))
    tiled = np.tile(INVERSE, (1, 1, 16))
    inverse[0] = tiled[:, :, :128]
    inverse[1, :, :, :32] = tiled[:, :, 128:]
    mean = np.zeros((128, 256))
    mean[:, :160] = np.kron(np.eye(16), np.ones((8, 10))) / SIDE**3
    mean[0, 160:] = 1.0
    wyz = np.broadcast_to(
        WEIGHTS[:, None, None] * np.tile(WEIGHTS, 16)[None, None, :], (8, 8, 128)
    )
    tables = [
        jnp.asarray(t, F32)
        for t in (wyz, forward, forward.T, assemble, np.stack([der.T, der]), inverse, mean)
    ]
    vmem = pl.BlockSpec(memory_space=pltpu.VMEM)
    dma = pltpu.SemaphoreType.DMA

    def block(*shape):
        return pltpu.VMEM(shape + (8, 128), F32)

    call = pl.pallas_call(
        make_kernel(sizes, z_run),
        out_shape=[jax.ShapeDtypeStruct((16, 32, 128), F32)] * 2,
        in_specs=[vmem] * 9,
        out_specs=[vmem] * 2,
        scratch_shapes=[
            pltpu.VMEM((512, 128), F32),
            block(3, 64), block(64), block(2),
            block(3, IN.total), block(3, IN.received), block(2, 10, 9), block(2, 10, 10),
            block(3, 2, 64), block(2, 10, 10), block(OUT.packed),
            block(2, OUT.total), block(2, OUT.received), block(12, 11),
            block(2, 64), block(4),
            block(sizes[1]), block(sizes[2] // z_run), block(ring),
            dma((3,)), dma((3,)), dma((2,)), dma((2,)), dma((3,)), dma((3,)),
        ],
        compiler_params=pltpu.CompilerParams(
            collective_id=0, has_side_effects=True, vmem_limit_bytes=48 * 1024 * 1024
        ),
    )

    def shards(right_side, coefficient):
        return tuple(call(right_side, coefficient, *tables))

    spec = P(*AXES)
    return jax.shard_map(
        shards, mesh=mesh, in_specs=(spec, spec), out_specs=(spec, spec), check_vma=False
    )
```

```python
import itertools

import jax
import jax.numpy as jnp
import numpy as np
from jax import lax
from jax.experimental import pallas as pl
from jax.experimental.pallas import tpu as pltpu
from jax.sharding import PartitionSpec as P

ORDER = 7
SIDE = ORDER + 1
BOX = ORDER + 3
AXES = ("gx", "gy", "gz")
MESH = pl.DeviceIdType.MESH
F32 = jnp.float32
NEAR = sorted(
    (o for o in itertools.product((-1, 0, 1), repeat=3) if o != (0, 0, 0)),
    key=lambda o: [(1, 1, 1), (1, 0, 1), (1, 1, 0), (0, 1, 1), (0, 0, 1), (1, 0, 0),
                   (0, 1, 0)].index(tuple(map(abs, o))),
)


def legendre_rows(points, degree):
    table_rows = [np.ones(points.shape), points * 1.0]
    for k in range(2, degree + 1):
        table_rows.append(
            ((2 * k - 1) * points * table_rows[k - 1] - (k - 1) * table_rows[k - 2]) / k
        )
    return table_rows


def lobatto_tables(degree):
    per_side = degree + 1
    points = np.cos(np.pi * np.arange(per_side) / degree)
    for newton_step in range(60):
        table_rows = legendre_rows(points, degree)
        points = points - (points * table_rows[degree] - table_rows[degree - 1]) / (
            per_side * table_rows[degree]
        )
    top_row = legendre_rows(points, degree)[degree][::-1]
    points = points[::-1]
    weights = 2.0 / (degree * per_side * top_row**2)
    deriv_np = np.zeros((per_side, per_side))
    for a in range(per_side):
        for b in range(per_side):
            if a != b:
                deriv_np[a, b] = top_row[a] / (top_row[b] * (points[a] - points[b]))
    deriv_np[0, 0] = -degree * per_side / 4.0
    deriv_np[-1, -1] = degree * per_side / 4.0
    return (weights, deriv_np)


def sine_tables(degree):
    box_side = degree + 3
    grid_index = np.arange(1, box_side + 1)
    sine_np = np.sqrt(2.0 / (box_side + 1)) * np.sin(
        np.pi * np.outer(grid_index, grid_index) / (box_side + 1)
    )
    eigen_values = 2.0 - 2.0 * np.cos(np.pi * grid_index / (box_side + 1))
    summed = eigen_values[:, None, None] + eigen_values[None, :, None] + eigen_values[None, None, :]
    return (sine_np, 1.0 / summed)


WEIGHTS, DERIV = lobatto_tables(ORDER)
SINE, INVERSE = sine_tables(ORDER)


def z_tables(elements):
    span = elements * SIDE
    assemble = np.zeros((span + 2, 2 * span))
    for i in range(span):
        assemble[1 + i, i] = 1.0
        if i % SIDE == 0 and i > 0:
            assemble[1 + i, i - 1] = 1.0
        if i % SIDE == SIDE - 1 and i < span - 1:
            assemble[1 + i, i + 1] = 1.0
    assemble[0, span] = 1.0
    assemble[1, span + 1] = 1.0
    assemble[span, 2 * span - 2] = 1.0
    assemble[span + 1, 2 * span - 1] = 1.0
    gather = np.zeros((elements * BOX, span + 2))
    for e in range(elements):
        gather[e * BOX, 0 if e == 0 else 1 + SIDE * e - 2] = 1.0
        for k in range(SIDE):
            gather[e * BOX + 1 + k, 1 + SIDE * e + k] = 1.0
        gather[e * BOX + BOX - 1, span + 1 if e == elements - 1 else 1 + SIDE * (e + 1) + 1] = 1.0
    to_modes = np.kron(np.eye(elements), SINE) @ gather @ assemble
    forward = np.zeros((2 * span, 2 * span))
    forward[:, : elements * BOX] = to_modes.T
    return forward, assemble[1:-1].T


def rotate(x, shift, axis):
    return pltpu.roll(x, shift % x.shape[axis], axis)


class Halo:
    def __init__(self, n, hf, hs, lf, ls):
        self.n, self.hf, self.hs, self.lf, self.ls = n, hf, hs, lf, ls
        self.own_z = -(-n * n // 64)
        self.corner = 4 * n
        self.z_part = {1: 4 * n + 4, -1: 4 * n + 7 + self.own_z}
        self.total = 4 * n + 10 + 2 * self.own_z
        self.slot, at, height = {}, 0, 0
        for o in NEAR:
            _, count, tall = self.part(o)
            self.slot[o] = at
            at += count
            height += count * tall
        self.received = at
        self.vectors = height // 8

    def part(self, o):
        n = self.n
        if o[2]:
            base = self.z_part[o[2]]
            if o[0]:
                return (base + self.own_z + (1 if o[0] > 0 else 2), 1, 2)
            return (base + self.own_z, 1, 8) if o[1] else (base, self.own_z, 8)
        if o[0] == 0:
            return (0 if o[1] > 0 else n, n, 8)
        if o[1] == 0:
            return (2 * n if o[0] > 0 else 3 * n, n, 8)
        return (4 * n + [(1, 1), (1, -1), (-1, 1), (-1, -1)].index(o[:2]), 1, 4)


IN = Halo(SIDE, 7, 6, 0, 1)
OUT = Halo(BOX, 8, 9, 1, 0)
RED = (8, 4, 16)


def make_kernel(sizes, z_run):
    nx, ny, nz = sizes
    runs = nz // z_run
    ring = nx * z_run

    def kernel(b_ref, c_ref, *rest):
        tables, rest = rest[:7], rest[7:]
        (sol_ref, res_ref, b_rows, c_rows, wyz_ref, fwd_ref, bwd_ref, asm_ref, der_ref, inv_ref,
         mean_ref, raw, wc, icb, gs, gr, ug, e, x, sp, ss, sr, us, zs, acc,
         red_y, red_x, red_z, gsend, grecv, ssend, srecv, rsend, rrecv, load) = rest
        gx, gy, gz = (lax.axis_index(a) for a in AXES)

        def near(o):
            return ((gx + o[0] + nx) % nx, (gy + o[1] + ny) % ny, (gz + o[2] + nz) % nz)

        def ring_y(t):
            return (gx, (gy + t) % ny, gz)

        def ring_x(t):
            return (gx, gy, ((gz // z_run + t) % runs) * z_run + gz % z_run)

        def ring_z(t):
            to = (gx * z_run + gz % z_run + t) % ring
            return (to // z_run, gy, (gz // z_run) * z_run + to % z_run)

        partners = [near(o) for o in NEAR]
        partners += [ring_y(t) for t in range(1, ny)]
        partners += [ring_x(t) for t in range(1, runs)]
        partners += [ring_z(t) for t in range(1, ring)]
        barrier = pltpu.get_barrier_semaphore()
        for device in partners:
            pl.semaphore_signal(barrier, inc=1, device_id=device, device_id_type=MESH)

        loads = []
        for source, target in ((b_ref, b_rows), (c_ref, c_rows)):
            for ex in range(2):
                loads.append((source.at[pl.ds(8 * ex, 8)], target.at[:, pl.ds(32 * ex, 32)]))
        kept = (wyz_ref, fwd_ref, bwd_ref, asm_ref, der_ref, inv_ref, mean_ref)
        loads += list(zip(tables, kept))
        loads = [
            pltpu.make_async_copy(source, target, load.at[k])
            for k, (source, target) in enumerate(loads)
        ]
        for copy in loads:
            copy.start()

        sub = lax.broadcasted_iota(jnp.int32, (8, 128), 0)
        lane = lax.broadcasted_iota(jnp.int32, (8, 128), 1)
        pair = lane // 2
        ey = sub % 4
        lower = sub < 4

        def flag(condition):
            return jnp.where(condition, 1.0, 0.0).astype(F32)

        fx_lo, fx_hi = flag(gx > 0), flag(gx < nx - 1)
        fy_lo, fy_hi = flag(gy > 0), flag(gy < ny - 1)
        fz_lo, fz_hi = flag(gz > 0), flag(gz < nz - 1)
        y_mask = jnp.where(ey >= 2, fy_lo, fy_hi)
        z_mask = jnp.where(lane < 2, fz_lo, jnp.where(lane >= 126, fz_hi, 0.0))
        x_mask = jnp.where(lower, 1.0, fx_hi)

        def pack(u, halo):
            y_hi = jnp.where(ey == 3, u[:, halo.hf], rotate(u[:, halo.hs], 7, 1))
            y_lo = jnp.where(ey == 0, u[:, halo.lf], rotate(u[:, halo.ls], 1, 1))
            x_hi = jnp.where(lower, rotate(u[halo.hs], 4, 1), u[halo.hf])
            x_lo = jnp.where(lower, u[halo.lf], rotate(u[halo.ls], 4, 1))
            corner = [
                jnp.where(lower, rotate(y_hi[halo.hs], 4, 0), y_hi[halo.hf]),
                jnp.where(lower, rotate(y_lo[halo.hs], 4, 0), y_lo[halo.hf]),
                jnp.where(lower, y_hi[halo.lf], rotate(y_hi[halo.ls], 4, 0)),
                jnp.where(lower, y_lo[halo.lf], rotate(y_lo[halo.ls], 4, 0)),
            ]
            return y_hi, y_lo, x_hi, x_lo, corner

        def store_packed(ref, parts, n):
            for k in range(4):
                ref[k * n : (k + 1) * n] = parts[k]
            for k, corner in enumerate(parts[4]):
                if k % 2 == 0:
                    corner = jnp.where(sub < 2, rotate(corner, 2, 0), corner)
                else:
                    corner = jnp.where(sub < 2, corner, rotate(corner, 6, 0))
                ref[4 * n + k, 0:4] = corner[0:4]

        def lane_pack(values, up):
            total = None
            for k, value in enumerate(values):
                moved = rotate(value, 2 * k + 2 if up else 2 * k, 1)
                total = moved if total is None else jnp.where(pair == k, moved, total)
            return total

        def fan(value, sign):
            turned = value
            for k in range(1, 4):
                turned = jnp.where(ey == k, rotate(value, sign * 32 * k, 1), turned)
            return turned

        def store_lanes(ref, own, parts, halo):
            for up, base in ((True, halo.z_part[1]), (False, halo.z_part[-1])):
                for k in range(halo.own_z):
                    ref[base + k] = lane_pack(own[64 * k : 64 * k + 64], up)
                n, at = halo.n, base + halo.own_z
                planes = [parts[side][k] for side in (0, 1) for k in range(n)]
                ref[at] = lane_pack(planes, up)
                for k in range(2):
                    planes = [parts[2 + k][j] for j in range(n)] + parts[4][2 * k : 2 * k + 2]
                    moved = fan(lane_pack(planes, up), 1)
                    moved = jnp.where(lane // 32 == ey, moved, 0.0)
                    ref[at + 1 + k, 0:1] = jnp.sum(moved[0:4], axis=0, keepdims=True)
                    ref[at + 1 + k, 1:2] = jnp.sum(moved[4:8], axis=0, keepdims=True)

        def send(src, dst, halo, send_sem, recv_sem):
            for o in NEAR:
                at, count, tall = halo.part(o)
                to = halo.slot[(-o[0], -o[1], -o[2])]
                pltpu.make_async_remote_copy(
                    src_ref=src.at[pl.ds(at, count), pl.ds(0, tall)],
                    dst_ref=dst.at[pl.ds(to, count), pl.ds(0, tall)],
                    send_sem=send_sem,
                    recv_sem=recv_sem,
                    device_id=near(o),
                    device_id_type=MESH,
                ).start()

        def wait_all(ref, sem):
            pltpu.make_async_copy(ref, ref, sem).wait()

        def wait_halo(ref, halo, sem):
            wait_all(ref.at[pl.ds(0, halo.vectors)], sem)

        def y_lanes(dst, halo, dz):
            low, high = dst[halo.slot[(0, -1, dz)]], dst[halo.slot[(0, 1, dz)]]
            return jnp.where(ey >= 2, low, rotate(high, -2 * halo.n, 1))

        def x_lanes(dst, halo, dx, dz):
            def got(dy):
                at = halo.slot[(dx, dy, dz)]
                value = jnp.where(lower, dst[at, 0:1], dst[at, 1:2])
                return fan(value, -1)

            corner = jnp.where(ey >= 2, got(-1), rotate(got(1), -2, 1))
            return jnp.where(pair >= halo.n, corner, got(0))

        def xy_corner(dst, halo, dx):
            low, high = dst[halo.slot[(dx, -1, 0)], 0:4], dst[halo.slot[(dx, 1, 0)], 0:4]
            low, high = jnp.concatenate([low, low], 0), jnp.concatenate([high, high], 0)
            low = jnp.where(lower, low, rotate(low, 2, 0))
            high = jnp.where(lower, high, rotate(high, 6, 0))
            return jnp.where(ey >= 2, low, high)

        def unlane(low, high, k):
            return z_mask * jnp.where(
                lane < 2, rotate(low, -2 * k, 1), rotate(high, 126 - 2 * k, 1)
            )

        def receive(dst, halo, put):
            n = halo.n

            def at(o, k=0):
                return dst[halo.slot[o] + k]

            own_lo = [dst[halo.slot[(0, 0, -1)] + k] for k in range(halo.own_z)]
            own_hi = [dst[halo.slot[(0, 0, 1)] + k] for k in range(halo.own_z)]
            for i in range(n):
                for j in range(n):
                    k = i * n + j
                    put(1, i, j, unlane(own_lo[k // 64], own_hi[k // 64], k % 64))
            low, high = y_lanes(dst, halo, -1), y_lanes(dst, halo, 1)
            below = x_lanes(dst, halo, -1, -1), x_lanes(dst, halo, -1, 1)
            above = x_lanes(dst, halo, 1, -1), x_lanes(dst, halo, 1, 1)
            for k in range(n):
                put(0, k, n, y_mask * jnp.where(ey >= 2, at((0, -1, 0), k), at((0, 1, 0), k)))
                put(1, k, n, y_mask * unlane(low, high, k))
                put(0, n, k, fx_lo * at((-1, 0, 0), k))
                put(1, n, k, fx_lo * unlane(*below, k))
                put(0, n + 1, k, fx_hi * at((1, 0, 0), k))
                put(1, n + 1, k, fx_hi * unlane(*above, k))
            put(0, n, n, fx_lo * y_mask * xy_corner(dst, halo, -1))
            put(1, n, n, fx_lo * y_mask * unlane(*below, n))
            put(0, n + 1, n, fx_hi * y_mask * xy_corner(dst, halo, 1))
            put(1, n + 1, n, fx_hi * y_mask * unlane(*above, n))

        def from_x(u, plo, phi, hf, hs, lf, ls):
            face_lo = rotate(jnp.where(lower, u[hf], plo), 4, 1)
            next_lo = jnp.where(lower, plo, rotate(u[hs], 4, 1))
            face_hi = rotate(jnp.where(lower, phi, u[lf]), 4, 1)
            next_hi = jnp.where(lower, rotate(u[ls], 4, 1), phi)
            return face_lo, next_lo, face_hi, next_hi

        def from_y(u, h, hf, hs, lf, ls):
            turned = rotate(h, 4, 1)
            face_lo = rotate(jnp.where(ey == 3, turned, u(hf)), 1, 1)
            next_lo = jnp.where(ey == 0, rotate(h, 6, 1), rotate(u(hs), 1, 1))
            face_hi = rotate(jnp.where(ey == 0, turned, u(lf)), 7, 1)
            next_hi = jnp.where(ey == 3, rotate(h, 2, 1), rotate(u(ls), 7, 1))
            return face_lo, next_lo, face_hi, next_hi

        def gather_send(it):
            u = raw[it].reshape(8, 8, 8, 128)
            parts = pack(u, IN)
            store_packed(gs.at[it], parts, SIDE)
            store_lanes(gs.at[it], [raw[it, k] for k in range(64)], parts, IN)
            send(gs.at[it], gr.at[it], IN, gsend.at[it], grecv.at[it])

        def gather_receive(it):
            def put(tile, i, j, value):
                ug[tile, i, j] = value

            receive(gr.at[it], IN, put)
            ug[0, 0:8, 0:8] = raw[it].reshape(8, 8, 8, 128)
            for tile in range(2):
                u = [ug[tile, i] for i in range(10)]
                face_lo, next_lo, face_hi, next_hi = from_x(u, u[8], u[9], 7, 6, 0, 1)
                wide = [next_lo, u[0] + face_lo] + u[1:7]
                wide += [(u[7] + face_hi) * x_mask, next_hi]
                for i in range(10):
                    w = wide[i]
                    face_lo, next_lo, face_hi, next_hi = from_y(
                        lambda j: w[j : j + 1], w[8:9], 7, 6, 0, 1
                    )
                    e[tile, i, 0:1] = next_lo
                    e[tile, i, 1:2] = w[0:1] + face_lo
                    e[tile, i, 2:8] = w[1:7]
                    e[tile, i, 8:9] = w[7:8] + face_hi
                    e[tile, i, 9:10] = next_hi
                x[it, tile] = e[tile, 1:9, 1:9].reshape(64, 8, 128)

        def halves(v, even, odd):
            plus = [v[a] + v[9 - a] for a in range(5)]
            minus = [v[a] - v[9 - a] for a in range(5)]
            out = []
            for k in range(10):
                part = plus if k % 2 == 0 else minus
                total = part[0] * float(SINE[0, k])
                for a in range(1, 5):
                    total = total + part[a] * float(SINE[a, k])
                out.append(total)
            return out

        def unhalves(f):
            first, last = [], []
            for a in range(5):
                even = f[0] * float(SINE[a, 0])
                odd = f[1] * float(SINE[a, 1])
                for k in range(1, 5):
                    even = even + f[2 * k] * float(SINE[a, 2 * k])
                    odd = odd + f[2 * k + 1] * float(SINE[a, 2 * k + 1])
                first.append(even + odd)
                last.append(even - odd)
            return first + last[::-1]

        def boxes(it):
            wide = jnp.concatenate(
                [e[0].reshape(800, 128), e[1].reshape(800, 128)], axis=1
            )
            modes = jnp.dot(wide, fwd_ref[...], precision=lax.Precision.HIGH,
                            preferred_element_type=F32)
            sp[0] = modes[:, :128].reshape(10, 10, 8, 128)
            sp[1] = modes[:, 128:].reshape(10, 10, 8, 128)

            def along_x(j, carry):
                for tile in range(2):
                    out = halves([sp[tile, i, j] for i in range(10)], None, None)
                    for i in range(10):
                        sp[tile, i, j] = out[i]
                return carry

            def middle(i, total):
                for tile in range(2):
                    f = halves([sp[tile, i, j] for j in range(10)], None, None)
                    scale = icb[tile]
                    g = [f[j] * (inv_ref[tile, i, j : j + 1] * scale) for j in range(10)]
                    for j in range(10):
                        total = total + f[j] * g[j]
                    out = unhalves(g)
                    for j in range(10):
                        sp[tile, i, j] = out[j]
                return total

            def back_x(j, carry):
                for tile in range(2):
                    out = unhalves([sp[tile, i, j] for i in range(10)])
                    for i in range(10):
                        sp[tile, i, j] = out[i]
                return carry

            lax.fori_loop(0, 10, along_x, 0)
            acc[2 * it] = lax.fori_loop(0, 10, middle, jnp.zeros((8, 128), F32))
            lax.fori_loop(0, 10, back_x, 0)
            wide = jnp.concatenate(
                [sp[0].reshape(800, 128), sp[1].reshape(800, 128)], axis=1
            )
            back = jnp.dot(wide, bwd_ref[...], precision=lax.Precision.HIGH,
                           preferred_element_type=F32)
            sp[0] = back[:, :128].reshape(10, 10, 8, 128)
            sp[1] = back[:, 128:].reshape(10, 10, 8, 128)

        def scatter_send(it):
            store_packed(ss.at[it], pack(sp[0], OUT), BOX)
            own = [sp[1, k // 10, k % 10] for k in range(100)]
            store_lanes(ss.at[it], own, pack(sp[1], OUT), OUT)
            send(ss.at[it], sr.at[it], OUT, ssend.at[it], srecv.at[it])

        def scatter_receive(it):
            def put(tile, i, j, value):
                if tile == 0:
                    us[i, j] = value
                else:
                    us[i, j] = us[i, j] + value

            us[0:10, 0:10] = sp[0]
            later = []
            receive(sr.at[it], OUT, lambda t, i, j, v: put(t, i, j, v) if t == 0
                    else later.append((i, j, v)))
            for i, j, v in later:
                put(1, i, j, v)
            u = [us[i] for i in range(12)]
            face_lo, next_lo, face_hi, next_hi = from_x(u, u[10], u[11], 8, 9, 1, 0)
            fold = [u[1] + face_lo, u[2] + next_lo, u[3], u[4], u[5], u[6],
                    u[7] + next_hi, (u[8] + face_hi) * x_mask]
            for i in range(8):
                w = fold[i]
                last = x_mask if i == 7 else 1.0
                face_lo, next_lo, face_hi, next_hi = from_y(
                    lambda j: w[j : j + 1], w[10:11], 8, 9, 1, 0
                )
                zs[it, 8 * i : 8 * i + 1] = (w[1:2] + face_lo) * last
                zs[it, 8 * i + 1 : 8 * i + 2] = (w[2:3] + next_lo) * last
                zs[it, 8 * i + 2 : 8 * i + 6] = w[3:7] * last
                zs[it, 8 * i + 6 : 8 * i + 7] = (w[7:8] + next_hi) * last
                zs[it, 8 * i + 7 : 8 * i + 8] = (w[8:9] + face_hi) * last

        def derive(v, matrix):
            plus = [v[k] + v[7 - k] for k in range(4)]
            minus = [v[k] - v[7 - k] for k in range(4)]
            first, last = [], []
            for a in range(4):
                even = odd = None
                for k in range(4):
                    p = plus[k] * float(0.5 * (matrix[a, k] + matrix[a, 7 - k]))
                    m = minus[k] * float(0.5 * (matrix[a, k] - matrix[a, 7 - k]))
                    even = p if even is None else even + p
                    odd = m if odd is None else odd + m
                first.append(even + odd)
                last.append(odd - even)
            return first + last[::-1]

        def stiffness(it):
            def over_x(j, carry):
                grad = derive([zs[it, 8 * i + j] for i in range(8)], DERIV)
                flux = [grad[i] * wc[8 * i + j] for i in range(8)]
                out = derive(flux, DERIV.T)
                for i in range(8):
                    raw[it + 1, 8 * i + j] = out[i]
                return carry

            def over_y(i, carry):
                grad = derive([zs[it, 8 * i + j] for j in range(8)], DERIV)
                flux = [grad[j] * wc[8 * i + j] for j in range(8)]
                out = derive(flux, DERIV.T)
                for j in range(8):
                    raw[it + 1, 8 * i + j] = raw[it + 1, 8 * i + j] + out[j]
                return carry

            lax.fori_loop(0, 8, over_x, 0)
            lax.fori_loop(0, 8, over_y, 0)
            field = zs[it].reshape(512, 128)
            grad = jnp.dot(field, der_ref[0], precision=lax.Precision.HIGH,
                           preferred_element_type=F32)
            flux = grad * wc[...].reshape(512, 128)
            out = jnp.dot(flux, der_ref[1], precision=lax.Precision.HIGH,
                          preferred_element_type=F32)
            total = raw[it + 1].reshape(512, 128) + out
            raw[it + 1] = total.reshape(64, 8, 128)
            acc[2 * it + 1] = jnp.sum((total * field).reshape(64, 8, 128), axis=0)

        rings = ((red_y, ny, gy, ring_y), (red_x, runs, gz // z_run, ring_x),
                 (red_z, ring, gx * z_run + gz % z_run, ring_z))

        def reduce_start(phase, value):
            ref, count, me, to = rings[phase]
            ref[me, 0:1] = value
            for t in range(1, count):
                pltpu.make_async_remote_copy(
                    src_ref=ref.at[me, pl.ds(0, 1)],
                    dst_ref=ref.at[me, pl.ds(0, 1)],
                    send_sem=rsend.at[phase],
                    recv_sem=rrecv.at[phase],
                    device_id=to(t),
                    device_id_type=MESH,
                ).start()

        def reduce_wait(phase):
            ref, count, _, _ = rings[phase]
            if count > 1:
                wait_all(ref.at[pl.ds(0, count - 1), pl.ds(0, 1)], rrecv.at[phase])
            return jnp.sum(ref[0:count, 0:1], axis=0)

        def reduce_end(phase):
            ref, count, _, _ = rings[phase]
            if count > 1:
                wait_all(ref.at[pl.ds(0, count - 1), pl.ds(0, 1)], rsend.at[phase])

        def relaid(ref, store):
            for i in range(8):
                for j in range(8):
                    store(8 * i + j, ref[i, pl.ds(j, 8, stride=8), :])

        def put_b(k, value):
            raw[0, k] = value

        def put_c(k, value):
            zs[0, k] = value

        loads[0].wait()
        loads[1].wait()
        relaid(b_rows, put_b)
        pl.semaphore_wait(barrier, len(partners))
        gather_send(0)
        for copy in loads[2:]:
            copy.wait()
        relaid(c_rows, put_c)
        mean = jnp.dot(jnp.sum(zs[0], axis=0), mean_ref[...], precision=lax.Precision.HIGHEST,
                       preferred_element_type=F32)
        icb[0] = 1.0 / mean[:, :128]
        icb[1] = 1.0 / mean[:, 128:]
        for i in range(8):
            wc[8 * i : 8 * i + 8] = zs[0, 8 * i : 8 * i + 8] * (wyz_ref[...] * float(WEIGHTS[i]))

        def step(it, carry):
            wait_halo(gr.at[it], IN, grecv.at[it])
            gather_receive(it)
            boxes(it)
            scatter_send(it)
            wait_halo(sr.at[it], OUT, srecv.at[it])
            scatter_receive(it)
            stiffness(it)

            @pl.when(it == 1)
            def _():
                local = jnp.zeros((1, 128), F32)
                for k in range(4):
                    total = jnp.sum(acc[k], axis=(0, 1), keepdims=True)
                    local = jnp.where(lane[0:1] == k, total, local)
                reduce_start(0, local)

            gather_send(it + 1)
            return carry

        lax.fori_loop(0, 2, step, 0)
        reduce_start(1, reduce_wait(0))
        reduce_start(2, reduce_wait(1))
        wait_halo(gr.at[2], IN, grecv.at[2])
        gather_receive(2)
        sums = reduce_wait(2)
        rho, delta, gamma, eps = (sums[:, k : k + 1] for k in range(4))
        a0 = rho / delta
        rz = a0 * a0 * gamma - rho
        up = 1.0 + rz / rho
        curve = up * up * delta - 2.0 * a0 * up * gamma + a0 * a0 * eps
        a1 = rz / curve
        first = a0 + a1 * up
        second = a1 * a0

        def write(values, ref):
            for k in range(64):
                for ex in range(2):
                    ref[8 * ex + k // 8, pl.ds(k % 8, 4, stride=8), :] = values[
                        k, 4 * ex : 4 * ex + 4
                    ]

        write(zs[0] * first - zs[1] * second, sol_ref)
        mixed = x[0] - x[1] * first + x[2] * second
        wide = jnp.concatenate(
            [mixed[0].reshape(512, 128), mixed[1].reshape(512, 128)], axis=1
        )
        out = jnp.dot(wide, asm_ref[...], precision=lax.Precision.HIGH,
                      preferred_element_type=F32)
        write(out.reshape(64, 8, 128), res_ref)
        for it in range(3):
            wait_halo(gr.at[it], IN, gsend.at[it])
        for it in range(2):
            wait_halo(sr.at[it], OUT, ssend.at[it])
        for phase in range(3):
            reduce_end(phase)

    return kernel


def solution(mesh):
    sizes = tuple(mesh.shape[a] for a in AXES)
    z_run = 4 if sizes[2] % 4 == 0 else sizes[2]
    ring = sizes[0] * z_run
    forward, assemble = z_tables(16)
    der = np.kron(np.eye(16), DERIV)
    inverse = np.zeros((2, 10, 10, 128))
    tiled = np.tile(INVERSE, (1, 1, 16))
    inverse[0] = tiled[:, :, :128]
    inverse[1, :, :, :32] = tiled[:, :, 128:]
    mean = np.zeros((128, 256))
    mean[:, :160] = np.kron(np.eye(16), np.ones((8, 10))) / SIDE**3
    mean[0, 160:] = 1.0
    wyz = np.broadcast_to(
        WEIGHTS[:, None, None] * np.tile(WEIGHTS, 16)[None, None, :], (8, 8, 128)
    )
    tables = [
        jnp.asarray(t, F32)
        for t in (wyz, forward, forward.T, assemble, np.stack([der.T, der]), inverse, mean)
    ]
    vmem = pl.BlockSpec(memory_space=pltpu.VMEM)
    dma = pltpu.SemaphoreType.DMA

    def block(*shape):
        return pltpu.VMEM(shape + (8, 128), F32)

    call = pl.pallas_call(
        make_kernel(sizes, z_run),
        out_shape=[jax.ShapeDtypeStruct((16, 32, 128), F32)] * 2,
        in_specs=[pl.BlockSpec(memory_space=pltpu.HBM)] * 9,
        out_specs=[vmem] * 2,
        scratch_shapes=[
            pltpu.VMEM((8, 64, 128), F32), pltpu.VMEM((8, 64, 128), F32),
            *[pltpu.VMEM(t.shape, F32) for t in tables],
            block(3, 64), block(64), block(2),
            block(3, IN.total), block(3, IN.received), block(2, 10, 9), block(2, 10, 10),
            block(3, 2, 64), block(2, 10, 10),
            block(2, OUT.total), block(2, OUT.received), block(12, 11),
            block(2, 64), block(4),
            block(sizes[1]), block(sizes[2] // z_run), block(ring),
            dma((3,)), dma((3,)), dma((2,)), dma((2,)), dma((3,)), dma((3,)), dma((11,)),
        ],
        compiler_params=pltpu.CompilerParams(
            collective_id=0, has_side_effects=True, vmem_limit_bytes=48 * 1024 * 1024
        ),
    )

    def shards(right_side, coefficient):
        return tuple(call(right_side, coefficient, *tables))

    spec = P(*AXES)
    return jax.shard_map(
        shards, mesh=mesh, in_specs=(spec, spec), out_specs=(spec, spec), check_vma=False
    )
```

```python
import itertools

import jax
import jax.numpy as jnp
import numpy as np
from jax import lax
from jax.experimental import pallas as pl
from jax.experimental.pallas import tpu as pltpu
from jax.sharding import PartitionSpec as P

ORDER = 7
SIDE = ORDER + 1
BOX = ORDER + 3
AXES = ("gx", "gy", "gz")
MESH = pl.DeviceIdType.MESH
F32 = jnp.float32
NEAR = sorted(
    (o for o in itertools.product((-1, 0, 1), repeat=3) if o != (0, 0, 0)),
    key=lambda o: [(1, 1, 1), (1, 0, 1), (1, 1, 0), (0, 1, 1), (0, 0, 1), (1, 0, 0),
                   (0, 1, 0)].index(tuple(map(abs, o))),
)


def legendre_rows(points, degree):
    table_rows = [np.ones(points.shape), points * 1.0]
    for k in range(2, degree + 1):
        table_rows.append(
            ((2 * k - 1) * points * table_rows[k - 1] - (k - 1) * table_rows[k - 2]) / k
        )
    return table_rows


def lobatto_tables(degree):
    per_side = degree + 1
    points = np.cos(np.pi * np.arange(per_side) / degree)
    for newton_step in range(60):
        table_rows = legendre_rows(points, degree)
        points = points - (points * table_rows[degree] - table_rows[degree - 1]) / (
            per_side * table_rows[degree]
        )
    top_row = legendre_rows(points, degree)[degree][::-1]
    points = points[::-1]
    weights = 2.0 / (degree * per_side * top_row**2)
    deriv_np = np.zeros((per_side, per_side))
    for a in range(per_side):
        for b in range(per_side):
            if a != b:
                deriv_np[a, b] = top_row[a] / (top_row[b] * (points[a] - points[b]))
    deriv_np[0, 0] = -degree * per_side / 4.0
    deriv_np[-1, -1] = degree * per_side / 4.0
    return (weights, deriv_np)


def sine_tables(degree):
    box_side = degree + 3
    grid_index = np.arange(1, box_side + 1)
    sine_np = np.sqrt(2.0 / (box_side + 1)) * np.sin(
        np.pi * np.outer(grid_index, grid_index) / (box_side + 1)
    )
    eigen_values = 2.0 - 2.0 * np.cos(np.pi * grid_index / (box_side + 1))
    summed = eigen_values[:, None, None] + eigen_values[None, :, None] + eigen_values[None, None, :]
    return (sine_np, 1.0 / summed)


WEIGHTS, DERIV = lobatto_tables(ORDER)
SINE, INVERSE = sine_tables(ORDER)


def z_tables(elements):
    span = elements * SIDE
    assemble = np.zeros((span + 2, 2 * span))
    for i in range(span):
        assemble[1 + i, i] = 1.0
        if i % SIDE == 0 and i > 0:
            assemble[1 + i, i - 1] = 1.0
        if i % SIDE == SIDE - 1 and i < span - 1:
            assemble[1 + i, i + 1] = 1.0
    assemble[0, span] = 1.0
    assemble[1, span + 1] = 1.0
    assemble[span, 2 * span - 2] = 1.0
    assemble[span + 1, 2 * span - 1] = 1.0
    gather = np.zeros((elements * BOX, span + 2))
    for e in range(elements):
        gather[e * BOX, 0 if e == 0 else 1 + SIDE * e - 2] = 1.0
        for k in range(SIDE):
            gather[e * BOX + 1 + k, 1 + SIDE * e + k] = 1.0
        gather[e * BOX + BOX - 1, span + 1 if e == elements - 1 else 1 + SIDE * (e + 1) + 1] = 1.0
    to_modes = np.kron(np.eye(elements), SINE) @ gather @ assemble
    forward = np.zeros((2 * span, 2 * span))
    forward[:, : elements * BOX] = to_modes.T
    return forward, assemble[1:-1].T


def rotate(x, shift, axis):
    return pltpu.roll(x, shift % x.shape[axis], axis)


class Halo:
    def __init__(self, n, hf, hs, lf, ls):
        self.n, self.hf, self.hs, self.lf, self.ls = n, hf, hs, lf, ls
        self.own_z = -(-n * n // 64)
        self.corner = 4 * n
        self.z_part = {1: 4 * n + 4, -1: 4 * n + 7 + self.own_z}
        self.total = 4 * n + 10 + 2 * self.own_z
        self.slot, at, height = {}, 0, [0, 0]
        for o in NEAR:
            _, count, tall = self.part(o)
            self.slot[o] = at
            at += count
            height[tall < 8] += count * tall
        self.received = at
        self.vectors = [h // 8 for h in height]

    def part(self, o):
        n = self.n
        if o[2]:
            base = self.z_part[o[2]]
            if o[0]:
                return (base + self.own_z + (1 if o[0] > 0 else 2), 1, 2)
            return (base + self.own_z, 1, 8) if o[1] else (base, self.own_z, 8)
        if o[0] == 0:
            return (0 if o[1] > 0 else n, n, 8)
        if o[1] == 0:
            return (2 * n if o[0] > 0 else 3 * n, n, 8)
        return (4 * n + [(1, 1), (1, -1), (-1, 1), (-1, -1)].index(o[:2]), 1, 4)


IN = Halo(SIDE, 7, 6, 0, 1)
OUT = Halo(BOX, 8, 9, 1, 0)


def make_kernel(sizes, z_run):
    nx, ny, nz = sizes
    runs = nz // z_run
    ring = nx * z_run

    def kernel(b_ref, c_ref, *rest):
        tables, rest = rest[:7], rest[7:]
        (sol_ref, res_ref, b_rows, c_rows, wyz_ref, fwd_ref, bwd_ref, asm_ref, der_ref, inv_ref,
         mean_ref, raw, wc, icb, gs, gr, ug, e, x, sp, ss, sr, us, zs, acc,
         red_xy, red_z, gsend, grecv, ssend, srecv, rsend, rrecv, load) = rest
        gx, gy, gz = (lax.axis_index(a) for a in AXES)

        def near(o):
            return ((gx + o[0] + nx) % nx, (gy + o[1] + ny) % ny, (gz + o[2] + nz) % nz)

        def ring_xy(t):
            to = (gz // z_run + t // ny) % runs
            return (gx, (gy + t % ny) % ny, to * z_run + gz % z_run)

        def ring_z(t):
            to = (gx * z_run + gz % z_run + t) % ring
            return (to // z_run, gy, (gz // z_run) * z_run + to % z_run)

        partners = [near(o) for o in NEAR]
        partners += [ring_xy(t) for t in range(1, ny * runs)]
        partners += [ring_z(t) for t in range(1, ring)]
        barrier = pltpu.get_barrier_semaphore()
        for device in partners:
            pl.semaphore_signal(barrier, inc=1, device_id=device, device_id_type=MESH)

        loads = []
        for source, target in ((b_ref, b_rows), (c_ref, c_rows)):
            for ex in range(2):
                loads.append((source.at[pl.ds(8 * ex, 8)], target.at[:, pl.ds(32 * ex, 32)]))
        kept = (wyz_ref, fwd_ref, bwd_ref, asm_ref, der_ref, inv_ref, mean_ref)
        loads += list(zip(tables, kept))
        loads = [
            pltpu.make_async_copy(source, target, load.at[k])
            for k, (source, target) in enumerate(loads)
        ]
        for copy in loads:
            copy.start()

        sub = lax.broadcasted_iota(jnp.int32, (8, 128), 0)
        lane = lax.broadcasted_iota(jnp.int32, (8, 128), 1)
        pair = lane // 2
        ey = sub % 4
        lower = sub < 4

        def flag(condition):
            return jnp.where(condition, 1.0, 0.0).astype(F32)

        fx_lo, fx_hi = flag(gx > 0), flag(gx < nx - 1)
        fy_lo, fy_hi = flag(gy > 0), flag(gy < ny - 1)
        fz_lo, fz_hi = flag(gz > 0), flag(gz < nz - 1)
        y_mask = jnp.where(ey >= 2, fy_lo, fy_hi)
        z_mask = jnp.where(lane < 2, fz_lo, jnp.where(lane >= 126, fz_hi, 0.0))
        x_mask = jnp.where(lower, 1.0, fx_hi)

        def pack(u, halo):
            y_hi = jnp.where(ey == 3, u[:, halo.hf], rotate(u[:, halo.hs], 7, 1))
            y_lo = jnp.where(ey == 0, u[:, halo.lf], rotate(u[:, halo.ls], 1, 1))
            x_hi = jnp.where(lower, rotate(u[halo.hs], 4, 1), u[halo.hf])
            x_lo = jnp.where(lower, u[halo.lf], rotate(u[halo.ls], 4, 1))
            corner = [
                jnp.where(lower, rotate(y_hi[halo.hs], 4, 0), y_hi[halo.hf]),
                jnp.where(lower, rotate(y_lo[halo.hs], 4, 0), y_lo[halo.hf]),
                jnp.where(lower, y_hi[halo.lf], rotate(y_hi[halo.ls], 4, 0)),
                jnp.where(lower, y_lo[halo.lf], rotate(y_lo[halo.ls], 4, 0)),
            ]
            return y_hi, y_lo, x_hi, x_lo, corner

        def lane_pack(values, up):
            total = None
            for k, value in enumerate(values):
                moved = rotate(value, 2 * k + 2 if up else 2 * k, 1)
                total = moved if total is None else jnp.where(pair == k, moved, total)
            return total

        def fan(value, sign):
            turned = value
            for k in range(1, 4):
                turned = jnp.where(ey == k, rotate(value, sign * 32 * k, 1), turned)
            return turned

        def store_and_send(own, planes, lanes, halo, link):
            src, dst, send_sem, recv_sem = link
            n = halo.n

            def send(*kinds):
                for o in NEAR:
                    if tuple(map(abs, o)) not in kinds:
                        continue
                    at, count, tall = halo.part(o)
                    to = halo.slot[(-o[0], -o[1], -o[2])]
                    pltpu.make_async_remote_copy(
                        src_ref=src.at[pl.ds(at, count), pl.ds(0, tall)],
                        dst_ref=dst.at[pl.ds(to, count), pl.ds(0, tall)],
                        send_sem=send_sem,
                        recv_sem=recv_sem.at[1 if tall < 8 else 0],
                        device_id=near(o),
                        device_id_type=MESH,
                    ).start()

            ends = ((True, halo.z_part[1]), (False, halo.z_part[-1]))
            for up, base in ends:
                for k in range(2):
                    edge = [lanes[2 + k][j] for j in range(n)] + lanes[4][2 * k : 2 * k + 2]
                    moved = fan(lane_pack(edge, up), 1)
                    moved = jnp.where(lane // 32 == ey, moved, 0.0)
                    at = base + halo.own_z + 1 + k
                    src[at, 0:1] = jnp.sum(moved[0:4], axis=0, keepdims=True)
                    src[at, 1:2] = jnp.sum(moved[4:8], axis=0, keepdims=True)
            send((1, 1, 1), (1, 0, 1))
            for k, corner in enumerate(planes[4]):
                if k % 2 == 0:
                    corner = jnp.where(sub < 2, rotate(corner, 2, 0), corner)
                else:
                    corner = jnp.where(sub < 2, corner, rotate(corner, 6, 0))
                src[4 * n + k, 0:4] = corner[0:4]
            send((1, 1, 0))
            src[2 * n : 3 * n] = planes[2]
            src[3 * n : 4 * n] = planes[3]
            send((1, 0, 0))
            for up, base in ends:
                edge = [lanes[side][k] for side in (0, 1) for k in range(n)]
                src[base + halo.own_z] = lane_pack(edge, up)
            send((0, 1, 1))
            for up, base in ends:
                for k in range(halo.own_z):
                    src[base + k] = lane_pack(own[64 * k : 64 * k + 64], up)
            send((0, 0, 1))
            src[0:n] = planes[0]
            src[n : 2 * n] = planes[1]
            send((0, 1, 0))

        def wait_all(ref, sem):
            pltpu.make_async_copy(ref, ref, sem).wait()

        def wait_halo(ref, halo, sem, far):
            wait_all(ref.at[pl.ds(0, halo.vectors[far])], sem.at[far])

        def wait_sent(ref, halo, sem):
            wait_all(ref.at[pl.ds(0, sum(halo.vectors))], sem)

        def y_lanes(dst, halo, dz):
            low, high = dst[halo.slot[(0, -1, dz)]], dst[halo.slot[(0, 1, dz)]]
            return jnp.where(ey >= 2, low, rotate(high, -2 * halo.n, 1))

        def x_lanes(dst, halo, dx, dz):
            def got(dy):
                at = halo.slot[(dx, dy, dz)]
                value = jnp.where(lower, dst[at, 0:1], dst[at, 1:2])
                return fan(value, -1)

            corner = jnp.where(ey >= 2, got(-1), rotate(got(1), -2, 1))
            return jnp.where(pair >= halo.n, corner, got(0))

        def xy_corner(dst, halo, dx):
            low, high = dst[halo.slot[(dx, -1, 0)], 0:4], dst[halo.slot[(dx, 1, 0)], 0:4]
            low, high = jnp.concatenate([low, low], 0), jnp.concatenate([high, high], 0)
            low = jnp.where(lower, low, rotate(low, 2, 0))
            high = jnp.where(lower, high, rotate(high, 6, 0))
            return jnp.where(ey >= 2, low, high)

        def unlane(low, high, k):
            return z_mask * jnp.where(
                lane < 2, rotate(low, -2 * k, 1), rotate(high, 126 - 2 * k, 1)
            )

        def receive(dst, halo, sem, put):
            n = halo.n

            def at(o, k=0):
                return dst[halo.slot[o] + k]

            wait_halo(dst, halo, sem, 0)
            own_lo = [dst[halo.slot[(0, 0, -1)] + k] for k in range(halo.own_z)]
            own_hi = [dst[halo.slot[(0, 0, 1)] + k] for k in range(halo.own_z)]
            for i in range(n):
                for j in range(n):
                    k = i * n + j
                    put(1, i, j, unlane(own_lo[k // 64], own_hi[k // 64], k % 64))
            low, high = y_lanes(dst, halo, -1), y_lanes(dst, halo, 1)
            for k in range(n):
                put(0, k, n, y_mask * jnp.where(ey >= 2, at((0, -1, 0), k), at((0, 1, 0), k)))
                put(1, k, n, y_mask * unlane(low, high, k))
                put(0, n, k, fx_lo * at((-1, 0, 0), k))
                put(0, n + 1, k, fx_hi * at((1, 0, 0), k))
            wait_halo(dst, halo, sem, 1)
            below = x_lanes(dst, halo, -1, -1), x_lanes(dst, halo, -1, 1)
            above = x_lanes(dst, halo, 1, -1), x_lanes(dst, halo, 1, 1)
            for k in range(n):
                put(1, n, k, fx_lo * unlane(*below, k))
                put(1, n + 1, k, fx_hi * unlane(*above, k))
            put(0, n, n, fx_lo * y_mask * xy_corner(dst, halo, -1))
            put(1, n, n, fx_lo * y_mask * unlane(*below, n))
            put(0, n + 1, n, fx_hi * y_mask * xy_corner(dst, halo, 1))
            put(1, n + 1, n, fx_hi * y_mask * unlane(*above, n))

        def from_x(u, plo, phi, hf, hs, lf, ls):
            face_lo = rotate(jnp.where(lower, u[hf], plo), 4, 1)
            next_lo = jnp.where(lower, plo, rotate(u[hs], 4, 1))
            face_hi = rotate(jnp.where(lower, phi, u[lf]), 4, 1)
            next_hi = jnp.where(lower, rotate(u[ls], 4, 1), phi)
            return face_lo, next_lo, face_hi, next_hi

        def from_y(u, h, hf, hs, lf, ls):
            turned = rotate(h, 4, 1)
            face_lo = rotate(jnp.where(ey == 3, turned, u(hf)), 1, 1)
            next_lo = jnp.where(ey == 0, rotate(h, 6, 1), rotate(u(hs), 1, 1))
            face_hi = rotate(jnp.where(ey == 0, turned, u(lf)), 7, 1)
            next_hi = jnp.where(ey == 3, rotate(h, 2, 1), rotate(u(ls), 7, 1))
            return face_lo, next_lo, face_hi, next_hi

        def gather_send(it):
            u = raw[it].reshape(8, 8, 8, 128)
            parts = pack(u, IN)
            link = (gs.at[it], gr.at[it], gsend.at[it], grecv.at[it])
            store_and_send([raw[it, k] for k in range(64)], parts, parts, IN, link)

        def gather_receive(it):
            def put(tile, i, j, value):
                ug[tile, i, j] = value

            receive(gr.at[it], IN, grecv.at[it], put)
            ug[0, 0:8, 0:8] = raw[it].reshape(8, 8, 8, 128)
            for tile in range(2):
                u = [ug[tile, i] for i in range(10)]
                face_lo, next_lo, face_hi, next_hi = from_x(u, u[8], u[9], 7, 6, 0, 1)
                wide = [next_lo, u[0] + face_lo] + u[1:7]
                wide += [(u[7] + face_hi) * x_mask, next_hi]
                for i in range(10):
                    w = wide[i]
                    face_lo, next_lo, face_hi, next_hi = from_y(
                        lambda j: w[j : j + 1], w[8:9], 7, 6, 0, 1
                    )
                    e[tile, i, 0:1] = next_lo
                    e[tile, i, 1:2] = w[0:1] + face_lo
                    e[tile, i, 2:8] = w[1:7]
                    e[tile, i, 8:9] = w[7:8] + face_hi
                    e[tile, i, 9:10] = next_hi
                x[it, tile] = e[tile, 1:9, 1:9].reshape(64, 8, 128)

        def halves(v, even, odd):
            plus = [v[a] + v[9 - a] for a in range(5)]
            minus = [v[a] - v[9 - a] for a in range(5)]
            out = []
            for k in range(10):
                part = plus if k % 2 == 0 else minus
                total = part[0] * float(SINE[0, k])
                for a in range(1, 5):
                    total = total + part[a] * float(SINE[a, k])
                out.append(total)
            return out

        def unhalves(f):
            first, last = [], []
            for a in range(5):
                even = f[0] * float(SINE[a, 0])
                odd = f[1] * float(SINE[a, 1])
                for k in range(1, 5):
                    even = even + f[2 * k] * float(SINE[a, 2 * k])
                    odd = odd + f[2 * k + 1] * float(SINE[a, 2 * k + 1])
                first.append(even + odd)
                last.append(even - odd)
            return first + last[::-1]

        def boxes(it):
            wide = jnp.concatenate(
                [e[0].reshape(800, 128), e[1].reshape(800, 128)], axis=1
            )
            modes = jnp.dot(wide, fwd_ref[...], precision=lax.Precision.HIGH,
                            preferred_element_type=F32)
            sp[0] = modes[:, :128].reshape(10, 10, 8, 128)
            sp[1] = modes[:, 128:].reshape(10, 10, 8, 128)

            def along_x(j, carry):
                for tile in range(2):
                    out = halves([sp[tile, i, j] for i in range(10)], None, None)
                    for i in range(10):
                        sp[tile, i, j] = out[i]
                return carry

            def middle(i, total):
                for tile in range(2):
                    f = halves([sp[tile, i, j] for j in range(10)], None, None)
                    scale = icb[tile]
                    g = [f[j] * (inv_ref[tile, i, j : j + 1] * scale) for j in range(10)]
                    for j in range(10):
                        total = total + f[j] * g[j]
                    out = unhalves(g)
                    for j in range(10):
                        sp[tile, i, j] = out[j]
                return total

            def back_x(j, carry):
                for tile in range(2):
                    out = unhalves([sp[tile, i, j] for i in range(10)])
                    for i in range(10):
                        sp[tile, i, j] = out[i]
                return carry

            lax.fori_loop(0, 10, along_x, 0)
            acc[2 * it] = lax.fori_loop(0, 10, middle, jnp.zeros((8, 128), F32))
            lax.fori_loop(0, 10, back_x, 0)
            wide = jnp.concatenate(
                [sp[0].reshape(800, 128), sp[1].reshape(800, 128)], axis=1
            )
            back = jnp.dot(wide, bwd_ref[...], precision=lax.Precision.HIGH,
                           preferred_element_type=F32)
            sp[0] = back[:, :128].reshape(10, 10, 8, 128)
            sp[1] = back[:, 128:].reshape(10, 10, 8, 128)

        def scatter_send(it):
            own = [sp[1, k // 10, k % 10] for k in range(100)]
            link = (ss.at[it], sr.at[it], ssend.at[it], srecv.at[it])
            store_and_send(own, pack(sp[0], OUT), pack(sp[1], OUT), OUT, link)

        def scatter_receive(it):
            halves = {}

            def put(tile, i, j, value):
                if i < 10 and j < 10:
                    us[i, j] = sp[0, i, j] + value
                elif (i, j) in halves:
                    us[i, j] = halves.pop((i, j)) + value
                else:
                    halves[i, j] = value

            receive(sr.at[it], OUT, srecv.at[it], put)
            u = [us[i] for i in range(12)]
            face_lo, next_lo, face_hi, next_hi = from_x(u, u[10], u[11], 8, 9, 1, 0)
            fold = [u[1] + face_lo, u[2] + next_lo, u[3], u[4], u[5], u[6],
                    u[7] + next_hi, (u[8] + face_hi) * x_mask]
            for i in range(8):
                w = fold[i]
                last = x_mask if i == 7 else 1.0
                face_lo, next_lo, face_hi, next_hi = from_y(
                    lambda j: w[j : j + 1], w[10:11], 8, 9, 1, 0
                )
                zs[it, 8 * i : 8 * i + 1] = (w[1:2] + face_lo) * last
                zs[it, 8 * i + 1 : 8 * i + 2] = (w[2:3] + next_lo) * last
                zs[it, 8 * i + 2 : 8 * i + 6] = w[3:7] * last
                zs[it, 8 * i + 6 : 8 * i + 7] = (w[7:8] + next_hi) * last
                zs[it, 8 * i + 7 : 8 * i + 8] = (w[8:9] + face_hi) * last

        def derive(v, matrix):
            plus = [v[k] + v[7 - k] for k in range(4)]
            minus = [v[k] - v[7 - k] for k in range(4)]
            first, last = [], []
            for a in range(4):
                even = odd = None
                for k in range(4):
                    p = plus[k] * float(0.5 * (matrix[a, k] + matrix[a, 7 - k]))
                    m = minus[k] * float(0.5 * (matrix[a, k] - matrix[a, 7 - k]))
                    even = p if even is None else even + p
                    odd = m if odd is None else odd + m
                first.append(even + odd)
                last.append(odd - even)
            return first + last[::-1]

        def stiffness(it):
            def over_x(j, carry):
                grad = derive([zs[it, 8 * i + j] for i in range(8)], DERIV)
                flux = [grad[i] * wc[8 * i + j] for i in range(8)]
                out = derive(flux, DERIV.T)
                for i in range(8):
                    raw[it + 1, 8 * i + j] = out[i]
                return carry

            def over_y(i, carry):
                grad = derive([zs[it, 8 * i + j] for j in range(8)], DERIV)
                flux = [grad[j] * wc[8 * i + j] for j in range(8)]
                out = derive(flux, DERIV.T)
                for j in range(8):
                    raw[it + 1, 8 * i + j] = raw[it + 1, 8 * i + j] + out[j]
                return carry

            lax.fori_loop(0, 8, over_x, 0)
            lax.fori_loop(0, 8, over_y, 0)
            field = zs[it].reshape(512, 128)
            grad = jnp.dot(field, der_ref[0], precision=lax.Precision.HIGH,
                           preferred_element_type=F32)
            flux = grad * wc[...].reshape(512, 128)
            out = jnp.dot(flux, der_ref[1], precision=lax.Precision.HIGH,
                          preferred_element_type=F32)
            total = raw[it + 1].reshape(512, 128) + out
            raw[it + 1] = total.reshape(64, 8, 128)
            acc[2 * it + 1] = jnp.sum((total * field).reshape(64, 8, 128), axis=0)

        def far_first(count, length):
            return sorted(range(1, count), key=lambda t: -length(t))

        rings = (
            (red_xy, ny * runs, gz // z_run * ny + gy, ring_xy,
             far_first(ny * runs, lambda t: min(t // ny, runs - t // ny)
                       + min(t % ny, ny - t % ny) / 2)),
            (red_z, ring, gx * z_run + gz % z_run, ring_z,
             far_first(ring, lambda t: min(t, ring - t))),
        )

        def reduce_start(phase, value):
            ref, count, me, to, order = rings[phase]
            ref[me, 0:1] = value
            for t in order:
                pltpu.make_async_remote_copy(
                    src_ref=ref.at[me, pl.ds(0, 1)],
                    dst_ref=ref.at[me, pl.ds(0, 1)],
                    send_sem=rsend.at[phase],
                    recv_sem=rrecv.at[phase],
                    device_id=to(t),
                    device_id_type=MESH,
                ).start()

        def reduce_wait(phase):
            ref, count = rings[phase][:2]
            if count > 1:
                wait_all(ref.at[pl.ds(0, count - 1), pl.ds(0, 1)], rrecv.at[phase])
            return jnp.sum(ref[0:count, 0:1], axis=0)

        def reduce_end(phase):
            ref, count = rings[phase][:2]
            if count > 1:
                wait_all(ref.at[pl.ds(0, count - 1), pl.ds(0, 1)], rsend.at[phase])

        def relaid(ref, store):
            for i in range(8):
                for j in range(8):
                    store(8 * i + j, ref[i, pl.ds(j, 8, stride=8), :])

        def put_b(k, value):
            raw[0, k] = value

        def put_c(k, value):
            zs[0, k] = value

        loads[0].wait()
        loads[1].wait()
        relaid(b_rows, put_b)
        pl.semaphore_wait(barrier, len(partners))
        gather_send(0)
        for copy in loads[2:]:
            copy.wait()
        relaid(c_rows, put_c)
        mean = jnp.dot(jnp.sum(zs[0], axis=0), mean_ref[...], precision=lax.Precision.HIGHEST,
                       preferred_element_type=F32)
        icb[0] = 1.0 / mean[:, :128]
        icb[1] = 1.0 / mean[:, 128:]
        for i in range(8):
            wc[8 * i : 8 * i + 8] = zs[0, 8 * i : 8 * i + 8] * (wyz_ref[...] * float(WEIGHTS[i]))

        def step(it, carry):
            gather_receive(it)
            boxes(it)
            scatter_send(it)
            scatter_receive(it)
            stiffness(it)

            @pl.when(it == 1)
            def _():
                local = jnp.zeros((1, 128), F32)
                for k in range(4):
                    total = jnp.sum(acc[k], axis=(0, 1), keepdims=True)
                    local = jnp.where(lane[0:1] == k, total, local)
                reduce_start(0, local)

            gather_send(it + 1)
            return carry

        lax.fori_loop(0, 2, step, 0)
        reduce_start(1, reduce_wait(0))
        gather_receive(2)
        sums = reduce_wait(1)
        rho, delta, gamma, eps = (sums[:, k : k + 1] for k in range(4))
        a0 = rho / delta
        rz = a0 * a0 * gamma - rho
        up = 1.0 + rz / rho
        curve = up * up * delta - 2.0 * a0 * up * gamma + a0 * a0 * eps
        a1 = rz / curve
        first = a0 + a1 * up
        second = a1 * a0

        def write(values, ref):
            for k in range(64):
                for ex in range(2):
                    ref[8 * ex + k // 8, pl.ds(k % 8, 4, stride=8), :] = values[
                        k, 4 * ex : 4 * ex + 4
                    ]

        write(zs[0] * first - zs[1] * second, sol_ref)
        mixed = x[0] - x[1] * first + x[2] * second
        wide = jnp.concatenate(
            [mixed[0].reshape(512, 128), mixed[1].reshape(512, 128)], axis=1
        )
        out = jnp.dot(wide, asm_ref[...], precision=lax.Precision.HIGH,
                      preferred_element_type=F32)
        write(out.reshape(64, 8, 128), res_ref)
        for it in range(3):
            wait_sent(gr.at[it], IN, gsend.at[it])
        for it in range(2):
            wait_sent(sr.at[it], OUT, ssend.at[it])
        for phase in range(2):
            reduce_end(phase)

    return kernel


def solution(mesh):
    sizes = tuple(mesh.shape[a] for a in AXES)
    z_run = 4 if sizes[2] % 4 == 0 else sizes[2]
    ring = sizes[0] * z_run
    forward, assemble = z_tables(16)
    der = np.kron(np.eye(16), DERIV)
    inverse = np.zeros((2, 10, 10, 128))
    tiled = np.tile(INVERSE, (1, 1, 16))
    inverse[0] = tiled[:, :, :128]
    inverse[1, :, :, :32] = tiled[:, :, 128:]
    mean = np.zeros((128, 256))
    mean[:, :160] = np.kron(np.eye(16), np.ones((8, 10))) / SIDE**3
    mean[0, 160:] = 1.0
    wyz = np.broadcast_to(
        WEIGHTS[:, None, None] * np.tile(WEIGHTS, 16)[None, None, :], (8, 8, 128)
    )
    tables = [
        jnp.asarray(t, F32)
        for t in (wyz, forward, forward.T, assemble, np.stack([der.T, der]), inverse, mean)
    ]
    vmem = pl.BlockSpec(memory_space=pltpu.VMEM)
    dma = pltpu.SemaphoreType.DMA

    def block(*shape):
        return pltpu.VMEM(shape + (8, 128), F32)

    call = pl.pallas_call(
        make_kernel(sizes, z_run),
        out_shape=[jax.ShapeDtypeStruct((16, 32, 128), F32)] * 2,
        in_specs=[pl.BlockSpec(memory_space=pltpu.HBM)] * 9,
        out_specs=[vmem] * 2,
        scratch_shapes=[
            pltpu.VMEM((8, 64, 128), F32), pltpu.VMEM((8, 64, 128), F32),
            *[pltpu.VMEM(t.shape, F32) for t in tables],
            block(3, 64), block(64), block(2),
            block(3, IN.total), block(3, IN.received), block(2, 10, 9), block(2, 10, 10),
            block(3, 2, 64), block(2, 10, 10),
            block(2, OUT.total), block(2, OUT.received), block(12, 11),
            block(2, 64), block(4),
            block(sizes[1] * sizes[2] // z_run), block(ring),
            dma((3,)), dma((3, 2)), dma((2,)), dma((2, 2)), dma((2,)), dma((2,)), dma((11,)),
        ],
        compiler_params=pltpu.CompilerParams(
            collective_id=0, has_side_effects=True, vmem_limit_bytes=60 * 1024 * 1024
        ),
    )

    def shards(right_side, coefficient):
        return tuple(call(right_side, coefficient, *tables))

    spec = P(*AXES)
    return jax.shard_map(
        shards, mesh=mesh, in_specs=(spec, spec), out_specs=(spec, spec), check_vma=False
    )
```

```python
import itertools

import jax
import jax.numpy as jnp
import numpy as np
from jax import lax
from jax.experimental import pallas as pl
from jax.experimental.pallas import tpu as pltpu
from jax.sharding import PartitionSpec as P

ORDER = 7
SIDE = ORDER + 1
BOX = ORDER + 3
AXES = ("gx", "gy", "gz")
MESH = pl.DeviceIdType.MESH
F32 = jnp.float32
NEAR = sorted(
    (o for o in itertools.product((-1, 0, 1), repeat=3) if o != (0, 0, 0)),
    key=lambda o: [(1, 1, 1), (1, 0, 1), (1, 1, 0), (0, 1, 1), (0, 0, 1), (1, 0, 0),
                   (0, 1, 0)].index(tuple(map(abs, o))),
)


def legendre_rows(points, degree):
    table_rows = [np.ones(points.shape), points * 1.0]
    for k in range(2, degree + 1):
        table_rows.append(
            ((2 * k - 1) * points * table_rows[k - 1] - (k - 1) * table_rows[k - 2]) / k
        )
    return table_rows


def lobatto_tables(degree):
    per_side = degree + 1
    points = np.cos(np.pi * np.arange(per_side) / degree)
    for newton_step in range(60):
        table_rows = legendre_rows(points, degree)
        points = points - (points * table_rows[degree] - table_rows[degree - 1]) / (
            per_side * table_rows[degree]
        )
    top_row = legendre_rows(points, degree)[degree][::-1]
    points = points[::-1]
    weights = 2.0 / (degree * per_side * top_row**2)
    deriv_np = np.zeros((per_side, per_side))
    for a in range(per_side):
        for b in range(per_side):
            if a != b:
                deriv_np[a, b] = top_row[a] / (top_row[b] * (points[a] - points[b]))
    deriv_np[0, 0] = -degree * per_side / 4.0
    deriv_np[-1, -1] = degree * per_side / 4.0
    return (weights, deriv_np)


def sine_tables(degree):
    box_side = degree + 3
    grid_index = np.arange(1, box_side + 1)
    sine_np = np.sqrt(2.0 / (box_side + 1)) * np.sin(
        np.pi * np.outer(grid_index, grid_index) / (box_side + 1)
    )
    eigen_values = 2.0 - 2.0 * np.cos(np.pi * grid_index / (box_side + 1))
    summed = eigen_values[:, None, None] + eigen_values[None, :, None] + eigen_values[None, None, :]
    return (sine_np, 1.0 / summed)


WEIGHTS, DERIV = lobatto_tables(ORDER)
SINE, INVERSE = sine_tables(ORDER)


def z_tables(elements):
    span = elements * SIDE
    assemble = np.zeros((span + 2, 2 * span))
    for i in range(span):
        assemble[1 + i, i] = 1.0
        if i % SIDE == 0 and i > 0:
            assemble[1 + i, i - 1] = 1.0
        if i % SIDE == SIDE - 1 and i < span - 1:
            assemble[1 + i, i + 1] = 1.0
    assemble[0, span] = 1.0
    assemble[1, span + 1] = 1.0
    assemble[span, 2 * span - 2] = 1.0
    assemble[span + 1, 2 * span - 1] = 1.0
    gather = np.zeros((elements * BOX, span + 2))
    for e in range(elements):
        gather[e * BOX, 0 if e == 0 else 1 + SIDE * e - 2] = 1.0
        for k in range(SIDE):
            gather[e * BOX + 1 + k, 1 + SIDE * e + k] = 1.0
        gather[e * BOX + BOX - 1, span + 1 if e == elements - 1 else 1 + SIDE * (e + 1) + 1] = 1.0
    to_modes = np.kron(np.eye(elements), SINE) @ gather @ assemble
    forward = np.zeros((2 * span, 2 * span))
    forward[:, : elements * BOX] = to_modes.T
    return forward, assemble[1:-1].T


def rotate(x, shift, axis):
    return pltpu.roll(x, shift % x.shape[axis], axis)


class Halo:
    def __init__(self, n, hf, hs, lf, ls):
        self.n, self.hf, self.hs, self.lf, self.ls = n, hf, hs, lf, ls
        self.own_z = -(-n * n // 64)
        self.corner = 4 * n
        self.z_part = {1: 4 * n + 4, -1: 4 * n + 7 + self.own_z}
        self.total = 4 * n + 10 + 2 * self.own_z
        self.slot, at, height = {}, 0, [0, 0]
        for o in NEAR:
            _, count, tall = self.part(o)
            self.slot[o] = at
            at += count
            height[tall < 8] += count * tall
        self.received = at
        self.vectors = [h // 8 for h in height]

    def part(self, o):
        n = self.n
        if o[2]:
            base = self.z_part[o[2]]
            if o[0]:
                return (base + self.own_z + (1 if o[0] > 0 else 2), 1, 2)
            return (base + self.own_z, 1, 8) if o[1] else (base, self.own_z, 8)
        if o[0] == 0:
            return (0 if o[1] > 0 else n, n, 8)
        if o[1] == 0:
            return (2 * n if o[0] > 0 else 3 * n, n, 8)
        return (4 * n + [(1, 1), (1, -1), (-1, 1), (-1, -1)].index(o[:2]), 1, 4)


IN = Halo(SIDE, 7, 6, 0, 1)
OUT = Halo(BOX, 8, 9, 1, 0)


def make_kernel(sizes, z_run):
    nx, ny, nz = sizes
    runs = nz // z_run
    ring = nx * z_run

    def kernel(b_ref, c_ref, *rest):
        tables, rest = rest[:7], rest[7:]
        (sol_ref, res_ref, b_rows, c_rows, wyz_ref, fwd_ref, bwd_ref, asm_ref, der_ref, inv_ref,
         mean_ref, raw, wc, icb, gs, gr, ug, e, x, sp, sq, fl, ss, sr, us, zs, acc,
         red_xy, red_z, gsend, grecv, ssend, srecv, rsend, rrecv, load, fin) = rest
        gx, gy, gz = (lax.axis_index(a) for a in AXES)

        def near(o):
            return ((gx + o[0] + nx) % nx, (gy + o[1] + ny) % ny, (gz + o[2] + nz) % nz)

        def ring_xy(t):
            to = (gz // z_run + t // ny) % runs
            return (gx, (gy + t % ny) % ny, to * z_run + gz % z_run)

        def ring_z(t):
            to = (gx * z_run + gz % z_run + t) % ring
            return (to // z_run, gy, (gz // z_run) * z_run + to % z_run)

        partners = [near(o) for o in NEAR]
        partners += [ring_xy(t) for t in range(1, ny * runs)]
        partners += [ring_z(t) for t in range(1, ring)]
        barrier = pltpu.get_barrier_semaphore()
        for device in partners:
            pl.semaphore_signal(barrier, inc=1, device_id=device, device_id_type=MESH)

        loads = []
        for source, target in ((b_ref, b_rows), (c_ref, c_rows)):
            for ex in range(2):
                loads.append((source.at[pl.ds(8 * ex, 8)], target.at[:, pl.ds(32 * ex, 32)]))
        kept = (wyz_ref, fwd_ref, bwd_ref, asm_ref, der_ref, inv_ref, mean_ref)
        loads += list(zip(tables, kept))
        loads = [
            pltpu.make_async_copy(source, target, load.at[k])
            for k, (source, target) in enumerate(loads)
        ]
        for copy in loads:
            copy.start()

        sub = lax.broadcasted_iota(jnp.int32, (8, 128), 0)
        lane = lax.broadcasted_iota(jnp.int32, (8, 128), 1)
        pair = lane // 2
        ey = sub % 4
        lower = sub < 4

        def flag(condition):
            return jnp.where(condition, 1.0, 0.0).astype(F32)

        fx_lo, fx_hi = flag(gx > 0), flag(gx < nx - 1)
        fy_lo, fy_hi = flag(gy > 0), flag(gy < ny - 1)
        fz_lo, fz_hi = flag(gz > 0), flag(gz < nz - 1)
        y_mask = jnp.where(ey >= 2, fy_lo, fy_hi)
        z_mask = jnp.where(lane < 2, fz_lo, jnp.where(lane >= 126, fz_hi, 0.0))
        x_mask = jnp.where(lower, 1.0, fx_hi)

        def y_plane(row, halo, up):
            if up:
                return jnp.where(ey == 3, row[halo.hf], rotate(row[halo.hs], 7, 0))
            return jnp.where(ey == 0, row[halo.lf], rotate(row[halo.ls], 1, 0))

        def x_planes(u, halo):
            out = []
            for up in (True, False):
                rows = (halo.hf, halo.hs) if up else (halo.lf, halo.ls)
                pairs = [(u[rows[0]][j], u[rows[1]][j]) for j in range(halo.n)]
                pairs += [tuple(y_plane(u[r], halo, y) for r in rows) for y in (True, False)]
                out.append([
                    jnp.where(lower, rotate(back, 4, 0), front) if up
                    else jnp.where(lower, front, rotate(back, 4, 0))
                    for front, back in pairs
                ])
            return out

        def lane_pack(values, up):
            total = None
            for k, value in enumerate(values):
                moved = rotate(value, 2 * k + 2 if up else 2 * k, 1)
                total = moved if total is None else jnp.where(pair == k, moved, total)
            return total

        def fan(value, sign):
            turned = value
            for k in range(1, 4):
                turned = jnp.where(ey == k, rotate(value, sign * 32 * k, 1), turned)
            return turned

        def sender(halo, link):
            src, dst, send_sem, recv_sem = link
            n = halo.n
            ends = ((True, halo.z_part[1]), (False, halo.z_part[-1]))

            def send(*kinds):
                for o in NEAR:
                    if tuple(map(abs, o)) not in kinds:
                        continue
                    at, count, tall = halo.part(o)
                    to = halo.slot[(-o[0], -o[1], -o[2])]
                    pltpu.make_async_remote_copy(
                        src_ref=src.at[pl.ds(at, count), pl.ds(0, tall)],
                        dst_ref=dst.at[pl.ds(to, count), pl.ds(0, tall)],
                        send_sem=send_sem,
                        recv_sem=recv_sem.at[1 if tall < 8 else 0],
                        device_id=near(o),
                        device_id_type=MESH,
                    ).start()

            def send_x(planes, lanes):
                lanes, planes = x_planes(lanes, halo), x_planes(planes, halo)
                for up, base in ends:
                    for k in range(2):
                        moved = fan(lane_pack(lanes[k], up), 1)
                        moved = jnp.where(lane // 32 == ey, moved, 0.0)
                        at = base + halo.own_z + 1 + k
                        src[at, 0:1] = jnp.sum(moved[0:4], axis=0, keepdims=True)
                        src[at, 1:2] = jnp.sum(moved[4:8], axis=0, keepdims=True)
                send((1, 1, 1), (1, 0, 1))
                for k in range(4):
                    corner = planes[k // 2][n + k % 2]
                    if k % 2 == 0:
                        corner = jnp.where(sub < 2, rotate(corner, 2, 0), corner)
                    else:
                        corner = jnp.where(sub < 2, corner, rotate(corner, 6, 0))
                    src[4 * n + k, 0:4] = corner[0:4]
                send((1, 1, 0))
                for k in range(2):
                    for j in range(n):
                        src[(2 + k) * n + j] = planes[k][j]
                send((1, 0, 0))

            def send_rest(planes, lanes, own):
                for up, base in ends:
                    edge = [y_plane(lanes[i], halo, y) for y in (True, False) for i in range(n)]
                    src[base + halo.own_z] = lane_pack(edge, up)
                send((0, 1, 1))
                for up, base in ends:
                    for k in range(halo.own_z):
                        src[base + k] = lane_pack(own[64 * k : 64 * k + 64], up)
                send((0, 0, 1))
                for i in range(n):
                    src[i] = y_plane(planes[i], halo, True)
                    src[n + i] = y_plane(planes[i], halo, False)
                send((0, 1, 0))

            return send_x, send_rest

        def wait_all(ref, sem):
            pltpu.make_async_copy(ref, ref, sem).wait()

        def wait_halo(ref, halo, sem, far):
            wait_all(ref.at[pl.ds(0, halo.vectors[far])], sem.at[far])

        def wait_sent(ref, halo, sem):
            wait_all(ref.at[pl.ds(0, sum(halo.vectors))], sem)

        def y_lanes(dst, halo, dz):
            low, high = dst[halo.slot[(0, -1, dz)]], dst[halo.slot[(0, 1, dz)]]
            return jnp.where(ey >= 2, low, rotate(high, -2 * halo.n, 1))

        def x_lanes(dst, halo, dx, dz):
            def got(dy):
                at = halo.slot[(dx, dy, dz)]
                value = jnp.where(lower, dst[at, 0:1], dst[at, 1:2])
                return fan(value, -1)

            corner = jnp.where(ey >= 2, got(-1), rotate(got(1), -2, 1))
            return jnp.where(pair >= halo.n, corner, got(0))

        def xy_corner(dst, halo, dx):
            low, high = dst[halo.slot[(dx, -1, 0)], 0:4], dst[halo.slot[(dx, 1, 0)], 0:4]
            low, high = jnp.concatenate([low, low], 0), jnp.concatenate([high, high], 0)
            low = jnp.where(lower, low, rotate(low, 2, 0))
            high = jnp.where(lower, high, rotate(high, 6, 0))
            return jnp.where(ey >= 2, low, high)

        def unlane(low, high, k):
            return z_mask * jnp.where(
                lane < 2, rotate(low, -2 * k, 1), rotate(high, 126 - 2 * k, 1)
            )

        def receive(dst, halo, sem, put):
            n = halo.n

            def at(o, k=0):
                return dst[halo.slot[o] + k]

            wait_halo(dst, halo, sem, 0)
            own_lo = [dst[halo.slot[(0, 0, -1)] + k] for k in range(halo.own_z)]
            own_hi = [dst[halo.slot[(0, 0, 1)] + k] for k in range(halo.own_z)]
            for i in range(n):
                for j in range(n):
                    k = i * n + j
                    put(1, i, j, unlane(own_lo[k // 64], own_hi[k // 64], k % 64))
            low, high = y_lanes(dst, halo, -1), y_lanes(dst, halo, 1)
            for k in range(n):
                put(0, k, n, y_mask * jnp.where(ey >= 2, at((0, -1, 0), k), at((0, 1, 0), k)))
                put(1, k, n, y_mask * unlane(low, high, k))
                put(0, n, k, fx_lo * at((-1, 0, 0), k))
                put(0, n + 1, k, fx_hi * at((1, 0, 0), k))
            wait_halo(dst, halo, sem, 1)
            below = x_lanes(dst, halo, -1, -1), x_lanes(dst, halo, -1, 1)
            above = x_lanes(dst, halo, 1, -1), x_lanes(dst, halo, 1, 1)
            for k in range(n):
                put(1, n, k, fx_lo * unlane(*below, k))
                put(1, n + 1, k, fx_hi * unlane(*above, k))
            put(0, n, n, fx_lo * y_mask * xy_corner(dst, halo, -1))
            put(1, n, n, fx_lo * y_mask * unlane(*below, n))
            put(0, n + 1, n, fx_hi * y_mask * xy_corner(dst, halo, 1))
            put(1, n + 1, n, fx_hi * y_mask * unlane(*above, n))

        def from_x(u, plo, phi, hf, hs, lf, ls):
            face_lo = rotate(jnp.where(lower, u[hf], plo), 4, 1)
            next_lo = jnp.where(lower, plo, rotate(u[hs], 4, 1))
            face_hi = rotate(jnp.where(lower, phi, u[lf]), 4, 1)
            next_hi = jnp.where(lower, rotate(u[ls], 4, 1), phi)
            return face_lo, next_lo, face_hi, next_hi

        def from_y(u, h, hf, hs, lf, ls):
            turned = rotate(h, 4, 1)
            face_lo = rotate(jnp.where(ey == 3, turned, u(hf)), 1, 1)
            next_lo = jnp.where(ey == 0, rotate(h, 6, 1), rotate(u(hs), 1, 1))
            face_hi = rotate(jnp.where(ey == 0, turned, u(lf)), 7, 1)
            next_hi = jnp.where(ey == 3, rotate(h, 2, 1), rotate(u(ls), 7, 1))
            return face_lo, next_lo, face_hi, next_hi

        def gather_sender(it):
            return sender(IN, (gs.at[it], gr.at[it], gsend.at[it], grecv.at[it]))

        def gather_x(it):
            rows = {i: raw[it, 8 * i : 8 * i + 8] for i in (0, 1, 6, 7)}
            gather_sender(it)[0](rows, rows)

        def gather_rest(it):
            rows = [raw[it, 8 * i : 8 * i + 8] for i in range(8)]
            gather_sender(it)[1](rows, rows, [raw[it, k] for k in range(64)])

        def gather_receive(it):
            def put(tile, i, j, value):
                ug[tile, i, j] = value

            receive(gr.at[it], IN, grecv.at[it], put)
            ug[0, 0:8, 0:8] = raw[it].reshape(8, 8, 8, 128)
            for tile in range(2):
                u = [ug[tile, i] for i in range(10)]
                face_lo, next_lo, face_hi, next_hi = from_x(u, u[8], u[9], 7, 6, 0, 1)
                wide = [next_lo, u[0] + face_lo] + u[1:7]
                wide += [(u[7] + face_hi) * x_mask, next_hi]
                for i in range(10):
                    w = wide[i]
                    face_lo, next_lo, face_hi, next_hi = from_y(
                        lambda j: w[j : j + 1], w[8:9], 7, 6, 0, 1
                    )
                    e[tile, i, 0:1] = next_lo
                    e[tile, i, 1:2] = w[0:1] + face_lo
                    e[tile, i, 2:8] = w[1:7]
                    e[tile, i, 8:9] = w[7:8] + face_hi
                    e[tile, i, 9:10] = next_hi
                x[it, tile] = e[tile, 1:9, 1:9].reshape(64, 8, 128)

        def to_modes(v):
            plus = [v[a] + v[9 - a] for a in range(5)]
            minus = [v[a] - v[9 - a] for a in range(5)]
            out = []
            for k in range(10):
                part = plus if k % 2 == 0 else minus
                total = part[0] * float(SINE[0, k])
                for a in range(1, 5):
                    total = total + part[a] * float(SINE[a, k])
                out.append(total)
            return out

        def from_modes(f, picks=range(5)):
            out = {}
            for a in picks:
                even = f[0] * float(SINE[a, 0])
                odd = f[1] * float(SINE[a, 1])
                for k in range(1, 5):
                    even = even + f[2 * k] * float(SINE[a, 2 * k])
                    odd = odd + f[2 * k + 1] * float(SINE[a, 2 * k + 1])
                out[a], out[9 - a] = even + odd, even - odd
            return out

        def boxes(it):
            for half in range(2):
                js = slice(5 * half, 5 * half + 5)
                wide = jnp.concatenate(
                    [e[0, :, js].reshape(400, 128), e[1, :, js].reshape(400, 128)], axis=1
                )
                modes = jnp.dot(wide, fwd_ref[...], precision=lax.Precision.HIGH,
                                preferred_element_type=F32)
                for tile in range(2):
                    part = modes[:, 128 * tile : 128 * tile + 128].reshape(10, 5, 8, 128)
                    out = to_modes([part[i] for i in range(10)])
                    for i in range(10):
                        sp[tile, i, js] = out[i]

            def middle(i, total):
                for tile in range(2):
                    f = to_modes([sp[tile, i, j] for j in range(10)])
                    scale = icb[tile]
                    g = [f[j] * (inv_ref[tile, i, j : j + 1] * scale) for j in range(10)]
                    for j in range(10):
                        total = total + f[j] * g[j]
                    out = from_modes(g)
                    for j in range(10):
                        sp[tile, i, j] = out[j]
                return total

            acc[2 * it] = lax.fori_loop(0, 10, middle, jnp.zeros((8, 128), F32), unroll=5)
            send_x, send_rest = sender(OUT, (ss.at[it], sr.at[it], ssend.at[it], srecv.at[it]))

            def answers(picks, spans):
                def back_x(j, carry):
                    for tile in range(2):
                        out = from_modes([sp[tile, i, j] for i in range(10)], picks)
                        for i, value in out.items():
                            sq[tile, i, j] = value
                    return carry

                lax.fori_loop(0, 10, back_x, 0, unroll=5)
                wide = jnp.concatenate(
                    [
                        jnp.concatenate([sq[tile, i0:i1] for i0, i1 in spans]).reshape(-1, 128)
                        for tile in range(2)
                    ],
                    axis=1,
                )
                back = jnp.dot(wide, bwd_ref[...], precision=lax.Precision.HIGH,
                               preferred_element_type=F32)
                at = 0
                for i0, i1 in spans:
                    rows = back[80 * at : 80 * (at + i1 - i0)]
                    for tile in range(2):
                        sq[tile, i0:i1] = rows[:, 128 * tile : 128 * tile + 128].reshape(
                            i1 - i0, 10, 8, 128
                        )
                    at += i1 - i0

            answers((0, 1), ((0, 2), (8, 10)))
            send_x({i: sq[0, i] for i in (0, 1, 8, 9)}, {i: sq[1, i] for i in (0, 1, 8, 9)})
            answers((2, 3, 4), ((2, 8),))
            own = [sq[1, k // 10, k % 10] for k in range(100)]
            send_rest([sq[0, i] for i in range(10)], [sq[1, i] for i in range(10)], own)

        def scatter_receive(it):
            halves = {}

            def put(tile, i, j, value):
                if i < 10 and j < 10:
                    us[i, j] = sq[0, i, j] + value
                elif (i, j) in halves:
                    us[i, j] = halves.pop((i, j)) + value
                else:
                    halves[i, j] = value

            receive(sr.at[it], OUT, srecv.at[it], put)
            u = [us[i] for i in range(12)]
            face_lo, next_lo, face_hi, next_hi = from_x(u, u[10], u[11], 8, 9, 1, 0)
            fold = [u[1] + face_lo, u[2] + next_lo, u[3], u[4], u[5], u[6],
                    u[7] + next_hi, (u[8] + face_hi) * x_mask]
            for i in range(8):
                w = fold[i]
                last = x_mask if i == 7 else 1.0
                face_lo, next_lo, face_hi, next_hi = from_y(
                    lambda j: w[j : j + 1], w[10:11], 8, 9, 1, 0
                )
                zs[it, 8 * i : 8 * i + 1] = (w[1:2] + face_lo) * last
                zs[it, 8 * i + 1 : 8 * i + 2] = (w[2:3] + next_lo) * last
                zs[it, 8 * i + 2 : 8 * i + 6] = w[3:7] * last
                zs[it, 8 * i + 6 : 8 * i + 7] = (w[7:8] + next_hi) * last
                zs[it, 8 * i + 7 : 8 * i + 8] = (w[8:9] + face_hi) * last

        def derive(v, matrix, picks=range(4)):
            plus = [v[k] + v[7 - k] for k in range(4)]
            minus = [v[k] - v[7 - k] for k in range(4)]
            out = {}
            for a in picks:
                even = odd = None
                for k in range(4):
                    p = plus[k] * float(0.5 * (matrix[a, k] + matrix[a, 7 - k]))
                    m = minus[k] * float(0.5 * (matrix[a, k] - matrix[a, 7 - k]))
                    even = p if even is None else even + p
                    odd = m if odd is None else odd + m
                out[a], out[7 - a] = even + odd, odd - even
            return out

        def fluxes(it):
            def over_x(j, total):
                grad = derive([zs[it, 8 * i + j] for i in range(8)], DERIV)
                for i in range(8):
                    flux = grad[i] * wc[8 * i + j]
                    total = total + flux * grad[i]
                    fl[0, 8 * i + j] = flux
                return total

            def over_y(i, total):
                grad = derive([zs[it, 8 * i + j] for j in range(8)], DERIV)
                for j in range(8):
                    flux = grad[j] * wc[8 * i + j]
                    total = total + flux * grad[j]
                    fl[1, 8 * i + j] = flux
                return total

            grad = jnp.dot(zs[it].reshape(512, 128), der_ref[0], precision=lax.Precision.HIGH,
                           preferred_element_type=F32).reshape(64, 8, 128)
            flux = grad * wc[...]
            fl[2] = flux
            total = jnp.sum(flux * grad, axis=0)
            total = lax.fori_loop(0, 8, over_x, total, unroll=8)
            acc[2 * it + 1] = lax.fori_loop(0, 8, over_y, total, unroll=8)

        def divergence(it, picks, spans):
            along_z = jnp.dot(
                jnp.concatenate([fl[2, 8 * i0 : 8 * i1] for i0, i1 in spans]).reshape(-1, 128),
                der_ref[1], precision=lax.Precision.HIGH, preferred_element_type=F32,
            ).reshape(-1, 8, 128)
            at = 0
            for i0, i1 in spans:
                raw[it + 1, 8 * i0 : 8 * i1] = along_z[at : at + 8 * (i1 - i0)]
                at += 8 * (i1 - i0)

            def over_x(j, carry):
                out = derive([fl[0, 8 * i + j] for i in range(8)], DERIV.T, picks)
                for i, value in out.items():
                    raw[it + 1, 8 * i + j] = raw[it + 1, 8 * i + j] + value
                return carry

            lax.fori_loop(0, 8, over_x, 0, unroll=8)
            for i0, i1 in spans:
                for i in range(i0, i1):
                    out = derive([fl[1, 8 * i + j] for j in range(8)], DERIV.T)
                    for j in range(8):
                        raw[it + 1, 8 * i + j] = raw[it + 1, 8 * i + j] + out[j]

        def far_first(count, length):
            return sorted(range(1, count), key=lambda t: -length(t))

        rings = (
            (red_xy, ny * runs, gz // z_run * ny + gy, ring_xy,
             far_first(ny * runs, lambda t: min(t // ny, runs - t // ny)
                       + min(t % ny, ny - t % ny) / 2)),
            (red_z, ring, gx * z_run + gz % z_run, ring_z,
             far_first(ring, lambda t: min(t, ring - t))),
        )

        def reduce_start(phase, value):
            ref, count, me, to, order = rings[phase]
            ref[me, 0:1] = value
            for t in order:
                pltpu.make_async_remote_copy(
                    src_ref=ref.at[me, pl.ds(0, 1)],
                    dst_ref=ref.at[me, pl.ds(0, 1)],
                    send_sem=rsend.at[phase],
                    recv_sem=rrecv.at[phase],
                    device_id=to(t),
                    device_id_type=MESH,
                ).start()

        def reduce_wait(phase):
            ref, count = rings[phase][:2]
            if count > 1:
                wait_all(ref.at[pl.ds(0, count - 1), pl.ds(0, 1)], rrecv.at[phase])
            return jnp.sum(ref[0:count, 0:1], axis=0)

        def reduce_end(phase):
            ref, count = rings[phase][:2]
            if count > 1:
                wait_all(ref.at[pl.ds(0, count - 1), pl.ds(0, 1)], rsend.at[phase])

        def relaid(ref, store):
            for i in range(8):
                for j in range(8):
                    store(8 * i + j, ref[i, pl.ds(j, 8, stride=8), :])

        def put_b(k, value):
            raw[0, k] = value

        def put_c(k, value):
            zs[0, k] = value

        loads[0].wait()
        loads[1].wait()
        relaid(b_rows, put_b)
        pl.semaphore_wait(barrier, len(partners))
        gather_x(0)
        gather_rest(0)
        for copy in loads[2:]:
            copy.wait()
        relaid(c_rows, put_c)
        mean = jnp.dot(jnp.sum(zs[0], axis=0), mean_ref[...], precision=lax.Precision.HIGHEST,
                       preferred_element_type=F32)
        icb[0] = 1.0 / mean[:, :128]
        icb[1] = 1.0 / mean[:, 128:]
        for i in range(8):
            wc[8 * i : 8 * i + 8] = zs[0, 8 * i : 8 * i + 8] * (wyz_ref[...] * float(WEIGHTS[i]))

        def step(it, carry):
            gather_receive(it)
            boxes(it)
            scatter_receive(it)
            fluxes(it)

            @pl.when(it == 1)
            def _():
                local = jnp.zeros((1, 128), F32)
                for k in range(4):
                    total = jnp.sum(acc[k], axis=(0, 1), keepdims=True)
                    local = jnp.where(lane[0:1] == k, total, local)
                reduce_start(0, local)

            divergence(it, (0, 1), ((0, 2), (6, 8)))
            gather_x(it + 1)
            divergence(it, (2, 3), ((2, 6),))
            gather_rest(it + 1)
            return carry

        lax.fori_loop(0, 2, step, 0)
        reduce_start(1, reduce_wait(0))
        gather_receive(2)
        def placed(k, values):
            for m in range(64):
                for ex in range(2):
                    fin[k, 8 * ex + m // 8, pl.ds(m % 8, 4, stride=8), :] = values[
                        m, 4 * ex : 4 * ex + 4
                    ]

        placed(0, zs[0])
        placed(1, zs[1])
        for it in range(3):
            wide = jnp.concatenate(
                [x[it, 0].reshape(512, 128), x[it, 1].reshape(512, 128)], axis=1
            )
            out = jnp.dot(wide, asm_ref[...], precision=lax.Precision.HIGH,
                          preferred_element_type=F32)
            placed(2 + it, out.reshape(64, 8, 128))
        sums = reduce_wait(1)
        rho, delta, gamma, eps = (sums[:, k : k + 1] for k in range(4))
        a0 = rho / delta
        rz = a0 * a0 * gamma - rho
        up = 1.0 + rz / rho
        curve = up * up * delta - 2.0 * a0 * up * gamma + a0 * a0 * eps
        a1 = rz / curve
        first = a0 + a1 * up
        second = a1 * a0
        stores = [
            pltpu.make_async_copy(fin.at[k], ref, load.at[k])
            for k, ref in ((0, sol_ref), (2, res_ref))
        ]
        fin[0] = fin[0] * first - fin[1] * second
        stores[0].start()
        fin[2] = fin[2] - fin[3] * first + fin[4] * second
        stores[1].start()
        for copy in stores:
            copy.wait()
        for it in range(3):
            wait_sent(gr.at[it], IN, gsend.at[it])
        for it in range(2):
            wait_sent(sr.at[it], OUT, ssend.at[it])
        for phase in range(2):
            reduce_end(phase)

    return kernel


def solution(mesh):
    sizes = tuple(mesh.shape[a] for a in AXES)
    z_run = 4 if sizes[2] % 4 == 0 else sizes[2]
    ring = sizes[0] * z_run
    forward, assemble = z_tables(16)
    der = np.kron(np.eye(16), DERIV)
    inverse = np.zeros((2, 10, 10, 128))
    tiled = np.tile(INVERSE, (1, 1, 16))
    inverse[0] = tiled[:, :, :128]
    inverse[1, :, :, :32] = tiled[:, :, 128:]
    mean = np.zeros((128, 256))
    mean[:, :160] = np.kron(np.eye(16), np.ones((8, 10))) / SIDE**3
    mean[0, 160:] = 1.0
    wyz = np.broadcast_to(
        WEIGHTS[:, None, None] * np.tile(WEIGHTS, 16)[None, None, :], (8, 8, 128)
    )
    tables = [
        jnp.asarray(t, F32)
        for t in (wyz, forward, forward.T, assemble, np.stack([der.T, der]), inverse, mean)
    ]
    hbm = pl.BlockSpec(memory_space=pltpu.HBM)
    dma = pltpu.SemaphoreType.DMA

    def block(*shape):
        return pltpu.VMEM(shape + (8, 128), F32)

    call = pl.pallas_call(
        make_kernel(sizes, z_run),
        out_shape=[jax.ShapeDtypeStruct((16, 32, 128), F32)] * 2,
        in_specs=[hbm] * 9,
        out_specs=[hbm] * 2,
        scratch_shapes=[
            pltpu.VMEM((8, 64, 128), F32), pltpu.VMEM((8, 64, 128), F32),
            *[pltpu.VMEM(t.shape, F32) for t in tables],
            block(3, 64), block(64), block(2),
            block(3, IN.total), block(3, IN.received), block(2, 10, 9), block(2, 10, 10),
            block(3, 2, 64), block(2, 10, 10), block(2, 10, 10), block(3, 64),
            block(2, OUT.total), block(2, OUT.received), block(12, 11),
            block(2, 64), block(4),
            block(sizes[1] * sizes[2] // z_run), block(ring),
            dma((3,)), dma((3, 2)), dma((2,)), dma((2, 2)), dma((2,)), dma((2,)), dma((11,)), pltpu.VMEM((5, 16, 32, 128), F32),
        ],
        compiler_params=pltpu.CompilerParams(
            collective_id=0, has_side_effects=True, vmem_limit_bytes=60 * 1024 * 1024
        ),
    )

    def hand_over(first, second, first_out, second_out, sems):
        copies = [
            pltpu.make_async_copy(source, target, sems.at[k])
            for k, (source, target) in enumerate(((first, first_out), (second, second_out)))
        ]
        for copy in copies:
            copy.start()
        for copy in copies:
            copy.wait()

    results = pl.pallas_call(
        hand_over,
        out_shape=[jax.ShapeDtypeStruct((16, 32, 128), F32)] * 2,
        in_specs=[pl.BlockSpec(memory_space=pltpu.VMEM)] * 2,
        out_specs=[hbm] * 2,
        scratch_shapes=[dma((2,))],
    )

    def shards(right_side, coefficient):
        return tuple(results(*call(right_side, coefficient, *tables)))

    spec = P(*AXES)
    return jax.shard_map(
        shards, mesh=mesh, in_specs=(spec, spec), out_specs=(spec, spec), check_vma=False
    )
```

```python
import itertools

import jax
import jax.numpy as jnp
import numpy as np
from jax import lax
from jax.experimental import pallas as pl
from jax.experimental.pallas import tpu as pltpu
from jax.sharding import PartitionSpec as P

ORDER = 7
SIDE = ORDER + 1
BOX = ORDER + 3
AXES = ("gx", "gy", "gz")
MESH = pl.DeviceIdType.MESH
F32 = jnp.float32
NEAR = sorted(
    (o for o in itertools.product((-1, 0, 1), repeat=3) if o != (0, 0, 0)),
    key=lambda o: [(1, 1, 1), (1, 0, 1), (1, 1, 0), (0, 1, 1), (0, 0, 1), (1, 0, 0),
                   (0, 1, 0)].index(tuple(map(abs, o))),
)


def legendre_rows(points, degree):
    table_rows = [np.ones(points.shape), points * 1.0]
    for k in range(2, degree + 1):
        table_rows.append(
            ((2 * k - 1) * points * table_rows[k - 1] - (k - 1) * table_rows[k - 2]) / k
        )
    return table_rows


def lobatto_tables(degree):
    per_side = degree + 1
    points = np.cos(np.pi * np.arange(per_side) / degree)
    for newton_step in range(60):
        table_rows = legendre_rows(points, degree)
        points = points - (points * table_rows[degree] - table_rows[degree - 1]) / (
            per_side * table_rows[degree]
        )
    top_row = legendre_rows(points, degree)[degree][::-1]
    points = points[::-1]
    weights = 2.0 / (degree * per_side * top_row**2)
    deriv_np = np.zeros((per_side, per_side))
    for a in range(per_side):
        for b in range(per_side):
            if a != b:
                deriv_np[a, b] = top_row[a] / (top_row[b] * (points[a] - points[b]))
    deriv_np[0, 0] = -degree * per_side / 4.0
    deriv_np[-1, -1] = degree * per_side / 4.0
    return (weights, deriv_np)


def sine_tables(degree):
    box_side = degree + 3
    grid_index = np.arange(1, box_side + 1)
    sine_np = np.sqrt(2.0 / (box_side + 1)) * np.sin(
        np.pi * np.outer(grid_index, grid_index) / (box_side + 1)
    )
    eigen_values = 2.0 - 2.0 * np.cos(np.pi * grid_index / (box_side + 1))
    summed = eigen_values[:, None, None] + eigen_values[None, :, None] + eigen_values[None, None, :]
    return (sine_np, 1.0 / summed)


WEIGHTS, DERIV = lobatto_tables(ORDER)
SINE, INVERSE = sine_tables(ORDER)


def z_tables(elements):
    span = elements * SIDE
    assemble = np.zeros((span + 2, 2 * span))
    for i in range(span):
        assemble[1 + i, i] = 1.0
        if i % SIDE == 0 and i > 0:
            assemble[1 + i, i - 1] = 1.0
        if i % SIDE == SIDE - 1 and i < span - 1:
            assemble[1 + i, i + 1] = 1.0
    assemble[0, span] = 1.0
    assemble[1, span + 1] = 1.0
    assemble[span, 2 * span - 2] = 1.0
    assemble[span + 1, 2 * span - 1] = 1.0
    gather = np.zeros((elements * BOX, span + 2))
    for e in range(elements):
        gather[e * BOX, 0 if e == 0 else 1 + SIDE * e - 2] = 1.0
        for k in range(SIDE):
            gather[e * BOX + 1 + k, 1 + SIDE * e + k] = 1.0
        gather[e * BOX + BOX - 1, span + 1 if e == elements - 1 else 1 + SIDE * (e + 1) + 1] = 1.0
    to_modes = np.kron(np.eye(elements), SINE) @ gather @ assemble
    forward = np.zeros((2 * span, 2 * span))
    forward[:, : elements * BOX] = to_modes.T
    return forward, assemble[1:-1].T


def rotate(x, shift, axis):
    return pltpu.roll(x, shift % x.shape[axis], axis)


class Halo:
    def __init__(self, n, hf, hs, lf, ls):
        self.n, self.hf, self.hs, self.lf, self.ls = n, hf, hs, lf, ls
        self.own_z = -(-n * n // 64)
        self.corner = 4 * n
        self.z_part = {1: 4 * n + 4, -1: 4 * n + 7 + self.own_z}
        self.total = 4 * n + 10 + 2 * self.own_z
        self.slot, at, height = {}, 0, [0, 0]
        for o in NEAR:
            _, count, tall = self.part(o)
            self.slot[o] = at
            at += count
            height[tall < 8] += count * tall
        self.received = at
        self.vectors = [h // 8 for h in height]

    def part(self, o):
        n = self.n
        if o[2]:
            base = self.z_part[o[2]]
            if o[0]:
                return (base + self.own_z + (1 if o[0] > 0 else 2), 1, 2)
            return (base + self.own_z, 1, 8) if o[1] else (base, self.own_z, 8)
        if o[0] == 0:
            return (0 if o[1] > 0 else n, n, 8)
        if o[1] == 0:
            return (2 * n if o[0] > 0 else 3 * n, n, 8)
        return (4 * n + [(1, 1), (1, -1), (-1, 1), (-1, -1)].index(o[:2]), 1, 4)


IN = Halo(SIDE, 7, 6, 0, 1)
OUT = Halo(BOX, 8, 9, 1, 0)


def make_kernel(sizes, z_run):
    nx, ny, nz = sizes
    runs = nz // z_run
    ring = nx * z_run

    def kernel(b_ref, c_ref, *rest):
        tables, rest = rest[:7], rest[7:]
        (sol_ref, res_ref, b_rows, c_rows, wyz_ref, fwd_ref, bwd_ref, asm_ref, der_ref, inv_ref,
         mean_ref, raw, wc, icb, gs, gr, ug, e, x, sp, sq, fl, ss, sr, us, zs, acc,
         red_xy, red_z, gsend, grecv, ssend, srecv, rsend, rrecv, load, fin) = rest
        gx, gy, gz = (lax.axis_index(a) for a in AXES)

        def near(o):
            return ((gx + o[0] + nx) % nx, (gy + o[1] + ny) % ny, (gz + o[2] + nz) % nz)

        def ring_xy(t):
            to = (gz // z_run + t // ny) % runs
            return (gx, (gy + t % ny) % ny, to * z_run + gz % z_run)

        def ring_z(t):
            to = (gx * z_run + gz % z_run + t) % ring
            return (to // z_run, gy, (gz // z_run) * z_run + to % z_run)

        partners = [near(o) for o in NEAR]
        partners += [ring_xy(t) for t in range(1, ny * runs)]
        partners += [ring_z(t) for t in range(1, ring)]
        barrier = pltpu.get_barrier_semaphore()
        for device in partners:
            pl.semaphore_signal(barrier, inc=1, device_id=device, device_id_type=MESH)

        loads = []
        for source, target in ((b_ref, b_rows), (c_ref, c_rows)):
            for ex in range(2):
                loads.append((source.at[pl.ds(8 * ex, 8)], target.at[:, pl.ds(32 * ex, 32)]))
        kept = (wyz_ref, fwd_ref, bwd_ref, asm_ref, der_ref, inv_ref, mean_ref)
        loads += list(zip(tables, kept))
        loads = [
            pltpu.make_async_copy(source, target, load.at[k])
            for k, (source, target) in enumerate(loads)
        ]
        for copy in loads:
            copy.start()

        sub = lax.broadcasted_iota(jnp.int32, (8, 128), 0)
        lane = lax.broadcasted_iota(jnp.int32, (8, 128), 1)
        pair = lane // 2
        ey = sub % 4
        lower = sub < 4

        def flag(condition):
            return jnp.where(condition, 1.0, 0.0).astype(F32)

        fx_lo, fx_hi = flag(gx > 0), flag(gx < nx - 1)
        fy_lo, fy_hi = flag(gy > 0), flag(gy < ny - 1)
        fz_lo, fz_hi = flag(gz > 0), flag(gz < nz - 1)
        y_mask = jnp.where(ey >= 2, fy_lo, fy_hi)
        z_mask = jnp.where(lane < 2, fz_lo, jnp.where(lane >= 126, fz_hi, 0.0))
        x_mask = jnp.where(lower, 1.0, fx_hi)

        def y_plane(row, halo, up):
            if up:
                return jnp.where(ey == 3, row[halo.hf], rotate(row[halo.hs], 7, 0))
            return jnp.where(ey == 0, row[halo.lf], rotate(row[halo.ls], 1, 0))

        def x_planes(u, halo):
            out = []
            for up in (True, False):
                rows = (halo.hf, halo.hs) if up else (halo.lf, halo.ls)
                pairs = [(u[rows[0]][j], u[rows[1]][j]) for j in range(halo.n)]
                pairs += [tuple(y_plane(u[r], halo, y) for r in rows) for y in (True, False)]
                out.append([
                    jnp.where(lower, rotate(back, 4, 0), front) if up
                    else jnp.where(lower, front, rotate(back, 4, 0))
                    for front, back in pairs
                ])
            return out

        def lane_pack(values, up):
            total = None
            for k, value in enumerate(values):
                moved = rotate(value, 2 * k + 2 if up else 2 * k, 1)
                total = moved if total is None else jnp.where(pair == k, moved, total)
            return total

        def fan(value, sign):
            turned = value
            for k in range(1, 4):
                turned = jnp.where(ey == k, rotate(value, sign * 32 * k, 1), turned)
            return turned

        def sender(halo, link):
            src, dst, send_sem, recv_sem = link
            n = halo.n
            ends = ((True, halo.z_part[1]), (False, halo.z_part[-1]))

            def send(*kinds):
                for o in NEAR:
                    if tuple(map(abs, o)) not in kinds:
                        continue
                    at, count, tall = halo.part(o)
                    to = halo.slot[(-o[0], -o[1], -o[2])]
                    pltpu.make_async_remote_copy(
                        src_ref=src.at[pl.ds(at, count), pl.ds(0, tall)],
                        dst_ref=dst.at[pl.ds(to, count), pl.ds(0, tall)],
                        send_sem=send_sem,
                        recv_sem=recv_sem.at[1 if tall < 8 else 0],
                        device_id=near(o),
                        device_id_type=MESH,
                    ).start()

            def send_x(planes, lanes):
                lanes, planes = x_planes(lanes, halo), x_planes(planes, halo)
                for up, base in ends:
                    for k in range(2):
                        moved = fan(lane_pack(lanes[k], up), 1)
                        moved = jnp.where(lane // 32 == ey, moved, 0.0)
                        at = base + halo.own_z + 1 + k
                        src[at, 0:1] = jnp.sum(moved[0:4], axis=0, keepdims=True)
                        src[at, 1:2] = jnp.sum(moved[4:8], axis=0, keepdims=True)
                send((1, 1, 1), (1, 0, 1))
                for k in range(4):
                    corner = planes[k // 2][n + k % 2]
                    if k % 2 == 0:
                        corner = jnp.where(sub < 2, rotate(corner, 2, 0), corner)
                    else:
                        corner = jnp.where(sub < 2, corner, rotate(corner, 6, 0))
                    src[4 * n + k, 0:4] = corner[0:4]
                send((1, 1, 0))
                for k in range(2):
                    for j in range(n):
                        src[(2 + k) * n + j] = planes[k][j]
                send((1, 0, 0))

            def send_rest(planes, lanes, own):
                for up, base in ends:
                    edge = [y_plane(lanes[i], halo, y) for y in (True, False) for i in range(n)]
                    src[base + halo.own_z] = lane_pack(edge, up)
                send((0, 1, 1))
                for up, base in ends:
                    for k in range(halo.own_z):
                        src[base + k] = lane_pack(own[64 * k : 64 * k + 64], up)
                send((0, 0, 1))
                for i in range(n):
                    src[i] = y_plane(planes[i], halo, True)
                    src[n + i] = y_plane(planes[i], halo, False)
                send((0, 1, 0))

            return send_x, send_rest

        def wait_all(ref, sem):
            pltpu.make_async_copy(ref, ref, sem).wait()

        def wait_halo(ref, halo, sem, far):
            wait_all(ref.at[pl.ds(0, halo.vectors[far])], sem.at[far])

        def wait_sent(ref, halo, sem):
            wait_all(ref.at[pl.ds(0, sum(halo.vectors))], sem)

        def y_lanes(dst, halo, dz):
            low, high = dst[halo.slot[(0, -1, dz)]], dst[halo.slot[(0, 1, dz)]]
            return jnp.where(ey >= 2, low, rotate(high, -2 * halo.n, 1))

        def x_lanes(dst, halo, dx, dz):
            def got(dy):
                at = halo.slot[(dx, dy, dz)]
                value = jnp.where(lower, dst[at, 0:1], dst[at, 1:2])
                return fan(value, -1)

            corner = jnp.where(ey >= 2, got(-1), rotate(got(1), -2, 1))
            return jnp.where(pair >= halo.n, corner, got(0))

        def xy_corner(dst, halo, dx):
            low, high = dst[halo.slot[(dx, -1, 0)], 0:4], dst[halo.slot[(dx, 1, 0)], 0:4]
            low, high = jnp.concatenate([low, low], 0), jnp.concatenate([high, high], 0)
            low = jnp.where(lower, low, rotate(low, 2, 0))
            high = jnp.where(lower, high, rotate(high, 6, 0))
            return jnp.where(ey >= 2, low, high)

        def unlane(low, high, k):
            return z_mask * jnp.where(
                lane < 2, rotate(low, -2 * k, 1), rotate(high, 126 - 2 * k, 1)
            )

        def receive_near(dst, halo, sem, put):
            n = halo.n

            def at(o, k=0):
                return dst[halo.slot[o] + k]

            wait_halo(dst, halo, sem, 0)
            own_lo = [dst[halo.slot[(0, 0, -1)] + k] for k in range(halo.own_z)]
            own_hi = [dst[halo.slot[(0, 0, 1)] + k] for k in range(halo.own_z)]
            for i in range(n):
                for j in range(n):
                    k = i * n + j
                    put(1, i, j, unlane(own_lo[k // 64], own_hi[k // 64], k % 64))
            low, high = y_lanes(dst, halo, -1), y_lanes(dst, halo, 1)
            for k in range(n):
                put(0, k, n, y_mask * jnp.where(ey >= 2, at((0, -1, 0), k), at((0, 1, 0), k)))
                put(1, k, n, y_mask * unlane(low, high, k))
                put(0, n, k, fx_lo * at((-1, 0, 0), k))
                put(0, n + 1, k, fx_hi * at((1, 0, 0), k))
        def receive_far(dst, halo, sem, put):
            n = halo.n
            wait_halo(dst, halo, sem, 1)
            below = x_lanes(dst, halo, -1, -1), x_lanes(dst, halo, -1, 1)
            above = x_lanes(dst, halo, 1, -1), x_lanes(dst, halo, 1, 1)
            for k in range(n):
                put(1, n, k, fx_lo * unlane(*below, k))
                put(1, n + 1, k, fx_hi * unlane(*above, k))
            put(0, n, n, fx_lo * y_mask * xy_corner(dst, halo, -1))
            put(1, n, n, fx_lo * y_mask * unlane(*below, n))
            put(0, n + 1, n, fx_hi * y_mask * xy_corner(dst, halo, 1))
            put(1, n + 1, n, fx_hi * y_mask * unlane(*above, n))

        def from_x(u, plo, phi, hf, hs, lf, ls):
            face_lo = rotate(jnp.where(lower, u[hf], plo), 4, 1)
            next_lo = jnp.where(lower, plo, rotate(u[hs], 4, 1))
            face_hi = rotate(jnp.where(lower, phi, u[lf]), 4, 1)
            next_hi = jnp.where(lower, rotate(u[ls], 4, 1), phi)
            return face_lo, next_lo, face_hi, next_hi

        def from_y(u, h, hf, hs, lf, ls):
            turned = rotate(h, 4, 1)
            face_lo = rotate(jnp.where(ey == 3, turned, u(hf)), 1, 1)
            next_lo = jnp.where(ey == 0, rotate(h, 6, 1), rotate(u(hs), 1, 1))
            face_hi = rotate(jnp.where(ey == 0, turned, u(lf)), 7, 1)
            next_hi = jnp.where(ey == 3, rotate(h, 2, 1), rotate(u(ls), 7, 1))
            return face_lo, next_lo, face_hi, next_hi

        def gather_sender(it):
            return sender(IN, (gs.at[it], gr.at[it], gsend.at[it], grecv.at[it]))

        def gather_x(it):
            rows = {i: raw[it, 8 * i : 8 * i + 8] for i in (0, 1, 6, 7)}
            gather_sender(it)[0](rows, rows)

        def gather_rest(it):
            rows = [raw[it, 8 * i : 8 * i + 8] for i in range(8)]
            gather_sender(it)[1](rows, rows, [raw[it, k] for k in range(64)])

        def spread_rows(tile, rows):
            for i, w in rows.items():
                face_lo, next_lo, face_hi, next_hi = from_y(
                    lambda j: w[j : j + 1], w[8:9], 7, 6, 0, 1
                )
                e[tile, i, 0:1] = next_lo
                e[tile, i, 1:2] = w[0:1] + face_lo
                e[tile, i, 2:8] = w[1:7]
                e[tile, i, 8:9] = w[7:8] + face_hi
                e[tile, i, 9:10] = next_hi

        def put_gathered(tile, i, j, value):
            ug[tile, i, j] = value

        def gather_near(it):
            receive_near(gr.at[it], IN, grecv.at[it], put_gathered)
            ug[0, 0:8, 0:8] = raw[it].reshape(8, 8, 8, 128)
            for tile in range(2):
                spread_rows(tile, {i + 1: ug[tile, i] for i in range(1, 7)})

        def gather_far(it):
            receive_far(gr.at[it], IN, grecv.at[it], put_gathered)
            for tile in range(2):
                u = [ug[tile, i] for i in range(10)]
                face_lo, next_lo, face_hi, next_hi = from_x(u, u[8], u[9], 7, 6, 0, 1)
                spread_rows(tile, {0: next_lo, 1: u[0] + face_lo,
                                   8: (u[7] + face_hi) * x_mask, 9: next_hi})

        def gather_keep(it):
            for tile in range(2):
                x[it, tile] = e[tile, 1:9, 1:9].reshape(64, 8, 128)

        def to_modes(v, picks=range(5)):
            plus = {a: v[a] + v[9 - a] for a in picks}
            minus = {a: v[a] - v[9 - a] for a in picks}
            out = []
            for k in range(10):
                total = None
                for a in picks:
                    term = (plus if k % 2 == 0 else minus)[a] * float(SINE[a, k])
                    total = term if total is None else total + term
                out.append(total)
            return out

        def from_modes(f, picks=range(5)):
            out = {}
            for a in picks:
                even = f[0] * float(SINE[a, 0])
                odd = f[1] * float(SINE[a, 1])
                for k in range(1, 5):
                    even = even + f[2 * k] * float(SINE[a, 2 * k])
                    odd = odd + f[2 * k + 1] * float(SINE[a, 2 * k + 1])
                out[a], out[9 - a] = even + odd, even - odd
            return out

        def joined_rows(ref, spans):
            return jnp.concatenate(
                [
                    jnp.concatenate([ref[tile, i0:i1] for i0, i1 in spans]).reshape(-1, 128)
                    for tile in range(2)
                ],
                axis=1,
            )

        def store_rows(ref, spans, values):
            at = 0
            for i0, i1 in spans:
                rows = values[80 * at : 80 * (at + i1 - i0)]
                for tile in range(2):
                    ref[tile, i0:i1] = rows[:, 128 * tile : 128 * tile + 128].reshape(
                        i1 - i0, 10, 8, 128
                    )
                at += i1 - i0

        def row_modes(spans):
            modes = jnp.dot(joined_rows(e, spans), fwd_ref[...], precision=lax.Precision.HIGH,
                            preferred_element_type=F32)
            store_rows(sq, spans, modes)
            for i0, i1 in spans:
                def over_y(i, carry):
                    for tile in range(2):
                        out = to_modes([sq[tile, i, j] for j in range(10)])
                        for j in range(10):
                            sq[tile, i, j] = out[j]
                    return carry

                lax.fori_loop(i0, i1, over_y, 0, unroll=i1 - i0)

        def near_modes():
            row_modes(((2, 8),))

            def over_x(j, carry):
                for tile in range(2):
                    out = to_modes({i: sq[tile, i, j] for i in range(2, 8)}, (2, 3, 4))
                    for i in range(10):
                        sp[tile, i, j] = out[i]
                return carry

            lax.fori_loop(0, 10, over_x, 0, unroll=5)

        def boxes(it):
            row_modes(((0, 2), (8, 10)))

            def middle(j, total):
                for tile in range(2):
                    f = to_modes({i: sq[tile, i, j] for i in (0, 1, 8, 9)}, (0, 1))
                    f = [f[i] + sp[tile, i, j] for i in range(10)]
                    scale = icb[tile]
                    g = [f[i] * (inv_ref[tile, j, i : i + 1] * scale) for i in range(10)]
                    for i in range(10):
                        total = total + f[i] * g[i]
                        sp[tile, i, j] = g[i]
                    for i, value in from_modes(g, (0, 1)).items():
                        sq[tile, i, j] = value
                return total

            acc[2 * it] = lax.fori_loop(0, 10, middle, jnp.zeros((8, 128), F32), unroll=5)
            send_x, send_rest = sender(OUT, (ss.at[it], sr.at[it], ssend.at[it], srecv.at[it]))

            def answers(spans):
                for i0, i1 in spans:
                    def back_y(i, carry):
                        for tile in range(2):
                            out = from_modes([sq[tile, i, j] for j in range(10)])
                            for j, value in out.items():
                                sq[tile, i, j] = value
                        return carry

                    lax.fori_loop(i0, i1, back_y, 0, unroll=i1 - i0)
                back = jnp.dot(joined_rows(sq, spans), bwd_ref[...],
                               precision=lax.Precision.HIGH, preferred_element_type=F32)
                store_rows(sq, spans, back)

            answers(((0, 2), (8, 10)))
            send_x({i: sq[0, i] for i in (0, 1, 8, 9)}, {i: sq[1, i] for i in (0, 1, 8, 9)})

            def back_x(j, carry):
                for tile in range(2):
                    out = from_modes([sp[tile, i, j] for i in range(10)], (2, 3, 4))
                    for i, value in out.items():
                        sq[tile, i, j] = value
                return carry

            lax.fori_loop(0, 10, back_x, 0, unroll=5)
            answers(((2, 8),))
            own = [sq[1, k // 10, k % 10] for k in range(100)]
            send_rest([sq[0, i] for i in range(10)], [sq[1, i] for i in range(10)], own)

        def put_scattered(tile, i, j, value):
            if i < 10 and j < 10:
                us[i, j] = sq[0, i, j] + value
            elif tile == 0:
                us[i, j] = value
            else:
                us[i, j] = us[i, j] + value

        def fold_rows(it, rows):
            for i, w in rows.items():
                last = x_mask if i == 7 else 1.0
                face_lo, next_lo, face_hi, next_hi = from_y(
                    lambda j: w[j : j + 1], w[10:11], 8, 9, 1, 0
                )
                zs[it, 8 * i : 8 * i + 1] = (w[1:2] + face_lo) * last
                zs[it, 8 * i + 1 : 8 * i + 2] = (w[2:3] + next_lo) * last
                zs[it, 8 * i + 2 : 8 * i + 6] = w[3:7] * last
                zs[it, 8 * i + 6 : 8 * i + 7] = (w[7:8] + next_hi) * last
                zs[it, 8 * i + 7 : 8 * i + 8] = (w[8:9] + face_hi) * last

        def scatter_near(it):
            receive_near(sr.at[it], OUT, srecv.at[it], put_scattered)
            fold_rows(it, {i: us[i + 1] for i in range(2, 6)})

        def scatter_far(it):
            receive_far(sr.at[it], OUT, srecv.at[it], put_scattered)
            u = [us[i] for i in range(12)]
            face_lo, next_lo, face_hi, next_hi = from_x(u, u[10], u[11], 8, 9, 1, 0)
            fold_rows(it, {0: u[1] + face_lo, 1: u[2] + next_lo, 6: u[7] + next_hi,
                           7: (u[8] + face_hi) * x_mask})

        def derive(v, matrix, picks=range(4)):
            plus = [v[k] + v[7 - k] for k in range(4)]
            minus = [v[k] - v[7 - k] for k in range(4)]
            out = {}
            for a in picks:
                even = odd = None
                for k in range(4):
                    p = plus[k] * float(0.5 * (matrix[a, k] + matrix[a, 7 - k]))
                    m = minus[k] * float(0.5 * (matrix[a, k] - matrix[a, 7 - k]))
                    even = p if even is None else even + p
                    odd = m if odd is None else odd + m
                out[a], out[7 - a] = even + odd, odd - even
            return out

        def fluxes_in_planes(it, spans):
            def joined(ref):
                return jnp.concatenate([ref[8 * i0 : 8 * i1] for i0, i1 in spans])

            grad = jnp.dot(joined(zs.at[it]).reshape(-1, 128), der_ref[0],
                           precision=lax.Precision.HIGH,
                           preferred_element_type=F32).reshape(-1, 8, 128)
            flux = grad * joined(wc)
            total = jnp.sum(flux * grad, axis=0)
            at = 0
            for i0, i1 in spans:
                fl[2, 8 * i0 : 8 * i1] = flux[at : at + 8 * (i1 - i0)]
                at += 8 * (i1 - i0)
                for i in range(i0, i1):
                    along = derive([zs[it, 8 * i + j] for j in range(8)], DERIV)
                    for j in range(8):
                        part = along[j] * wc[8 * i + j]
                        total = total + part * along[j]
                        fl[1, 8 * i + j] = part
            return total

        def fluxes_across(it, total):
            def over_x(j, total):
                grad = derive([zs[it, 8 * i + j] for i in range(8)], DERIV)
                for i in range(8):
                    flux = grad[i] * wc[8 * i + j]
                    total = total + flux * grad[i]
                    fl[0, 8 * i + j] = flux
                return total

            return lax.fori_loop(0, 8, over_x, total, unroll=8)

        def divergence(it, picks, spans):
            along_z = jnp.dot(
                jnp.concatenate([fl[2, 8 * i0 : 8 * i1] for i0, i1 in spans]).reshape(-1, 128),
                der_ref[1], precision=lax.Precision.HIGH, preferred_element_type=F32,
            ).reshape(-1, 8, 128)
            at = 0
            for i0, i1 in spans:
                raw[it + 1, 8 * i0 : 8 * i1] = along_z[at : at + 8 * (i1 - i0)]
                at += 8 * (i1 - i0)

            def over_x(j, carry):
                out = derive([fl[0, 8 * i + j] for i in range(8)], DERIV.T, picks)
                for i, value in out.items():
                    raw[it + 1, 8 * i + j] = raw[it + 1, 8 * i + j] + value
                return carry

            lax.fori_loop(0, 8, over_x, 0, unroll=8)
            for i0, i1 in spans:
                for i in range(i0, i1):
                    out = derive([fl[1, 8 * i + j] for j in range(8)], DERIV.T)
                    for j in range(8):
                        raw[it + 1, 8 * i + j] = raw[it + 1, 8 * i + j] + out[j]

        def far_first(count, length):
            return sorted(range(1, count), key=lambda t: -length(t))

        rings = (
            (red_xy, ny * runs, gz // z_run * ny + gy, ring_xy,
             far_first(ny * runs, lambda t: min(t // ny, runs - t // ny)
                       + min(t % ny, ny - t % ny) / 2)),
            (red_z, ring, gx * z_run + gz % z_run, ring_z,
             far_first(ring, lambda t: min(t, ring - t))),
        )

        def reduce_start(phase, value):
            ref, count, me, to, order = rings[phase]
            ref[me, 0:1] = value
            for t in order:
                pltpu.make_async_remote_copy(
                    src_ref=ref.at[me, pl.ds(0, 1)],
                    dst_ref=ref.at[me, pl.ds(0, 1)],
                    send_sem=rsend.at[phase],
                    recv_sem=rrecv.at[phase],
                    device_id=to(t),
                    device_id_type=MESH,
                ).start()

        def reduce_wait(phase):
            ref, count = rings[phase][:2]
            if count > 1:
                wait_all(ref.at[pl.ds(0, count - 1), pl.ds(0, 1)], rrecv.at[phase])
            return jnp.sum(ref[0:count, 0:1], axis=0)

        def reduce_end(phase):
            ref, count = rings[phase][:2]
            if count > 1:
                wait_all(ref.at[pl.ds(0, count - 1), pl.ds(0, 1)], rsend.at[phase])

        def relaid(ref, store):
            for i in range(8):
                for j in range(8):
                    store(8 * i + j, ref[i, pl.ds(j, 8, stride=8), :])

        def put_b(k, value):
            raw[0, k] = value

        def put_c(k, value):
            zs[0, k] = value

        loads[0].wait()
        loads[1].wait()
        relaid(b_rows, put_b)
        pl.semaphore_wait(barrier, len(partners))
        gather_x(0)
        gather_rest(0)
        for copy in loads[2:]:
            copy.wait()
        relaid(c_rows, put_c)
        mean = jnp.dot(jnp.sum(zs[0], axis=0), mean_ref[...], precision=lax.Precision.HIGHEST,
                       preferred_element_type=F32)
        icb[0] = 1.0 / mean[:, :128]
        icb[1] = 1.0 / mean[:, 128:]
        for i in range(8):
            wc[8 * i : 8 * i + 8] = zs[0, 8 * i : 8 * i + 8] * (wyz_ref[...] * float(WEIGHTS[i]))

        def step(it, carry):
            gather_near(it)
            near_modes()
            gather_far(it)
            boxes(it)
            gather_keep(it)
            scatter_near(it)
            total = fluxes_in_planes(it, ((2, 6),))
            scatter_far(it)
            total = total + fluxes_in_planes(it, ((0, 2), (6, 8)))
            acc[2 * it + 1] = fluxes_across(it, total)

            @pl.when(it == 1)
            def _():
                local = jnp.zeros((1, 128), F32)
                for k in range(4):
                    total = jnp.sum(acc[k], axis=(0, 1), keepdims=True)
                    local = jnp.where(lane[0:1] == k, total, local)
                reduce_start(0, local)

            divergence(it, (0, 1), ((0, 2), (6, 8)))
            gather_x(it + 1)
            divergence(it, (2, 3), ((2, 6),))
            gather_rest(it + 1)
            return carry

        lax.fori_loop(0, 2, step, 0)
        reduce_start(1, reduce_wait(0))
        gather_near(2)
        gather_far(2)
        gather_keep(2)
        def placed(k, values):
            for m in range(64):
                for ex in range(2):
                    fin[k, 8 * ex + m // 8, pl.ds(m % 8, 4, stride=8), :] = values[
                        m, 4 * ex : 4 * ex + 4
                    ]

        placed(0, zs[0])
        placed(1, zs[1])
        for it in range(3):
            wide = jnp.concatenate(
                [x[it, 0].reshape(512, 128), x[it, 1].reshape(512, 128)], axis=1
            )
            out = jnp.dot(wide, asm_ref[...], precision=lax.Precision.HIGH,
                          preferred_element_type=F32)
            placed(2 + it, out.reshape(64, 8, 128))
        sums = reduce_wait(1)
        rho, delta, gamma, eps = (sums[:, k : k + 1] for k in range(4))
        a0 = rho / delta
        rz = a0 * a0 * gamma - rho
        up = 1.0 + rz / rho
        curve = up * up * delta - 2.0 * a0 * up * gamma + a0 * a0 * eps
        a1 = rz / curve
        first = a0 + a1 * up
        second = a1 * a0
        stores = [
            pltpu.make_async_copy(fin.at[k], ref, load.at[k])
            for k, ref in ((0, sol_ref), (2, res_ref))
        ]
        fin[0] = fin[0] * first - fin[1] * second
        stores[0].start()
        fin[2] = fin[2] - fin[3] * first + fin[4] * second
        stores[1].start()
        for copy in stores:
            copy.wait()
        for it in range(3):
            wait_sent(gr.at[it], IN, gsend.at[it])
        for it in range(2):
            wait_sent(sr.at[it], OUT, ssend.at[it])
        for phase in range(2):
            reduce_end(phase)

    return kernel


def solution(mesh):
    sizes = tuple(mesh.shape[a] for a in AXES)
    z_run = 4 if sizes[2] % 4 == 0 else sizes[2]
    ring = sizes[0] * z_run
    forward, assemble = z_tables(16)
    der = np.kron(np.eye(16), DERIV)
    inverse = np.zeros((2, 10, 10, 128))
    tiled = np.tile(INVERSE, (1, 1, 16))
    inverse[0] = tiled[:, :, :128]
    inverse[1, :, :, :32] = tiled[:, :, 128:]
    mean = np.zeros((128, 256))
    mean[:, :160] = np.kron(np.eye(16), np.ones((8, 10))) / SIDE**3
    mean[0, 160:] = 1.0
    wyz = np.broadcast_to(
        WEIGHTS[:, None, None] * np.tile(WEIGHTS, 16)[None, None, :], (8, 8, 128)
    )
    tables = [
        jnp.asarray(t, F32)
        for t in (wyz, forward, forward.T, assemble, np.stack([der.T, der]), inverse, mean)
    ]
    hbm = pl.BlockSpec(memory_space=pltpu.HBM)
    dma = pltpu.SemaphoreType.DMA

    def block(*shape):
        return pltpu.VMEM(shape + (8, 128), F32)

    call = pl.pallas_call(
        make_kernel(sizes, z_run),
        out_shape=[jax.ShapeDtypeStruct((16, 32, 128), F32)] * 2,
        in_specs=[hbm] * 9,
        out_specs=[hbm] * 2,
        scratch_shapes=[
            pltpu.VMEM((8, 64, 128), F32), pltpu.VMEM((8, 64, 128), F32),
            *[pltpu.VMEM(t.shape, F32) for t in tables],
            block(3, 64), block(64), block(2),
            block(3, IN.total), block(3, IN.received), block(2, 10, 9), block(2, 10, 10),
            block(3, 2, 64), block(2, 10, 10), block(2, 10, 10), block(3, 64),
            block(2, OUT.total), block(2, OUT.received), block(12, 11),
            block(2, 64), block(4),
            block(sizes[1] * sizes[2] // z_run), block(ring),
            dma((3,)), dma((3, 2)), dma((2,)), dma((2, 2)), dma((2,)), dma((2,)), dma((11,)), pltpu.VMEM((5, 16, 32, 128), F32),
        ],
        compiler_params=pltpu.CompilerParams(
            collective_id=0, has_side_effects=True, vmem_limit_bytes=60 * 1024 * 1024
        ),
    )

    def hand_over(first, second, first_out, second_out, held, sems):
        pieces = [
            (source, target, pl.ds(8 * half, 8))
            for source, target in ((first, first_out), (second, second_out))
            for half in range(2)
        ]
        reads = [
            pltpu.make_async_copy(source.at[part], held.at[k], sems.at[0, k])
            for k, (source, _, part) in enumerate(pieces)
        ]
        writes = [
            pltpu.make_async_copy(held.at[k], target.at[part], sems.at[1, k])
            for k, (_, target, part) in enumerate(pieces)
        ]
        for copy in reads:
            copy.start()
        for read, write in zip(reads, writes):
            read.wait()
            write.start()
        for copy in writes:
            copy.wait()

    results = pl.pallas_call(
        hand_over,
        out_shape=[jax.ShapeDtypeStruct((16, 32, 128), F32)] * 2,
        in_specs=[hbm] * 2,
        out_specs=[hbm] * 2,
        scratch_shapes=[pltpu.VMEM((4, 8, 32, 128), F32), dma((2, 4))],
        compiler_params=pltpu.CompilerParams(vmem_limit_bytes=60 * 1024 * 1024),
    )

    def shards(right_side, coefficient):
        return tuple(results(*call(right_side, coefficient, *tables)))

    spec = P(*AXES)
    return jax.shard_map(
        shards, mesh=mesh, in_specs=(spec, spec), out_specs=(spec, spec), check_vma=False
    )
```

```python
import itertools

import jax
import jax.numpy as jnp
import numpy as np
from jax import lax
from jax.experimental import pallas as pl
from jax.experimental.pallas import tpu as pltpu
from jax.sharding import PartitionSpec as P

ORDER = 7
SIDE = ORDER + 1
BOX = ORDER + 3
AXES = ("gx", "gy", "gz")
MESH = pl.DeviceIdType.MESH
F32 = jnp.float32
NEAR = sorted(
    (o for o in itertools.product((-1, 0, 1), repeat=3) if o != (0, 0, 0)),
    key=lambda o: [(1, 1, 1), (1, 0, 1), (1, 1, 0), (0, 1, 1), (0, 0, 1), (1, 0, 0),
                   (0, 1, 0)].index(tuple(map(abs, o))),
)


def legendre_rows(points, degree):
    table_rows = [np.ones(points.shape), points * 1.0]
    for k in range(2, degree + 1):
        table_rows.append(
            ((2 * k - 1) * points * table_rows[k - 1] - (k - 1) * table_rows[k - 2]) / k
        )
    return table_rows


def lobatto_tables(degree):
    per_side = degree + 1
    points = np.cos(np.pi * np.arange(per_side) / degree)
    for newton_step in range(60):
        table_rows = legendre_rows(points, degree)
        points = points - (points * table_rows[degree] - table_rows[degree - 1]) / (
            per_side * table_rows[degree]
        )
    top_row = legendre_rows(points, degree)[degree][::-1]
    points = points[::-1]
    weights = 2.0 / (degree * per_side * top_row**2)
    deriv_np = np.zeros((per_side, per_side))
    for a in range(per_side):
        for b in range(per_side):
            if a != b:
                deriv_np[a, b] = top_row[a] / (top_row[b] * (points[a] - points[b]))
    deriv_np[0, 0] = -degree * per_side / 4.0
    deriv_np[-1, -1] = degree * per_side / 4.0
    return (weights, deriv_np)


def sine_tables(degree):
    box_side = degree + 3
    grid_index = np.arange(1, box_side + 1)
    sine_np = np.sqrt(2.0 / (box_side + 1)) * np.sin(
        np.pi * np.outer(grid_index, grid_index) / (box_side + 1)
    )
    eigen_values = 2.0 - 2.0 * np.cos(np.pi * grid_index / (box_side + 1))
    summed = eigen_values[:, None, None] + eigen_values[None, :, None] + eigen_values[None, None, :]
    return (sine_np, 1.0 / summed)


WEIGHTS, DERIV = lobatto_tables(ORDER)
SINE, INVERSE = sine_tables(ORDER)


def z_tables(elements):
    span = elements * SIDE
    assemble = np.zeros((span + 2, 2 * span))
    for i in range(span):
        assemble[1 + i, i] = 1.0
        if i % SIDE == 0 and i > 0:
            assemble[1 + i, i - 1] = 1.0
        if i % SIDE == SIDE - 1 and i < span - 1:
            assemble[1 + i, i + 1] = 1.0
    assemble[0, span] = 1.0
    assemble[1, span + 1] = 1.0
    assemble[span, 2 * span - 2] = 1.0
    assemble[span + 1, 2 * span - 1] = 1.0
    gather = np.zeros((elements * BOX, span + 2))
    for e in range(elements):
        gather[e * BOX, 0 if e == 0 else 1 + SIDE * e - 2] = 1.0
        for k in range(SIDE):
            gather[e * BOX + 1 + k, 1 + SIDE * e + k] = 1.0
        gather[e * BOX + BOX - 1, span + 1 if e == elements - 1 else 1 + SIDE * (e + 1) + 1] = 1.0
    to_modes = np.kron(np.eye(elements), SINE) @ gather @ assemble
    forward = np.zeros((2 * span, 2 * span))
    forward[:, : elements * BOX] = to_modes.T
    return forward, assemble[1:-1].T


def rotate(x, shift, axis):
    return pltpu.roll(x, shift % x.shape[axis], axis)


class Halo:
    def __init__(self, n, hf, hs, lf, ls):
        self.n, self.hf, self.hs, self.lf, self.ls = n, hf, hs, lf, ls
        self.own_z = -(-n * n // 64)
        self.corner = 4 * n
        self.z_part = {1: 4 * n + 4, -1: 4 * n + 7 + self.own_z}
        self.total = 4 * n + 10 + 2 * self.own_z
        self.slot, at, height = {}, 0, [0, 0]
        for o in NEAR:
            _, count, tall = self.part(o)
            self.slot[o] = at
            at += count
            height[o[0] != 0] += count * tall
        self.received = at
        self.vectors = [h // 8 for h in height]

    def part(self, o):
        n = self.n
        if o[2]:
            base = self.z_part[o[2]]
            if o[0]:
                return (base + self.own_z + (1 if o[0] > 0 else 2), 1, 2)
            return (base + self.own_z, 1, 8) if o[1] else (base, self.own_z, 8)
        if o[0] == 0:
            return (0 if o[1] > 0 else n, n, 8)
        if o[1] == 0:
            return (2 * n if o[0] > 0 else 3 * n, n, 8)
        return (4 * n + [(1, 1), (1, -1), (-1, 1), (-1, -1)].index(o[:2]), 1, 4)


IN = Halo(SIDE, 7, 6, 0, 1)
OUT = Halo(BOX, 8, 9, 1, 0)


def make_kernel(sizes, z_run):
    nx, ny, nz = sizes
    runs = nz // z_run
    ring = nx * z_run

    def kernel(b_ref, c_ref, *rest):
        tables, rest = rest[:7], rest[7:]
        (sol_ref, res_ref, b_rows, c_rows, wyz_ref, fwd_ref, bwd_ref, asm_ref, der_ref, inv_ref,
         mean_ref, raw, wc, icb, gs, gr, ug, e, x, sp, sq, fl, ss, sr, us, zs, acc,
         red_xy, red_z, gsend, grecv, ssend, srecv, rsend, rrecv, load, fin) = rest
        gx, gy, gz = (lax.axis_index(a) for a in AXES)

        steps = [
            {0: at, 1: (at + 1) % size, -1: (at + size - 1) % size}
            for at, size in ((gx, nx), (gy, ny), (gz, nz))
        ]

        def near(o):
            return tuple(step[k] for step, k in zip(steps, o))

        def ring_xy(t):
            to = (gz // z_run + t // ny) % runs
            return (gx, (gy + t % ny) % ny, to * z_run + gz % z_run)

        def ring_z(t):
            to = (gx * z_run + gz % z_run + t) % ring
            return (to // z_run, gy, (gz // z_run) * z_run + to % z_run)

        partners = [near(o) for o in NEAR]
        partners += [ring_xy(t) for t in range(1, ny * runs)]
        partners += [ring_z(t) for t in range(1, ring)]
        barrier = pltpu.get_barrier_semaphore()
        for device in partners:
            pl.semaphore_signal(barrier, inc=1, device_id=device, device_id_type=MESH)

        loads = []
        for source, target in ((b_ref, b_rows), (c_ref, c_rows)):
            for ex in range(2):
                loads.append((source.at[pl.ds(8 * ex, 8)], target.at[:, pl.ds(32 * ex, 32)]))
        kept = (wyz_ref, fwd_ref, bwd_ref, asm_ref, der_ref, inv_ref, mean_ref)
        loads += list(zip(tables, kept))
        loads = [
            pltpu.make_async_copy(source, target, load.at[k])
            for k, (source, target) in enumerate(loads)
        ]
        for copy in loads:
            copy.start()

        sub = lax.broadcasted_iota(jnp.int32, (8, 128), 0)
        lane = lax.broadcasted_iota(jnp.int32, (8, 128), 1)
        pair = lane // 2
        ey = sub % 4
        lower = sub < 4

        def flag(condition):
            return jnp.where(condition, 1.0, 0.0).astype(F32)

        fx_lo, fx_hi = flag(gx > 0), flag(gx < nx - 1)
        fy_lo, fy_hi = flag(gy > 0), flag(gy < ny - 1)
        fz_lo, fz_hi = flag(gz > 0), flag(gz < nz - 1)
        y_mask = jnp.where(ey >= 2, fy_lo, fy_hi)
        z_mask = jnp.where(lane < 2, fz_lo, jnp.where(lane >= 126, fz_hi, 0.0))
        x_mask = jnp.where(lower, 1.0, fx_hi)

        def y_plane(row, halo, up):
            if up:
                return jnp.where(ey == 3, row[halo.hf], rotate(row[halo.hs], 7, 0))
            return jnp.where(ey == 0, row[halo.lf], rotate(row[halo.ls], 1, 0))

        def x_planes(u, halo):
            out = []
            for up in (True, False):
                rows = (halo.hf, halo.hs) if up else (halo.lf, halo.ls)
                pairs = [(u[rows[0]][j], u[rows[1]][j]) for j in range(halo.n)]
                pairs += [tuple(y_plane(u[r], halo, y) for r in rows) for y in (True, False)]
                out.append([
                    jnp.where(lower, rotate(back, 4, 0), front) if up
                    else jnp.where(lower, front, rotate(back, 4, 0))
                    for front, back in pairs
                ])
            return out

        def lane_pack(values, up):
            total = None
            for k, value in enumerate(values):
                moved = rotate(value, 2 * k + 2 if up else 2 * k, 1)
                total = moved if total is None else jnp.where(pair == k, moved, total)
            return total

        def fan(value, sign):
            turned = value
            for k in range(1, 4):
                turned = jnp.where(ey == k, rotate(value, sign * 32 * k, 1), turned)
            return turned

        def sender(halo, link):
            src, dst, send_sem, recv_sem = link
            n = halo.n
            ends = ((True, halo.z_part[1]), (False, halo.z_part[-1]))

            def send(*kinds):
                for o in NEAR:
                    if tuple(map(abs, o)) not in kinds:
                        continue
                    at, count, tall = halo.part(o)
                    to = halo.slot[(-o[0], -o[1], -o[2])]
                    pltpu.make_async_remote_copy(
                        src_ref=src.at[pl.ds(at, count), pl.ds(0, tall)],
                        dst_ref=dst.at[pl.ds(to, count), pl.ds(0, tall)],
                        send_sem=send_sem,
                        recv_sem=recv_sem.at[1 if o[0] else 0],
                        device_id=near(o),
                        device_id_type=MESH,
                    ).start()

            def send_x(planes, lanes):
                lanes, planes = x_planes(lanes, halo), x_planes(planes, halo)
                for up, base in ends:
                    for k in range(2):
                        moved = fan(lane_pack(lanes[k], up), 1)
                        moved = jnp.where(lane // 32 == ey, moved, 0.0)
                        at = base + halo.own_z + 1 + k
                        src[at, 0:1] = jnp.sum(moved[0:4], axis=0, keepdims=True)
                        src[at, 1:2] = jnp.sum(moved[4:8], axis=0, keepdims=True)
                send((1, 1, 1), (1, 0, 1))
                for k in range(4):
                    corner = planes[k // 2][n + k % 2]
                    if k % 2 == 0:
                        corner = jnp.where(sub < 2, rotate(corner, 2, 0), corner)
                    else:
                        corner = jnp.where(sub < 2, corner, rotate(corner, 6, 0))
                    src[4 * n + k, 0:4] = corner[0:4]
                send((1, 1, 0))
                for k in range(2):
                    for j in range(n):
                        src[(2 + k) * n + j] = planes[k][j]
                send((1, 0, 0))

            def send_rest(planes, lanes, own):
                for up, base in ends:
                    edge = [y_plane(lanes[i], halo, y) for y in (True, False) for i in range(n)]
                    src[base + halo.own_z] = lane_pack(edge, up)
                send((0, 1, 1))
                for up, base in ends:
                    for k in range(halo.own_z):
                        src[base + k] = lane_pack(own[64 * k : 64 * k + 64], up)
                send((0, 0, 1))
                for i in range(n):
                    src[i] = y_plane(planes[i], halo, True)
                    src[n + i] = y_plane(planes[i], halo, False)
                send((0, 1, 0))

            return send_x, send_rest

        def wait_all(ref, sem):
            pltpu.make_async_copy(ref, ref, sem).wait()

        def wait_halo(ref, halo, sem, far):
            wait_all(ref.at[pl.ds(0, halo.vectors[far])], sem.at[far])

        def wait_sent(ref, halo, sem):
            wait_all(ref.at[pl.ds(0, sum(halo.vectors))], sem)

        def y_lanes(dst, halo, dz):
            low, high = dst[halo.slot[(0, -1, dz)]], dst[halo.slot[(0, 1, dz)]]
            return jnp.where(ey >= 2, low, rotate(high, -2 * halo.n, 1))

        def x_lanes(dst, halo, dx, dz):
            def got(dy):
                at = halo.slot[(dx, dy, dz)]
                value = jnp.where(lower, dst[at, 0:1], dst[at, 1:2])
                return fan(value, -1)

            corner = jnp.where(ey >= 2, got(-1), rotate(got(1), -2, 1))
            return jnp.where(pair >= halo.n, corner, got(0))

        def xy_corner(dst, halo, dx):
            low, high = dst[halo.slot[(dx, -1, 0)], 0:4], dst[halo.slot[(dx, 1, 0)], 0:4]
            low, high = jnp.concatenate([low, low], 0), jnp.concatenate([high, high], 0)
            low = jnp.where(lower, low, rotate(low, 2, 0))
            high = jnp.where(lower, high, rotate(high, 6, 0))
            return jnp.where(ey >= 2, low, high)

        def unlane(low, high, k):
            return z_mask * jnp.where(
                lane < 2, rotate(low, -2 * k, 1), rotate(high, 126 - 2 * k, 1)
            )

        def receive_near(dst, halo, sem, put):
            n = halo.n

            def at(o, k=0):
                return dst[halo.slot[o] + k]

            wait_halo(dst, halo, sem, 0)
            own_lo = [dst[halo.slot[(0, 0, -1)] + k] for k in range(halo.own_z)]
            own_hi = [dst[halo.slot[(0, 0, 1)] + k] for k in range(halo.own_z)]
            for i in range(n):
                for j in range(n):
                    k = i * n + j
                    put(1, i, j, unlane(own_lo[k // 64], own_hi[k // 64], k % 64))
            low, high = y_lanes(dst, halo, -1), y_lanes(dst, halo, 1)
            for k in range(n):
                put(0, k, n, y_mask * jnp.where(ey >= 2, at((0, -1, 0), k), at((0, 1, 0), k)))
                put(1, k, n, y_mask * unlane(low, high, k))
        def receive_far(dst, halo, sem, put):
            n = halo.n
            wait_halo(dst, halo, sem, 1)
            for k in range(n):
                put(0, n, k, fx_lo * dst[halo.slot[(-1, 0, 0)] + k])
                put(0, n + 1, k, fx_hi * dst[halo.slot[(1, 0, 0)] + k])
            below = x_lanes(dst, halo, -1, -1), x_lanes(dst, halo, -1, 1)
            above = x_lanes(dst, halo, 1, -1), x_lanes(dst, halo, 1, 1)
            for k in range(n):
                put(1, n, k, fx_lo * unlane(*below, k))
                put(1, n + 1, k, fx_hi * unlane(*above, k))
            put(0, n, n, fx_lo * y_mask * xy_corner(dst, halo, -1))
            put(1, n, n, fx_lo * y_mask * unlane(*below, n))
            put(0, n + 1, n, fx_hi * y_mask * xy_corner(dst, halo, 1))
            put(1, n + 1, n, fx_hi * y_mask * unlane(*above, n))

        def from_x(u, plo, phi, hf, hs, lf, ls):
            face_lo = rotate(jnp.where(lower, u[hf], plo), 4, 1)
            next_lo = jnp.where(lower, plo, rotate(u[hs], 4, 1))
            face_hi = rotate(jnp.where(lower, phi, u[lf]), 4, 1)
            next_hi = jnp.where(lower, rotate(u[ls], 4, 1), phi)
            return face_lo, next_lo, face_hi, next_hi

        def from_y(u, h, hf, hs, lf, ls):
            turned = rotate(h, 4, 1)
            face_lo = rotate(jnp.where(ey == 3, turned, u(hf)), 1, 1)
            next_lo = jnp.where(ey == 0, rotate(h, 6, 1), rotate(u(hs), 1, 1))
            face_hi = rotate(jnp.where(ey == 0, turned, u(lf)), 7, 1)
            next_hi = jnp.where(ey == 3, rotate(h, 2, 1), rotate(u(ls), 7, 1))
            return face_lo, next_lo, face_hi, next_hi

        def gather_sender(it):
            return sender(IN, (gs.at[it], gr.at[it], gsend.at[it], grecv.at[it]))

        def gather_x(it):
            rows = {i: raw[it, 8 * i : 8 * i + 8] for i in (0, 1, 6, 7)}
            gather_sender(it)[0](rows, rows)

        def gather_rest(it):
            rows = [raw[it, 8 * i : 8 * i + 8] for i in range(8)]
            gather_sender(it)[1](rows, rows, [raw[it, k] for k in range(64)])

        def spread_rows(tile, rows):
            for i, w in rows.items():
                face_lo, next_lo, face_hi, next_hi = from_y(
                    lambda j: w[j : j + 1], w[8:9], 7, 6, 0, 1
                )
                e[tile, i, 0:1] = next_lo
                e[tile, i, 1:2] = w[0:1] + face_lo
                e[tile, i, 2:8] = w[1:7]
                e[tile, i, 8:9] = w[7:8] + face_hi
                e[tile, i, 9:10] = next_hi

        def put_gathered(tile, i, j, value):
            ug[tile, i, j] = value

        def gather_near(it):
            receive_near(gr.at[it], IN, grecv.at[it], put_gathered)
            ug[0, 0:8, 0:8] = raw[it].reshape(8, 8, 8, 128)
            for tile in range(2):
                spread_rows(tile, {i + 1: ug[tile, i] for i in range(1, 7)})

        def gather_far(it):
            receive_far(gr.at[it], IN, grecv.at[it], put_gathered)
            for tile in range(2):
                u = [ug[tile, i] for i in range(10)]
                face_lo, next_lo, face_hi, next_hi = from_x(u, u[8], u[9], 7, 6, 0, 1)
                spread_rows(tile, {0: next_lo, 1: u[0] + face_lo,
                                   8: (u[7] + face_hi) * x_mask, 9: next_hi})

        def gather_keep(it):
            for tile in range(2):
                x[it, tile] = e[tile, 1:9, 1:9].reshape(64, 8, 128)

        def to_modes(v, picks=range(5)):
            plus = {a: v[a] + v[9 - a] for a in picks}
            minus = {a: v[a] - v[9 - a] for a in picks}
            out = []
            for k in range(10):
                total = None
                for a in picks:
                    term = (plus if k % 2 == 0 else minus)[a] * float(SINE[a, k])
                    total = term if total is None else total + term
                out.append(total)
            return out

        def from_modes(f, picks=range(5)):
            out = {}
            for a in picks:
                even = f[0] * float(SINE[a, 0])
                odd = f[1] * float(SINE[a, 1])
                for k in range(1, 5):
                    even = even + f[2 * k] * float(SINE[a, 2 * k])
                    odd = odd + f[2 * k + 1] * float(SINE[a, 2 * k + 1])
                out[a], out[9 - a] = even + odd, even - odd
            return out

        def joined_rows(ref, spans):
            return jnp.concatenate(
                [
                    jnp.concatenate([ref[tile, i0:i1] for i0, i1 in spans]).reshape(-1, 128)
                    for tile in range(2)
                ],
                axis=1,
            )

        def store_rows(ref, spans, values):
            at = 0
            for i0, i1 in spans:
                rows = values[80 * at : 80 * (at + i1 - i0)]
                for tile in range(2):
                    ref[tile, i0:i1] = rows[:, 128 * tile : 128 * tile + 128].reshape(
                        i1 - i0, 10, 8, 128
                    )
                at += i1 - i0

        def row_modes(spans):
            modes = jnp.dot(joined_rows(e, spans), fwd_ref[...], precision=lax.Precision.HIGH,
                            preferred_element_type=F32)
            store_rows(sq, spans, modes)
            for i0, i1 in spans:
                def over_y(i, carry):
                    for tile in range(2):
                        out = to_modes([sq[tile, i, j] for j in range(10)])
                        for j in range(10):
                            sq[tile, i, j] = out[j]
                    return carry

                lax.fori_loop(i0, i1, over_y, 0, unroll=i1 - i0)

        def near_modes():
            row_modes(((2, 8),))

            def over_x(j, carry):
                for tile in range(2):
                    out = to_modes({i: sq[tile, i, j] for i in range(2, 8)}, (2, 3, 4))
                    for i in range(10):
                        sp[tile, i, j] = out[i]
                return carry

            lax.fori_loop(0, 10, over_x, 0, unroll=5)

        def boxes(it):
            row_modes(((0, 2), (8, 10)))

            def middle(j, total):
                for tile in range(2):
                    f = to_modes({i: sq[tile, i, j] for i in (0, 1, 8, 9)}, (0, 1))
                    f = [f[i] + sp[tile, i, j] for i in range(10)]
                    scale = icb[tile]
                    g = [f[i] * (inv_ref[tile, j, i : i + 1] * scale) for i in range(10)]
                    for i in range(10):
                        total = total + f[i] * g[i]
                        sp[tile, i, j] = g[i]
                    for i, value in from_modes(g, (0, 1)).items():
                        sq[tile, i, j] = value
                return total

            acc[2 * it] = lax.fori_loop(0, 10, middle, jnp.zeros((8, 128), F32), unroll=5)
            send_x, send_rest = sender(OUT, (ss.at[it], sr.at[it], ssend.at[it], srecv.at[it]))

            def answers(spans):
                for i0, i1 in spans:
                    def back_y(i, carry):
                        for tile in range(2):
                            out = from_modes([sq[tile, i, j] for j in range(10)])
                            for j, value in out.items():
                                sq[tile, i, j] = value
                        return carry

                    lax.fori_loop(i0, i1, back_y, 0, unroll=i1 - i0)
                back = jnp.dot(joined_rows(sq, spans), bwd_ref[...],
                               precision=lax.Precision.HIGH, preferred_element_type=F32)
                store_rows(sq, spans, back)

            answers(((0, 2), (8, 10)))
            send_x({i: sq[0, i] for i in (0, 1, 8, 9)}, {i: sq[1, i] for i in (0, 1, 8, 9)})

            def back_x(j, carry):
                for tile in range(2):
                    out = from_modes([sp[tile, i, j] for i in range(10)], (2, 3, 4))
                    for i, value in out.items():
                        sq[tile, i, j] = value
                return carry

            lax.fori_loop(0, 10, back_x, 0, unroll=5)
            answers(((2, 8),))
            own = [sq[1, k // 10, k % 10] for k in range(100)]
            send_rest([sq[0, i] for i in range(10)], [sq[1, i] for i in range(10)], own)

        def put_scattered(tile, i, j, value):
            if i < 10 and j < 10:
                us[i, j] = sq[0, i, j] + value
            elif tile == 0:
                us[i, j] = value
            else:
                us[i, j] = us[i, j] + value

        def fold_rows(it, rows):
            for i, w in rows.items():
                last = x_mask if i == 7 else 1.0
                face_lo, next_lo, face_hi, next_hi = from_y(
                    lambda j: w[j : j + 1], w[10:11], 8, 9, 1, 0
                )
                zs[it, 8 * i : 8 * i + 1] = (w[1:2] + face_lo) * last
                zs[it, 8 * i + 1 : 8 * i + 2] = (w[2:3] + next_lo) * last
                zs[it, 8 * i + 2 : 8 * i + 6] = w[3:7] * last
                zs[it, 8 * i + 6 : 8 * i + 7] = (w[7:8] + next_hi) * last
                zs[it, 8 * i + 7 : 8 * i + 8] = (w[8:9] + face_hi) * last

        def scatter_near(it):
            receive_near(sr.at[it], OUT, srecv.at[it], put_scattered)
            fold_rows(it, {i: us[i + 1] for i in range(2, 6)})

        def scatter_far(it):
            receive_far(sr.at[it], OUT, srecv.at[it], put_scattered)
            u = [us[i] for i in range(12)]
            face_lo, next_lo, face_hi, next_hi = from_x(u, u[10], u[11], 8, 9, 1, 0)
            fold_rows(it, {0: u[1] + face_lo, 1: u[2] + next_lo, 6: u[7] + next_hi,
                           7: (u[8] + face_hi) * x_mask})

        def derive(v, matrix, picks=range(4)):
            plus = [v[k] + v[7 - k] for k in range(4)]
            minus = [v[k] - v[7 - k] for k in range(4)]
            out = {}
            for a in picks:
                even = odd = None
                for k in range(4):
                    p = plus[k] * float(0.5 * (matrix[a, k] + matrix[a, 7 - k]))
                    m = minus[k] * float(0.5 * (matrix[a, k] - matrix[a, 7 - k]))
                    even = p if even is None else even + p
                    odd = m if odd is None else odd + m
                out[a], out[7 - a] = even + odd, odd - even
            return out

        def fluxes_in_planes(it, spans):
            def joined(ref):
                return jnp.concatenate([ref[8 * i0 : 8 * i1] for i0, i1 in spans])

            grad = jnp.dot(joined(zs.at[it]).reshape(-1, 128), der_ref[0],
                           precision=lax.Precision.HIGH,
                           preferred_element_type=F32).reshape(-1, 8, 128)
            flux = grad * joined(wc)
            total = jnp.sum(flux * grad, axis=0)
            at = 0
            for i0, i1 in spans:
                fl[2, 8 * i0 : 8 * i1] = flux[at : at + 8 * (i1 - i0)]
                at += 8 * (i1 - i0)
                for i in range(i0, i1):
                    along = derive([zs[it, 8 * i + j] for j in range(8)], DERIV)
                    for j in range(8):
                        part = along[j] * wc[8 * i + j]
                        total = total + part * along[j]
                        fl[1, 8 * i + j] = part
            return total

        def fluxes_across(it, total):
            def over_x(j, total):
                grad = derive([zs[it, 8 * i + j] for i in range(8)], DERIV)
                for i in range(8):
                    flux = grad[i] * wc[8 * i + j]
                    total = total + flux * grad[i]
                    fl[0, 8 * i + j] = flux
                return total

            return lax.fori_loop(0, 8, over_x, total, unroll=8)

        def divergence(it, picks, spans):
            along_z = jnp.dot(
                jnp.concatenate([fl[2, 8 * i0 : 8 * i1] for i0, i1 in spans]).reshape(-1, 128),
                der_ref[1], precision=lax.Precision.HIGH, preferred_element_type=F32,
            ).reshape(-1, 8, 128)
            at = 0
            for i0, i1 in spans:
                raw[it + 1, 8 * i0 : 8 * i1] = along_z[at : at + 8 * (i1 - i0)]
                at += 8 * (i1 - i0)

            def over_x(j, carry):
                out = derive([fl[0, 8 * i + j] for i in range(8)], DERIV.T, picks)
                for i, value in out.items():
                    raw[it + 1, 8 * i + j] = raw[it + 1, 8 * i + j] + value
                return carry

            lax.fori_loop(0, 8, over_x, 0, unroll=8)
            for i0, i1 in spans:
                for i in range(i0, i1):
                    out = derive([fl[1, 8 * i + j] for j in range(8)], DERIV.T)
                    for j in range(8):
                        raw[it + 1, 8 * i + j] = raw[it + 1, 8 * i + j] + out[j]

        def far_first(count, length):
            return sorted(range(1, count), key=lambda t: -length(t))

        rings = (
            (red_xy, ny * runs, gz // z_run * ny + gy, ring_xy,
             far_first(ny * runs, lambda t: min(t // ny, runs - t // ny)
                       + min(t % ny, ny - t % ny) / 2)),
            (red_z, ring, gx * z_run + gz % z_run, ring_z,
             far_first(ring, lambda t: min(t, ring - t))),
        )

        def reduce_start(phase, value):
            ref, count, me, to, order = rings[phase]
            ref[me, 0:1] = value
            for t in order:
                pltpu.make_async_remote_copy(
                    src_ref=ref.at[me, pl.ds(0, 1)],
                    dst_ref=ref.at[me, pl.ds(0, 1)],
                    send_sem=rsend.at[phase],
                    recv_sem=rrecv.at[phase],
                    device_id=to(t),
                    device_id_type=MESH,
                ).start()

        def reduce_wait(phase):
            ref, count = rings[phase][:2]
            if count > 1:
                wait_all(ref.at[pl.ds(0, count - 1), pl.ds(0, 1)], rrecv.at[phase])
            return jnp.sum(ref[0:count, 0:1], axis=0)

        def reduce_end(phase):
            ref, count = rings[phase][:2]
            if count > 1:
                wait_all(ref.at[pl.ds(0, count - 1), pl.ds(0, 1)], rsend.at[phase])

        def relaid(ref, store):
            for i in range(8):
                for j in range(8):
                    store(8 * i + j, ref[i, pl.ds(j, 8, stride=8), :])

        def put_b(k, value):
            raw[0, k] = value

        def put_c(k, value):
            zs[0, k] = value

        loads[0].wait()
        loads[1].wait()
        relaid(b_rows, put_b)
        pl.semaphore_wait(barrier, len(partners))
        gather_x(0)
        gather_rest(0)
        for copy in loads[2:]:
            copy.wait()
        relaid(c_rows, put_c)
        mean = jnp.dot(jnp.sum(zs[0], axis=0), mean_ref[...], precision=lax.Precision.HIGHEST,
                       preferred_element_type=F32)
        icb[0] = 1.0 / mean[:, :128]
        icb[1] = 1.0 / mean[:, 128:]
        for i in range(8):
            wc[8 * i : 8 * i + 8] = zs[0, 8 * i : 8 * i + 8] * (wyz_ref[...] * float(WEIGHTS[i]))

        def step(it, carry):
            gather_near(it)
            near_modes()
            gather_far(it)
            boxes(it)
            gather_keep(it)
            scatter_near(it)
            total = fluxes_in_planes(it, ((2, 6),))
            scatter_far(it)
            total = total + fluxes_in_planes(it, ((0, 2), (6, 8)))
            acc[2 * it + 1] = fluxes_across(it, total)

            @pl.when(it == 1)
            def _():
                local = jnp.zeros((1, 128), F32)
                for k in range(4):
                    total = jnp.sum(acc[k], axis=(0, 1), keepdims=True)
                    local = jnp.where(lane[0:1] == k, total, local)
                reduce_start(0, local)

            divergence(it, (0, 1), ((0, 2), (6, 8)))
            gather_x(it + 1)
            divergence(it, (2, 3), ((2, 6),))
            gather_rest(it + 1)
            return carry

        lax.fori_loop(0, 2, step, 0)
        reduce_start(1, reduce_wait(0))
        gather_near(2)
        gather_far(2)
        gather_keep(2)
        def placed(k, values):
            for m in range(64):
                for ex in range(2):
                    fin[k, 8 * ex + m // 8, pl.ds(m % 8, 4, stride=8), :] = values[
                        m, 4 * ex : 4 * ex + 4
                    ]

        placed(0, zs[0])
        placed(1, zs[1])
        for it in range(3):
            wide = jnp.concatenate(
                [x[it, 0].reshape(512, 128), x[it, 1].reshape(512, 128)], axis=1
            )
            out = jnp.dot(wide, asm_ref[...], precision=lax.Precision.HIGH,
                          preferred_element_type=F32)
            placed(2 + it, out.reshape(64, 8, 128))
        sums = reduce_wait(1)
        rho, delta, gamma, eps = (sums[:, k : k + 1] for k in range(4))
        a0 = rho / delta
        rz = a0 * a0 * gamma - rho
        up = 1.0 + rz / rho
        curve = up * up * delta - 2.0 * a0 * up * gamma + a0 * a0 * eps
        a1 = rz / curve
        first = a0 + a1 * up
        second = a1 * a0
        stores = [
            pltpu.make_async_copy(fin.at[k], ref, load.at[k])
            for k, ref in ((0, sol_ref), (2, res_ref))
        ]
        fin[0] = fin[0] * first - fin[1] * second
        stores[0].start()
        fin[2] = fin[2] - fin[3] * first + fin[4] * second
        stores[1].start()
        for copy in stores:
            copy.wait()
        for it in range(3):
            wait_sent(gr.at[it], IN, gsend.at[it])
        for it in range(2):
            wait_sent(sr.at[it], OUT, ssend.at[it])
        for phase in range(2):
            reduce_end(phase)

    return kernel


def solution(mesh):
    sizes = tuple(mesh.shape[a] for a in AXES)
    z_run = 4 if sizes[2] % 4 == 0 else sizes[2]
    ring = sizes[0] * z_run
    forward, assemble = z_tables(16)
    der = np.kron(np.eye(16), DERIV)
    inverse = np.zeros((2, 10, 10, 128))
    tiled = np.tile(INVERSE, (1, 1, 16))
    inverse[0] = tiled[:, :, :128]
    inverse[1, :, :, :32] = tiled[:, :, 128:]
    mean = np.zeros((128, 256))
    mean[:, :160] = np.kron(np.eye(16), np.ones((8, 10))) / SIDE**3
    mean[0, 160:] = 1.0
    wyz = np.broadcast_to(
        WEIGHTS[:, None, None] * np.tile(WEIGHTS, 16)[None, None, :], (8, 8, 128)
    )
    tables = [
        jnp.asarray(t, F32)
        for t in (wyz, forward, forward.T, assemble, np.stack([der.T, der]), inverse, mean)
    ]
    hbm = pl.BlockSpec(memory_space=pltpu.HBM)
    dma = pltpu.SemaphoreType.DMA

    def block(*shape):
        return pltpu.VMEM(shape + (8, 128), F32)

    call = pl.pallas_call(
        make_kernel(sizes, z_run),
        out_shape=[jax.ShapeDtypeStruct((16, 32, 128), F32)] * 2,
        in_specs=[hbm] * 9,
        out_specs=[hbm] * 2,
        scratch_shapes=[
            pltpu.VMEM((8, 64, 128), F32), pltpu.VMEM((8, 64, 128), F32),
            *[pltpu.VMEM(t.shape, F32) for t in tables],
            block(3, 64), block(64), block(2),
            block(3, IN.total), block(3, IN.received), block(2, 10, 9), block(2, 10, 10),
            block(3, 2, 64), block(2, 10, 10), block(2, 10, 10), block(3, 64),
            block(2, OUT.total), block(2, OUT.received), block(12, 11),
            block(2, 64), block(4),
            block(sizes[1] * sizes[2] // z_run), block(ring),
            dma((3,)), dma((3, 2)), dma((2,)), dma((2, 2)), dma((2,)), dma((2,)), dma((11,)), pltpu.VMEM((5, 16, 32, 128), F32),
        ],
        compiler_params=pltpu.CompilerParams(
            collective_id=0, has_side_effects=True, vmem_limit_bytes=60 * 1024 * 1024
        ),
    )

    def hand_over(first, second, first_out, second_out, held, sems):
        pieces = [
            (source, target, pl.ds(8 * half, 8))
            for source, target in ((first, first_out), (second, second_out))
            for half in range(2)
        ]
        reads = [
            pltpu.make_async_copy(source.at[part], held.at[k], sems.at[0, k])
            for k, (source, _, part) in enumerate(pieces)
        ]
        writes = [
            pltpu.make_async_copy(held.at[k], target.at[part], sems.at[1, k])
            for k, (_, target, part) in enumerate(pieces)
        ]
        for copy in reads:
            copy.start()
        for read, write in zip(reads, writes):
            read.wait()
            write.start()
        for copy in writes:
            copy.wait()

    results = pl.pallas_call(
        hand_over,
        out_shape=[jax.ShapeDtypeStruct((16, 32, 128), F32)] * 2,
        in_specs=[hbm] * 2,
        out_specs=[hbm] * 2,
        scratch_shapes=[pltpu.VMEM((4, 8, 32, 128), F32), dma((2, 4))],
        compiler_params=pltpu.CompilerParams(vmem_limit_bytes=60 * 1024 * 1024),
    )

    def shards(right_side, coefficient):
        return tuple(results(*call(right_side, coefficient, *tables)))

    spec = P(*AXES)
    return jax.shard_map(
        shards, mesh=mesh, in_specs=(spec, spec), out_specs=(spec, spec), check_vma=False
    )
```
